128 devices in a mesh: gx: 8 (over x, core), yz: 16 (over y, z).
Axes of the slice: x: 4, y: 4, z: 4, core: 2. Of those that a mesh axis runs over, the one named last changes fastest.
Arguments:
- tokens: bfloat16 [512, 2, 18432], P('yz', None, 'gx'), may hold values from -15 to 15
- gain: float32 [18432], P('gx'), may hold values from 0.25 to 1.75
- w_query: bfloat16 [18432, 12288], P('gx', 'yz'), may hold values from -0.046875 to 0.046875
- w_keyval: bfloat16 [18432, 512], P('gx'), may hold values from -0.046875 to 0.046875
- w_out: bfloat16 [12288, 18432], P('yz', 'gx'), may hold values from -0.21875 to 0.21875
- key_cache: bfloat16 [512, 2048, 256], P(('gx', 'yz')), may hold values from -256 to 256
- value_cache: bfloat16 [512, 2048, 256], P(('gx', 'yz')), may hold values from -5 to 5
- lengths: int32 [512], P(('gx', 'yz')), may hold values from 1 to 2048, as said below
Outputs:
- mixed: bfloat16 [512, 2, 18432], P('yz', None, 'gx')
- new_keyval: bfloat16 [512, 2, 512], P(('gx', 'yz'))
The draws below stay inside these ranges and needn't reach their ends.
Inputs may be any that keep to these rules, and one draw needn't show every extreme that they name: `lengths`: each sequence has this many filled cache positions from the start; its two new tokens stand at this position and the next; in every draw some sequence fills all 2048.
All inputs are finite; a program needn't handle non-finite values.
Results may differ from the reference program's by a relative error of at most 0.009.
The reference program's roundings to bfloat16 on the way count: a program that leaves them out, or rounds other values in their place, can miss the bound.
Values may be sent and summed in bfloat16 or wider, within the bound.
No kernel may reach another device: no remote copies, remote signals or barrier semaphores. Data moves between devices by JAX's collectives and lax.ppermute only.
A program may use at most 128 MiB of HBM per device.

```python
import jax
import jax.numpy as jnp
from jax import lax

D = 18432
HEADS = 48
HEAD = 256
CTX = 2048
BATCH = 512


def draw_tokens(key, part):
    key = jax.random.fold_in(key, 1)
    key_a = jax.random.fold_in(key, 0)
    column = jnp.arange(D, dtype=jnp.float32) / D
    rise = 3.0 ** (column - 0.5)
    values = jnp.clip(jax.random.normal(key_a, (BATCH, 2, D), jnp.float32), -4.5, 4.5) * rise
    return values.astype(jnp.bfloat16)


def draw_key_cache(key, part):
    key = jax.random.fold_in(key, 2)
    key_a = jax.random.fold_in(key, 0)
    values = jnp.clip(jax.random.normal(key_a, (BATCH, CTX, HEAD), jnp.float32), -4.0, 4.0)
    return values.astype(jnp.bfloat16)


def draw_lengths(key, part):
    key = jax.random.fold_in(key, 3)
    key_a, key_b = jax.random.split(key, 2)
    filled = jax.random.randint(key_a, (BATCH,), 1, CTX + 1, dtype=jnp.int32)
    chosen = jax.random.randint(key_b, (), 0, BATCH, dtype=jnp.int32)
    return filled.at[chosen].set(CTX)


def shard_levels(rng, dims, cuts, least, high):
    factor_of = 1.0
    for axis_at, blocks in cuts:
        heights = jax.random.uniform(jax.random.fold_in(jax.random.fold_in(rng, 6), axis_at), (blocks,), jnp.float32, least / len(cuts), high / len(cuts))
        factor_of = factor_of * jnp.repeat(jnp.exp(heights), dims[axis_at] // blocks).reshape((-1,) + (1,) * (len(dims) - 1 - axis_at))
    return factor_of


def centred(stream_key, dims, scale, bound, cuts=(), kind=jnp.bfloat16):
    array = jax.random.normal(stream_key, dims, jnp.float32) * scale
    if len(cuts) > 0:
        array = shard_levels(stream_key, dims, cuts, -0.22, 0.18) * array
    return jnp.clip(array, min=-bound, max=bound).astype(kind)


def setup_inputs(seed: int = 0) -> dict:
    streams_of = jax.random.split(jax.random.key(seed), 9)
    return {
        "tokens": draw_tokens(jax.random.fold_in(streams_of[8], 71), 0),
        "gain": jnp.clip(1.0 + 0.15 * jax.random.normal(streams_of[1], (D,), jnp.float32), 0.25, 1.75),
        "w_query": centred(streams_of[2], (D, HEADS * HEAD), D ** -0.5, 0.046875, ((0, 8), (1, 16))),
        "w_keyval": centred(streams_of[3], (D, 2 * HEAD), D ** -0.5, 0.046875, ((0, 8),)),
        "w_out": centred(streams_of[4], (HEADS * HEAD, D), (HEADS * HEAD // 16) ** -0.5, 0.21875, ((0, 16), (1, 8))),
        "key_cache": draw_key_cache(jax.random.fold_in(streams_of[8], 71), 0),
        "value_cache": centred(streams_of[6], (BATCH, CTX, HEAD), 1.0, 5.0, ((0, 128),)),
        "lengths": draw_lengths(jax.random.fold_in(streams_of[8], 71), 0),
    }


def rotate(vec, positions):
    half = vec.shape[-1] // 2
    freq = 10000.0 ** (-jnp.arange(half, dtype=jnp.float32) * 2.0 / vec.shape[-1])
    angle = positions.astype(jnp.float32)[..., None] * freq
    cosine = jnp.cos(angle)
    sine = jnp.sin(angle)
    first = vec[..., :half]
    second = vec[..., half:]
    return jnp.concatenate([first * cosine - second * sine, second * cosine + first * sine], -1)

def attend(packed):
    query_rows, keys, values, length, key_new, value_new = packed
    heads = query_rows.shape[0] // 2
    scale = query_rows.shape[1] ** (-0.5)
    cached = jnp.dot(query_rows, keys.T, preferred_element_type=jnp.float32) * scale
    valid = jnp.arange(keys.shape[0], dtype=jnp.int32) < length
    cached = jnp.where(valid[None, :], cached, -jnp.inf)
    fresh = jnp.dot(query_rows, key_new.T, preferred_element_type=jnp.float32) * scale
    step_of = jnp.arange(2 * heads, dtype=jnp.int32) // heads
    allowed = jnp.arange(2, dtype=jnp.int32)[None, :] <= step_of[:, None]
    fresh = jnp.where(allowed, fresh, -jnp.inf)
    top = jnp.maximum(lax.optimization_barrier(jnp.max(cached, -1)), lax.optimization_barrier(jnp.max(fresh, -1)))
    exp_cached = jnp.exp(cached - top[:, None])
    exp_fresh = jnp.exp(fresh - top[:, None])
    total = lax.optimization_barrier(jnp.sum(exp_cached, -1)) + lax.optimization_barrier(jnp.sum(exp_fresh, -1))
    weight_cached = (exp_cached / total[:, None]).astype(jnp.bfloat16)
    weight_fresh = (exp_fresh / total[:, None]).astype(jnp.bfloat16)
    result = jnp.dot(weight_cached, values, preferred_element_type=jnp.float32)
    result = result + jnp.dot(weight_fresh, value_new, preferred_element_type=jnp.float32)
    return result.astype(jnp.bfloat16)

def reference(tokens, gain, w_query, w_keyval, w_out, key_cache, value_cache, lengths):
    batch = tokens.shape[0]
    width = tokens.shape[2]
    head = w_keyval.shape[1] // 2
    heads = w_query.shape[1] // head
    xfull = tokens.astype(jnp.float32)
    mean = lax.optimization_barrier(jnp.sum(xfull, -1)) / width
    var = lax.optimization_barrier(jnp.sum(xfull * xfull, -1)) / width - mean * mean
    normed = ((xfull - mean[..., None]) * lax.rsqrt(var + 1e-05)[..., None] * gain).astype(jnp.bfloat16)
    flat = normed.reshape(batch * 2, width)
    query = jnp.dot(flat, w_query, preferred_element_type=jnp.float32).astype(jnp.bfloat16)
    keyval = jnp.dot(flat, w_keyval, preferred_element_type=jnp.float32).astype(jnp.bfloat16)
    query = query.reshape(batch, 2, heads, head)
    keyval = keyval.reshape(batch, 2, 2 * head)
    positions = lengths[:, None] + jnp.arange(2, dtype=jnp.int32)[None, :]
    query_rot = rotate(query.astype(jnp.float32), positions[:, :, None]).astype(jnp.bfloat16)
    key_new = rotate(keyval[..., :head].astype(jnp.float32), positions).astype(jnp.bfloat16)
    value_new = keyval[..., head:]
    new_keyval = jnp.concatenate([key_new, value_new], -1)
    query_rows = query_rot.reshape(batch, 2 * heads, head)
    heads_out = lax.map(attend, (query_rows, key_cache, value_cache, lengths, key_new, value_new))
    heads_out = heads_out.reshape(batch * 2, heads * head)
    branch = jnp.dot(heads_out, w_out, preferred_element_type=jnp.float32).reshape(batch, 2, width)
    mixed = (xfull + branch).astype(jnp.bfloat16)
    return (mixed, new_keyval)
```

```python
import functools

import jax
import jax.numpy as jnp
from jax import lax
from jax.experimental import pallas as pl
from jax.experimental.pallas import tpu as pltpu
from jax.sharding import PartitionSpec as P

D = 18432
HEADS = 48
HEAD = 256
RING = 4
F32 = jnp.float32
BF16 = jnp.bfloat16


def shift(value, move):
    pairs = []
    for x in range(RING):
        for core in range(2):
            for y in range(RING):
                for z in range(RING):
                    dx, dy, dz = move(core)
                    target = (2 * ((x + dx) % RING) + core) * 16
                    target += RING * ((y + dy) % RING) + (z + dz) % RING
                    pairs.append(((2 * x + core) * 16 + RING * y + z, target))
    return lax.ppermute(value, ("gx", "yz"), pairs)


def send_core(value):
    pairs = [(2 * x + c, 2 * x + 1 - c) for x in range(RING) for c in range(2)]
    return lax.ppermute(value, "gx", pairs)


def send_x(value, step):
    return shift(value, lambda core: ((1 - 2 * core) * step, 0, 0))


def send_ahead(value, step):
    return shift(value, lambda core: (step, 0, 0))


def send_inner(value, step):
    return shift(value, lambda core: (0, core * step, (1 - core) * step))


def send_outer(value, step):
    return shift(value, lambda core: (0, (1 - core) * step, core * step))


def rotation_tables(positions):
    half = HEAD // 2
    freq = 10000.0 ** (-jnp.arange(half, dtype=F32) * 2.0 / HEAD)
    angle = positions.astype(F32)[..., None] * freq
    return jnp.cos(angle), jnp.sin(angle)


def stage_kernel(count, *refs):
    sources, targets, sems = refs[:count], refs[count : 2 * count], refs[2 * count]
    copies = []
    for index, (source, target) in enumerate(zip(sources, targets)):
        size = source.shape[0] // 4
        for part in range(4):
            at = pl.ds(part * size, size)
            copies.append(
                pltpu.make_async_copy(source.at[at], target.at[at], sems.at[index, part])
            )
    for copy in copies:
        copy.start()
    for copy in copies:
        copy.wait()


def stage(*arrays):
    count = len(arrays)
    size = sum(a.size * a.dtype.itemsize for a in arrays)
    return pl.pallas_call(
        functools.partial(stage_kernel, count),
        out_shape=[jax.ShapeDtypeStruct(a.shape, a.dtype) for a in arrays],
        in_specs=[pl.BlockSpec(memory_space=pl.ANY)] * count,
        out_specs=[pl.BlockSpec(memory_space=pltpu.VMEM)] * count,
        scratch_shapes=[pltpu.SemaphoreType.DMA((count, 4))],
        compiler_params=pltpu.CompilerParams(vmem_limit_bytes=20 * 2**20),
        cost_estimate=pl.CostEstimate(flops=0, bytes_accessed=2 * size, transcendentals=0),
        name="stage",
    )(*arrays)


def query_kernel(other, place, *refs):
    pieces, (w_ref, out_ref, rows_ref, sems) = refs[:8], refs[8:]
    x, y, z, core = place[0], place[1], place[2], place[3]
    for index, piece in enumerate(pieces):
        for part in range(2):
            outer = (0, 3, 1, 2)[index % 4]
            inner = ((0, 3), (1, 2))[index // 4][part]
            at_y = lax.rem(y + jnp.where(core == 0, outer, inner), RING)
            at_z = lax.rem(z + jnp.where(core == 0, inner, outer), RING)
            to_core = at_z // 2
            ahead = lax.rem(at_y - x + RING, RING)
            slot = jnp.where(to_core == 0, ahead, lax.rem(RING - ahead, RING))
            position = slot * 2 + lax.rem(at_z, 2)
            copy = pltpu.make_async_copy(
                piece.at[part * 64 : (part + 1) * 64], rows_ref.at[position], sems.at[position]
            )
            pl.when((to_core != core) == other)(copy.start)
    for m in range(2):
        for position in range(4 * m, 4 * m + 4):
            pltpu.make_async_copy(
                pieces[0].at[0:64], rows_ref.at[position], sems.at[position]
            ).wait()
        rows = rows_ref[4 * m : 4 * m + 4].reshape(256, w_ref.shape[0])
        out_ref[m * 256 : (m + 1) * 256, :] = jnp.dot(
            rows, w_ref[...], preferred_element_type=F32
        )


def project_query(place, pieces, w_query, other):
    depth, columns = w_query.shape
    vmem_spec = pl.BlockSpec(memory_space=pltpu.VMEM)
    return pl.pallas_call(
        functools.partial(query_kernel, other),
        out_shape=jax.ShapeDtypeStruct((512, columns), F32),
        in_specs=[pl.BlockSpec(memory_space=pltpu.SMEM)]
        + [pl.BlockSpec(memory_space=pl.ANY)] * 8
        + [vmem_spec],
        out_specs=vmem_spec,
        scratch_shapes=[pltpu.VMEM((8, 64, depth), BF16), pltpu.SemaphoreType.DMA((8,))],
        compiler_params=pltpu.CompilerParams(vmem_limit_bytes=20 * 2**20),
        cost_estimate=pl.CostEstimate(
            flops=2 * 512 * depth * columns, bytes_accessed=8 * 2**20, transcendentals=0
        ),
        name="query_projection",
    )(place, *pieces, w_query)


def attend_kernel(
    lengths, q_ref, cos_ref, sin_ref, new_ref, k_hbm, v_hbm, out_ref, acc_ref, k_ref, v_ref, sems
):
    loads = []
    for r in range(k_ref.shape[0]):
        loads.append(pltpu.make_async_copy(k_hbm.at[r], k_ref.at[r], sems.at[0, r]))
        loads.append(pltpu.make_async_copy(v_hbm.at[r], v_ref.at[r], sems.at[1, r]))
    for load in loads[:4]:
        load.start()
    half = HEAD // 2
    rows = q_ref.shape[0]
    scale = HEAD ** (-0.5)
    contract_last = (((1,), (1,)), ((), ()))
    pick_row = lax.broadcasted_iota(jnp.int32, (32, rows), 0)
    pick_col = lax.broadcasted_iota(jnp.int32, (32, rows), 1)
    odd = lax.rem(lax.broadcasted_iota(jnp.int32, (32, half), 0), 2) == 1
    second_step = lax.rem(lax.broadcasted_iota(jnp.int32, (96, 1), 0), 2) == 1
    for r in range(k_ref.shape[0]):
        pick = (pick_col == (pick_row // 2) * 8 + 2 * r + lax.rem(pick_row, 2)).astype(BF16)
        cosine = jnp.where(odd, cos_ref[r, 1:2, :], cos_ref[r, 0:1, :])
        sine = jnp.where(odd, sin_ref[r, 1:2, :], sin_ref[r, 0:1, :])
        parts = []
        for h in range(3):
            chosen = jnp.dot(pick, q_ref[:, h * HEAD : (h + 1) * HEAD], preferred_element_type=F32)
            first, second = chosen[:, :half], chosen[:, half:]
            parts.append(
                jnp.concatenate([first * cosine - second * sine, second * cosine + first * sine], 1)
            )
        query = jnp.concatenate(parts, 0).astype(BF16)
        loads[2 * r].wait()
        for load in loads[2 * r + 4 : 2 * r + 6]:
            load.start()
        cached = lax.dot_general(query, k_ref[r], contract_last, preferred_element_type=F32) * scale
        valid = lax.broadcasted_iota(jnp.int32, cached.shape, 1) < lengths[r]
        cached = jnp.where(valid, cached, -jnp.inf)
        new = new_ref[r].astype(F32)
        wide = query.astype(F32)
        fresh0 = jnp.sum(wide * new[0:1, :HEAD], -1, keepdims=True) * scale
        fresh1 = jnp.sum(wide * new[1:2, :HEAD], -1, keepdims=True) * scale
        fresh1 = jnp.where(second_step, fresh1, -jnp.inf)
        top = jnp.maximum(jnp.max(cached, -1, keepdims=True), jnp.maximum(fresh0, fresh1))
        exp_cached = jnp.exp(cached - top)
        exp0 = jnp.exp(fresh0 - top)
        exp1 = jnp.exp(fresh1 - top)
        inverse = 1.0 / (jnp.sum(exp_cached, -1, keepdims=True) + exp0 + exp1)
        weights = (exp_cached * inverse).astype(BF16)
        weight0 = (exp0 * inverse).astype(BF16).astype(F32)
        weight1 = (exp1 * inverse).astype(BF16).astype(F32)
        loads[2 * r + 1].wait()
        result = jnp.dot(weights, v_ref[r], preferred_element_type=F32)
        result = result + weight0 * new[0:1, HEAD:] + weight1 * new[1:2, HEAD:]
        result = result.astype(BF16)
        for h in range(3):
            spread = lax.dot_general(
                pick,
                result[h * 32 : (h + 1) * 32],
                (((0,), (0,)), ((), ())),
                preferred_element_type=F32,
            )
            columns = slice(h * HEAD, (h + 1) * HEAD)
            if r == 0:
                acc_ref[:, columns] = spread
            else:
                acc_ref[:, columns] += spread
    out_ref[...] = acc_ref[...].astype(BF16)


def attend(lengths, query, cosine, sine, new_keyval, keys, values):
    seqs, context, _ = keys.shape
    rows, columns = query.shape
    vmem_spec = pl.BlockSpec(memory_space=pltpu.VMEM)
    return pl.pallas_call(
        attend_kernel,
        out_shape=jax.ShapeDtypeStruct((rows, columns), BF16),
        in_specs=[pl.BlockSpec(memory_space=pltpu.SMEM)]
        + [vmem_spec] * 4
        + [pl.BlockSpec(memory_space=pltpu.HBM)] * 2,
        out_specs=vmem_spec,
        scratch_shapes=[
            pltpu.VMEM((rows, columns), F32),
            pltpu.VMEM(keys.shape, BF16),
            pltpu.VMEM(values.shape, BF16),
            pltpu.SemaphoreType.DMA((2, seqs)),
        ],
        compiler_params=pltpu.CompilerParams(vmem_limit_bytes=54 * 2**20),
        cost_estimate=pl.CostEstimate(
            flops=4 * seqs * 96 * context * HEAD,
            bytes_accessed=4 * seqs * context * HEAD,
            transcendentals=seqs * 96 * context,
        ),
        name="attention",
    )(lengths, query, cosine, sine, new_keyval, keys, values)


def output_kernel(groups, place, *refs):
    pieces, (w_ref, *outs), rows_ref = refs[:8], refs[8:-1], refs[-1]
    x, y, z, core = place[0], place[1], place[2], place[3]
    for index, piece in enumerate(pieces):
        at_core = core if index < 4 else 1 - core
        slot = (0, 3, 1, 2)[index % 4]
        ahead = jnp.where(at_core == 0, slot, (RING - slot) % RING)
        dy = lax.rem(x + ahead - y + RING, RING)
        for part in range(2):
            dz = lax.rem(2 * at_core + part - z + RING, RING)
            outer, inner = jnp.where(core == 0, dy, dz), jnp.where(core == 0, dz, dy)
            for position, group in enumerate(groups):

                @pl.when(outer == group)
                def _():
                    rows_ref[position * RING + inner] = piece[part * 64 : (part + 1) * 64, :]

    outs = list(outs)
    for position, group in enumerate(groups):
        rows = rows_ref[RING * position : RING * position + RING].reshape(256, w_ref.shape[0])
        targets = [outs.pop(0)] if group == 0 else [outs.pop(0), outs.pop(0)]
        for start in range(0, w_ref.shape[1], 768):
            columns = slice(start, start + 768)
            result = jnp.dot(rows, w_ref[:, columns], preferred_element_type=F32)
            if group == 0:
                targets[0][:, columns] = result
            else:
                targets[0][:, columns] = result[:128].astype(BF16)
                targets[1][:, columns] = result[128:].astype(BF16)


def project_output(place, pieces, w_out, groups):
    depth, columns = w_out.shape
    vmem_spec = pl.BlockSpec(memory_space=pltpu.VMEM)
    shapes = []
    for group in groups:
        if group == 0:
            shapes.append(jax.ShapeDtypeStruct((256, columns), F32))
        else:
            shapes += [jax.ShapeDtypeStruct((128, columns), BF16)] * 2
    return pl.pallas_call(
        functools.partial(output_kernel, groups),
        out_shape=shapes,
        in_specs=[pl.BlockSpec(memory_space=pltpu.SMEM)] + [vmem_spec] * 9,
        out_specs=[vmem_spec] * len(shapes),
        scratch_shapes=[pltpu.VMEM((RING * len(groups), 64, depth), BF16)],
        compiler_params=pltpu.CompilerParams(vmem_limit_bytes=20 * 2**20),
        cost_estimate=pl.CostEstimate(
            flops=2 * 256 * len(groups) * depth * columns,
            bytes_accessed=8 * 2**20,
            transcendentals=0,
        ),
        name="output_projection",
    )(place, *pieces, w_out)


def body(tokens, gain, w_query, w_keyval, w_out, key_cache, value_cache, lengths):
    seqs = lengths.shape[0]
    gx, yz = lax.axis_index("gx"), lax.axis_index("yz")
    place = jnp.stack([gx // 2, yz // RING, lax.rem(yz, RING), lax.rem(gx, 2)]).astype(jnp.int32)
    positions = lengths[:, None] + jnp.arange(2, dtype=jnp.int32)[None, :]
    cosine, sine = rotation_tables(positions)

    count = tokens.shape[0] * 2
    features = tokens.shape[2]
    xfull = tokens.reshape(count, features).astype(F32)
    stats = jnp.stack([jnp.sum(xfull, -1), jnp.sum(xfull * xfull, -1)])
    stats = stats + send_core(stats)
    stats = stats + send_x(stats, 1) + send_x(stats, 2) + send_x(stats, 3)
    mean = stats[0] / D
    var = stats[1] / D - mean * mean
    normed = ((xfull - mean[:, None]) * lax.rsqrt(var + 1e-05)[:, None] * gain).astype(BF16)

    normed = lax.optimization_barrier(normed)
    keyval = lax.optimization_barrier(jnp.dot(normed, w_keyval, preferred_element_type=F32))

    before = send_inner(normed, 1)
    after = send_inner(normed, -1)
    far = send_inner(before, 1)
    near = jnp.concatenate([normed, before], 0)
    near, keyval = lax.optimization_barrier((near, keyval))
    wide = jnp.concatenate([after, far], 0)
    near_before, near_after = send_outer(near, 1), send_outer(near, -1)
    near_before, near_after = lax.optimization_barrier((near_before, near_after))
    wide_before, wide_after = send_outer(wide, 1), send_outer(wide, -1)
    near_far = send_outer(near_before, 1)
    near_far, wide_after = lax.optimization_barrier((near_far, wide_after))
    wide_far = send_outer(wide_after, -1)

    blocks = keyval.reshape(RING, 2, count // 8, 2 * HEAD)
    blocks = lax.dynamic_slice_in_dim(jnp.concatenate([blocks, blocks], 0), place[0], RING, 0)
    kept = lax.dynamic_index_in_dim(blocks, place[3], 1, keepdims=False)
    kept = kept + send_core(lax.dynamic_index_in_dim(blocks, 1 - place[3], 1, keepdims=False))
    keyval = kept[0] + send_ahead(kept[1], 1) + send_ahead(kept[2], 2) + send_ahead(kept[3], 3)
    keyval = keyval.astype(BF16)
    moves = [
        (g * 16 + j, (j // 2) * 16 + (j % 2) * 8 + g) for g in range(8) for j in range(16)
    ]
    keyval = lax.ppermute(keyval, ("gx", "yz"), moves).reshape(seqs, 2, 2 * HEAD)
    first = keyval[..., : HEAD // 2].astype(F32)
    second = keyval[..., HEAD // 2 : HEAD].astype(F32)
    new_keyval = jnp.concatenate(
        [
            (first * cosine - second * sine).astype(BF16),
            (second * cosine + first * sine).astype(BF16),
            keyval[..., HEAD:],
        ],
        -1,
    )

    pieces = [near, near_before, near_after, near_far, wide, wide_before, wide_after, wide_far]
    columns = w_query.shape[1]
    staged_query = stage(w_query)[0]
    pieces, new_keyval, staged_query = lax.optimization_barrier((pieces, new_keyval, staged_query))
    away = project_query(place, pieces, staged_query, True)
    keep = project_query(place, pieces, staged_query, False)
    summed = (keep + send_core(away)).reshape(RING, 128, columns)
    far = send_x(summed[2], 1)
    behind = send_x(summed[3], -1)
    ahead = send_x(summed[1] + far, 1)
    query = (summed[0] + ahead + behind).astype(BF16).reshape(16, 8, columns)
    query = lax.all_to_all(query, "yz", split_axis=0, concat_axis=0)

    heads_out = attend(
        lengths, query.reshape(128, columns), cosine, sine, new_keyval, key_cache, value_cache
    )
    heads_out = lax.all_to_all(
        heads_out.reshape(16, 8, columns), "yz", split_axis=0, concat_axis=0
    ).reshape(128, columns)
    before = send_x(heads_out, 1)
    after = send_x(heads_out, -1)
    pieces = [heads_out, before, after, send_x(before, 1)]
    pieces = pieces + [send_core(p) for p in pieces]
    two_low, two_high = project_output(place, pieces, w_out, (2,))
    one_low, one_high, three_low, three_high, own = project_output(
        place, pieces, w_out, (1, 3, 0)
    )

    far_low, far_high = send_outer(two_low, 1), send_outer(two_high, -1)
    far_low, far_high = lax.optimization_barrier((far_low, far_high))
    early_high, early_low = send_outer(one_high, 1), send_outer(three_low, -1)
    late_low = send_outer((one_low.astype(F32) + far_low.astype(F32)).astype(BF16), 1)
    late_high = send_outer((three_high.astype(F32) + far_high.astype(F32)).astype(BF16), -1)
    low = own[:128] + early_low.astype(F32) + late_low.astype(F32)
    high = own[128:] + early_high.astype(F32) + late_high.astype(F32)
    here, one, two, three = low[:64], low[64:], high[:64], high[64:]
    far_low, far_high = send_inner(two[:32], 1), send_inner(two[32:], -1)
    early_high, early_low = send_inner(one[32:], 1), send_inner(three[:32], -1)
    late_low = send_inner(one[:32] + far_low, 1)
    late_high = send_inner(three[32:] + far_high, -1)
    branch = here + jnp.concatenate([early_low + late_low, early_high + late_high], 0)
    mixed = (xfull + branch).astype(BF16).reshape(tokens.shape)
    return (mixed, new_keyval)


def solution(mesh):
    return jax.shard_map(
        body,
        mesh=mesh,
        in_specs=(
            P("yz", None, "gx"),
            P("gx"),
            P("gx", "yz"),
            P("gx", None),
            P("yz", "gx"),
            P(("gx", "yz"), None, None),
            P(("gx", "yz"), None, None),
            P(("gx", "yz")),
        ),
        out_specs=(P("yz", None, "gx"), P(("gx", "yz"), None, None)),
        check_vma=False,
    )
```

```python
import functools

import jax
import jax.numpy as jnp
from jax import lax
from jax.experimental import pallas as pl
from jax.experimental.pallas import tpu as pltpu
from jax.sharding import PartitionSpec as P

D = 18432
HEADS = 48
HEAD = 256
RING = 4
F32 = jnp.float32
BF16 = jnp.bfloat16


def shift(value, move):
    pairs = []
    for x in range(RING):
        for core in range(2):
            for y in range(RING):
                for z in range(RING):
                    dx, dy, dz = move(core)
                    target = (2 * ((x + dx) % RING) + core) * 16
                    target += RING * ((y + dy) % RING) + (z + dz) % RING
                    pairs.append(((2 * x + core) * 16 + RING * y + z, target))
    return lax.ppermute(value, ("gx", "yz"), pairs)


def send_core(value):
    pairs = [(2 * x + c, 2 * x + 1 - c) for x in range(RING) for c in range(2)]
    return lax.ppermute(value, "gx", pairs)


def send_x(value, step):
    return shift(value, lambda core: ((1 - 2 * core) * step, 0, 0))


def send_ahead(value, step):
    return shift(value, lambda core: (step, 0, 0))


def send_inner(value, step):
    return shift(value, lambda core: (0, core * step, (1 - core) * step))


def send_outer(value, step):
    return shift(value, lambda core: (0, (1 - core) * step, core * step))


def exchange(value, along_y):
    groups = [
        [RING * i + k if along_y else RING * k + i for i in range(RING)] for k in range(RING)
    ]
    return lax.all_to_all(
        value, "yz", split_axis=0, concat_axis=0, axis_index_groups=groups, tiled=True
    )


def rotation_tables(positions):
    half = HEAD // 2
    freq = 10000.0 ** (-jnp.arange(half, dtype=F32) * 2.0 / HEAD)
    angle = positions.astype(F32)[..., None] * freq
    return jnp.cos(angle), jnp.sin(angle)


def keyval_kernel(place, rows_ref, w_ref, away_ref, keep_ref, sums_ref):
    x, core = place[0], place[3]
    sums_ref[...] = jnp.dot(rows_ref[...], w_ref[...], preferred_element_type=F32)
    for slot in range(RING):
        block = 2 * lax.rem(x + slot, RING)
        target = pl.ds(8 * slot, 8)
        keep_ref[target, :] = sums_ref[pl.ds(pl.multiple_of(8 * (block + core), 8), 8), :]
        away_ref[target, :] = sums_ref[pl.ds(pl.multiple_of(8 * (block + 1 - core), 8), 8), :]


def project_keyval(place, rows, w_keyval):
    count, depth = rows.shape
    columns = w_keyval.shape[1]
    vmem_spec = pl.BlockSpec(memory_space=pltpu.VMEM)
    half = jax.ShapeDtypeStruct((count // 2, columns), F32)
    return pl.pallas_call(
        keyval_kernel,
        out_shape=[half, half],
        in_specs=[pl.BlockSpec(memory_space=pltpu.SMEM)] + [vmem_spec] * 2,
        out_specs=[vmem_spec] * 2,
        scratch_shapes=[pltpu.VMEM((count, columns), F32)],
        compiler_params=pltpu.CompilerParams(vmem_limit_bytes=12 * 2**20),
        cost_estimate=pl.CostEstimate(
            flops=2 * count * depth * columns, bytes_accessed=3 * 2**20, transcendentals=0
        ),
        name="keyval_projection",
    )(place, rows, w_keyval)


def query_kernel(other, place, *refs):
    pieces, (w_ref, out_ref, rows_ref) = refs[:8], refs[8:]
    x, y, z, core = place[0], place[1], place[2], place[3]
    for index, piece in enumerate(pieces):
        for part in range(2):
            outer = (0, 3, 1, 2)[index % 4]
            inner = ((0, 3), (1, 2))[index // 4][part]
            at_y = lax.rem(y + jnp.where(core == 0, outer, inner), RING)
            at_z = lax.rem(z + jnp.where(core == 0, inner, outer), RING)
            to_core = at_z // 2
            ahead = lax.rem(at_y - x + RING, RING)
            slot = jnp.where(to_core == 0, ahead, lax.rem(RING - ahead, RING))
            position = slot * 2 + lax.rem(at_z, 2)

            @pl.when((to_core != core) == other)
            def _():
                rows_ref[position] = piece[part * 64 : (part + 1) * 64, :]

    rows = rows_ref[...].reshape(512, w_ref.shape[0])
    out_ref[...] = jnp.dot(rows, w_ref[...], preferred_element_type=F32)


def project_query(place, pieces, w_query, other):
    depth, columns = w_query.shape
    vmem_spec = pl.BlockSpec(memory_space=pltpu.VMEM)
    return pl.pallas_call(
        functools.partial(query_kernel, other),
        out_shape=jax.ShapeDtypeStruct((512, columns), F32),
        in_specs=[pl.BlockSpec(memory_space=pltpu.SMEM)] + [vmem_spec] * 9,
        out_specs=vmem_spec,
        scratch_shapes=[pltpu.VMEM((8, 64, depth), BF16)],
        compiler_params=pltpu.CompilerParams(vmem_limit_bytes=20 * 2**20),
        cost_estimate=pl.CostEstimate(
            flops=2 * 512 * depth * columns, bytes_accessed=8 * 2**20, transcendentals=0
        ),
        name="query_projection",
    )(place, *pieces, w_query)


def attend_kernel(lengths, q_ref, cos_ref, sin_ref, kv_ref, k_ref, v_ref, out_ref, new_ref, acc_ref):
    seqs = k_ref.shape[0]
    half = HEAD // 2
    rows = q_ref.shape[0]
    scale = HEAD ** (-0.5)
    contract_last = (((1,), (1,)), ((), ()))
    pick_row = lax.broadcasted_iota(jnp.int32, (32, rows), 0)
    pick_col = lax.broadcasted_iota(jnp.int32, (32, rows), 1)
    odd = lax.rem(lax.broadcasted_iota(jnp.int32, (32, half), 0), 2) == 1
    second_step = lax.rem(lax.broadcasted_iota(jnp.int32, (96, 1), 0), 2) == 1
    first = kv_ref[:, :half].astype(F32)
    second = kv_ref[:, half:HEAD].astype(F32)
    cosine, sine = cos_ref[...], sin_ref[...]
    new_ref[:, :half] = (first * cosine - second * sine).astype(BF16)
    new_ref[:, half:HEAD] = (second * cosine + first * sine).astype(BF16)
    new_ref[:, HEAD:] = kv_ref[:, HEAD:]
    new_rows = new_ref[...].astype(F32)

    def pick_of(r):
        return (pick_col == (pick_row // 2) * 8 + 2 * r + lax.rem(pick_row, 2)).astype(BF16)

    def query_of(r):
        pick = pick_of(r)
        cosine = jnp.where(odd, cos_ref[2 * r + 1 : 2 * r + 2, :], cos_ref[2 * r : 2 * r + 1, :])
        sine = jnp.where(odd, sin_ref[2 * r + 1 : 2 * r + 2, :], sin_ref[2 * r : 2 * r + 1, :])
        parts = []
        for h in range(3):
            chosen = jnp.dot(pick, q_ref[:, h * HEAD : (h + 1) * HEAD], preferred_element_type=F32)
            first, second = chosen[:, :half], chosen[:, half:]
            parts.append(
                jnp.concatenate([first * cosine - second * sine, second * cosine + first * sine], 1)
            )
        return jnp.concatenate(parts, 0).astype(BF16)

    def scores_of(r, query):
        return lax.dot_general(query, k_ref[r], contract_last, preferred_element_type=F32) * scale

    query = query_of(0)
    scores = scores_of(0, query)
    for r in range(seqs):
        if r + 1 < seqs:
            next_query = query_of(r + 1)
            next_scores = scores_of(r + 1, next_query)
        valid = lax.broadcasted_iota(jnp.int32, scores.shape, 1) < lengths[r]
        cached = jnp.where(valid, scores, -jnp.inf)
        new = new_rows[2 * r : 2 * r + 2, :]
        wide = query.astype(F32)
        fresh0 = jnp.sum(wide * new[0:1, :HEAD], -1, keepdims=True) * scale
        fresh1 = jnp.sum(wide * new[1:2, :HEAD], -1, keepdims=True) * scale
        fresh1 = jnp.where(second_step, fresh1, -jnp.inf)
        top = jnp.maximum(jnp.max(cached, -1, keepdims=True), jnp.maximum(fresh0, fresh1))
        exp_cached = jnp.exp(cached - top)
        exp0 = jnp.exp(fresh0 - top)
        exp1 = jnp.exp(fresh1 - top)
        inverse = 1.0 / (jnp.sum(exp_cached, -1, keepdims=True) + exp0 + exp1)
        weights = (exp_cached * inverse).astype(BF16)
        weight0 = (exp0 * inverse).astype(BF16).astype(F32)
        weight1 = (exp1 * inverse).astype(BF16).astype(F32)
        result = jnp.dot(weights, v_ref[r], preferred_element_type=F32)
        result = result + weight0 * new[0:1, HEAD:] + weight1 * new[1:2, HEAD:]
        result = result.astype(BF16)
        pick = pick_of(r)
        for h in range(3):
            spread = lax.dot_general(
                pick,
                result[h * 32 : (h + 1) * 32],
                (((0,), (0,)), ((), ())),
                preferred_element_type=F32,
            )
            columns = slice(h * HEAD, (h + 1) * HEAD)
            if r == 0:
                acc_ref[:, columns] = spread
            else:
                acc_ref[:, columns] += spread
        if r + 1 < seqs:
            query, scores = next_query, next_scores
    out_ref[...] = acc_ref[...].astype(BF16)


def attend(lengths, query, cosine, sine, keyval, keys, values):
    seqs, context, _ = keys.shape
    rows, columns = query.shape
    vmem_spec = pl.BlockSpec(memory_space=pltpu.VMEM)
    return pl.pallas_call(
        attend_kernel,
        out_shape=[
            jax.ShapeDtypeStruct((rows, columns), BF16),
            jax.ShapeDtypeStruct(keyval.shape, BF16),
        ],
        in_specs=[pl.BlockSpec(memory_space=pltpu.SMEM)] + [vmem_spec] * 6,
        out_specs=[vmem_spec] * 2,
        scratch_shapes=[pltpu.VMEM((rows, columns), F32)],
        compiler_params=pltpu.CompilerParams(vmem_limit_bytes=20 * 2**20),
        cost_estimate=pl.CostEstimate(
            flops=4 * seqs * 96 * context * HEAD,
            bytes_accessed=4 * seqs * context * HEAD,
            transcendentals=seqs * 96 * context,
        ),
        name="attention",
    )(lengths, query, cosine, sine, keyval, keys, values)


def output_kernel(groups, place, *refs):
    pieces, (w_ref, *outs), rows_ref = refs[:8], refs[8:-1], refs[-1]
    x, y, z, core = place[0], place[1], place[2], place[3]
    for index, piece in enumerate(pieces):
        at_core = core if index < 4 else 1 - core
        slot = (0, 3, 1, 2)[index % 4]
        ahead = jnp.where(at_core == 0, slot, (RING - slot) % RING)
        dy = lax.rem(x + ahead - y + RING, RING)
        for part in range(2):
            dz = lax.rem(2 * at_core + part - z + RING, RING)
            outer, inner = jnp.where(core == 0, dy, dz), jnp.where(core == 0, dz, dy)
            for position, group in enumerate(groups):

                @pl.when(outer == group)
                def _():
                    rows_ref[position * RING + inner] = piece[part * 64 : (part + 1) * 64, :]

    outs = list(outs)
    for position, group in enumerate(groups):
        rows = rows_ref[RING * position : RING * position + RING].reshape(256, w_ref.shape[0])
        targets = [outs.pop(0)] if group == 0 else [outs.pop(0), outs.pop(0)]
        for start in range(0, w_ref.shape[1], 768):
            columns = slice(start, start + 768)
            result = jnp.dot(rows, w_ref[:, columns], preferred_element_type=F32)
            if group == 0:
                targets[0][:, columns] = result
            else:
                targets[0][:, columns] = result[:128].astype(BF16)
                targets[1][:, columns] = result[128:].astype(BF16)


def project_output(place, pieces, w_out, groups):
    depth, columns = w_out.shape
    vmem_spec = pl.BlockSpec(memory_space=pltpu.VMEM)
    shapes = []
    for group in groups:
        if group == 0:
            shapes.append(jax.ShapeDtypeStruct((256, columns), F32))
        else:
            shapes += [jax.ShapeDtypeStruct((128, columns), BF16)] * 2
    return pl.pallas_call(
        functools.partial(output_kernel, groups),
        out_shape=shapes,
        in_specs=[pl.BlockSpec(memory_space=pltpu.SMEM)] + [vmem_spec] * 9,
        out_specs=[vmem_spec] * len(shapes),
        scratch_shapes=[pltpu.VMEM((RING * len(groups), 64, depth), BF16)],
        compiler_params=pltpu.CompilerParams(vmem_limit_bytes=20 * 2**20),
        cost_estimate=pl.CostEstimate(
            flops=2 * 256 * len(groups) * depth * columns,
            bytes_accessed=8 * 2**20,
            transcendentals=0,
        ),
        name="output_projection",
    )(place, *pieces, w_out)


def body(tokens, gain, w_query, w_keyval, w_out, key_cache, value_cache, lengths):
    seqs = lengths.shape[0]
    gx, yz = lax.axis_index("gx"), lax.axis_index("yz")
    place = jnp.stack([gx // 2, yz // RING, lax.rem(yz, RING), lax.rem(gx, 2)]).astype(jnp.int32)
    positions = jnp.repeat(lengths, 2) + lax.rem(jnp.arange(2 * seqs, dtype=jnp.int32), 2)
    cosine, sine = rotation_tables(positions)

    count = tokens.shape[0] * 2
    features = tokens.shape[2]
    xfull = tokens.reshape(count, features).astype(F32)
    stats = jnp.stack([jnp.sum(xfull, -1), jnp.sum(xfull * xfull, -1)])
    stats = stats + send_core(stats)
    stats, cosine, sine, place = lax.optimization_barrier((stats, cosine, sine, place))
    stats = stats + send_x(stats, 1) + send_x(stats, 2) + send_x(stats, 3)
    mean = stats[0] / D
    var = stats[1] / D - mean * mean
    normed = ((xfull - mean[:, None]) * lax.rsqrt(var + 1e-05)[:, None] * gain).astype(BF16)

    normed = lax.optimization_barrier(normed)
    keyval_away, keyval_keep = project_keyval(place, normed, w_keyval)

    before = send_inner(normed, 1)
    after = send_inner(normed, -1)
    far = send_inner(before, 1)
    near = jnp.concatenate([normed, before], 0)
    near, keyval_away = lax.optimization_barrier((near, keyval_away))
    wide = jnp.concatenate([after, far], 0)
    near_before, near_after = send_outer(near, 1), send_outer(near, -1)
    near_before, near_after = lax.optimization_barrier((near_before, near_after))
    wide_after = send_outer(wide, -1)
    near_far = send_outer(near_before, 1)
    near_far, wide_again = lax.optimization_barrier((near_far, wide))
    wide_before = send_outer(wide_again, 1)
    wide_far = send_outer(wide_after, -1)

    kept = (keyval_keep + send_core(keyval_away)).reshape(RING, count // 8, 2 * HEAD)
    keyval = kept[0] + send_ahead(kept[1], 1) + send_ahead(kept[2], 2) + send_ahead(kept[3], 3)
    keyval = keyval.astype(BF16)

    pieces = [near, near_before, near_after, near_far, wide, wide_before, wide_after, wide_far]
    columns = w_query.shape[1]
    pieces, keyval = lax.optimization_barrier((pieces, keyval))
    away = project_query(place, pieces, w_query, True)
    keep = project_query(place, pieces, w_query, False)
    summed = (keep + send_core(away)).reshape(RING, 128, columns)
    far = send_x(summed[2], 1)
    behind = send_x(summed[3], -1)
    ahead = send_x(summed[1] + far, 1)
    query = (summed[0] + ahead + behind).astype(BF16).reshape(16, 8, columns)
    moves = [
        (g * 16 + j, (j // 2) * 16 + (j % 2) * 8 + g) for g in range(8) for j in range(16)
    ]
    keyval = lax.ppermute(keyval, ("gx", "yz"), moves)
    query, keyval = lax.optimization_barrier((query, keyval))
    query = exchange(query.reshape(RING, RING, 8, columns), True)
    query = exchange(jnp.swapaxes(query, 0, 1), False)

    heads_out, new_keyval = attend(
        lengths, query.reshape(128, columns), cosine, sine, keyval, key_cache, value_cache
    )
    heads_out = exchange(heads_out.reshape(RING, RING, 8, columns), False)
    heads_out = exchange(jnp.swapaxes(heads_out, 0, 1), True).reshape(128, columns)
    before = send_x(heads_out, 1)
    after = send_x(heads_out, -1)
    pieces = [heads_out, before, after, send_x(before, 1)]
    pieces = pieces + [send_core(p) for p in pieces]
    two_low, two_high = project_output(place, pieces, w_out, (2,))
    one_low, one_high, three_low, three_high, own = project_output(
        place, pieces, w_out, (1, 3, 0)
    )

    far_low, far_high = send_outer(two_low, 1), send_outer(two_high, -1)
    far_low, far_high = lax.optimization_barrier((far_low, far_high))
    early_high, early_low = send_outer(one_high, 1), send_outer(three_low, -1)
    late_low = send_outer((one_low.astype(F32) + far_low.astype(F32)).astype(BF16), 1)
    late_high = send_outer((three_high.astype(F32) + far_high.astype(F32)).astype(BF16), -1)
    low = own[:128] + early_low.astype(F32) + late_low.astype(F32)
    high = own[128:] + early_high.astype(F32) + late_high.astype(F32)
    here, one, two, three = low[:64], low[64:], high[:64], high[64:]
    far_low, far_high = send_inner(two[:32], 1), send_inner(two[32:], -1)
    one = jnp.concatenate([one[:32] + far_low, one[32:]], 0)
    three = jnp.concatenate([three[:32], three[32:] + far_high], 0)
    branch = here + send_inner(one, 1) + send_inner(three, -1)
    mixed = (xfull + branch).astype(BF16).reshape(tokens.shape)
    return (mixed, new_keyval.reshape(seqs, 2, 2 * HEAD))


def solution(mesh):
    return jax.shard_map(
        body,
        mesh=mesh,
        in_specs=(
            P("yz", None, "gx"),
            P("gx"),
            P("gx", "yz"),
            P("gx", None),
            P("yz", "gx"),
            P(("gx", "yz"), None, None),
            P(("gx", "yz"), None, None),
            P(("gx", "yz")),
        ),
        out_specs=(P("yz", None, "gx"), P(("gx", "yz"), None, None)),
        check_vma=False,
    )
```

```python
import functools

import jax
import jax.numpy as jnp
from jax import lax
from jax.experimental import pallas as pl
from jax.experimental.pallas import tpu as pltpu
from jax.sharding import PartitionSpec as P

D = 18432
HEADS = 48
HEAD = 256
RING = 4
F32 = jnp.float32
BF16 = jnp.bfloat16


def shift(value, move):
    pairs = []
    for x in range(RING):
        for core in range(2):
            for y in range(RING):
                for z in range(RING):
                    dx, dy, dz = move(core)
                    target = (2 * ((x + dx) % RING) + core) * 16
                    target += RING * ((y + dy) % RING) + (z + dz) % RING
                    pairs.append(((2 * x + core) * 16 + RING * y + z, target))
    return lax.ppermute(value, ("gx", "yz"), pairs)


def send_core(value):
    pairs = [(2 * x + c, 2 * x + 1 - c) for x in range(RING) for c in range(2)]
    return lax.ppermute(value, "gx", pairs)


def send_x(value, step):
    return shift(value, lambda core: ((1 - 2 * core) * step, 0, 0))


def send_ahead(value, step):
    return shift(value, lambda core: (step, 0, 0))


def send_inner(value, step):
    return shift(value, lambda core: (0, core * step, (1 - core) * step))


def send_outer(value, step):
    return shift(value, lambda core: (0, (1 - core) * step, core * step))


def rotation_tables(positions):
    half = HEAD // 2
    freq = 10000.0 ** (-jnp.arange(half, dtype=F32) * 2.0 / HEAD)
    angle = positions.astype(F32)[..., None] * freq
    return jnp.cos(angle), jnp.sin(angle)


def sums_kernel(rows_ref, out_ref):
    rows = rows_ref[...].astype(F32)
    total = jnp.sum(rows, -1, keepdims=True)
    squares = jnp.sum(rows * rows, -1, keepdims=True)
    out_ref[...] = jnp.concatenate([total, squares], 1)


def row_sums(rows):
    vmem_spec = pl.BlockSpec(memory_space=pltpu.VMEM)
    return pl.pallas_call(
        sums_kernel,
        out_shape=jax.ShapeDtypeStruct((rows.shape[0], 2), F32),
        in_specs=[vmem_spec],
        out_specs=vmem_spec,
        compiler_params=pltpu.CompilerParams(vmem_limit_bytes=12 * 2**20),
        name="row_sums",
    )(rows)


def normalize_kernel(one_ref, two_ref, one_sums, two_sums, gain_ref, out_ref):
    count = one_ref.shape[0]
    for index, (rows_ref, sums_ref) in enumerate(((one_ref, one_sums), (two_ref, two_sums))):
        mean = sums_ref[:, 0:1] / D
        var = sums_ref[:, 1:2] / D - mean * mean
        rows = rows_ref[...].astype(F32)
        normed = (rows - mean) * lax.rsqrt(var + 1e-05) * gain_ref[...]
        out_ref[index * count : (index + 1) * count, :] = normed.astype(BF16)


def normalize(one, two, one_sums, two_sums, gain):
    vmem_spec = pl.BlockSpec(memory_space=pltpu.VMEM)
    return pl.pallas_call(
        normalize_kernel,
        out_shape=jax.ShapeDtypeStruct((2 * one.shape[0], one.shape[1]), BF16),
        in_specs=[vmem_spec] * 5,
        out_specs=vmem_spec,
        compiler_params=pltpu.CompilerParams(vmem_limit_bytes=12 * 2**20),
        name="normalize",
    )(one, two, one_sums, two_sums, gain)


def keyval_kernel(place, rows_ref, w_ref, away_ref, keep_ref, sums_ref):
    x, core = place[0], place[3]
    rows = rows_ref[: sums_ref.shape[0], :]
    sums_ref[...] = jnp.dot(rows, w_ref[...], preferred_element_type=F32)
    for slot in range(RING):
        block = 2 * lax.rem(x + slot, RING)
        target = pl.ds(8 * slot, 8)
        keep_ref[target, :] = sums_ref[pl.ds(pl.multiple_of(8 * (block + core), 8), 8), :]
        away_ref[target, :] = sums_ref[pl.ds(pl.multiple_of(8 * (block + 1 - core), 8), 8), :]


def project_keyval(place, rows, w_keyval):
    count, depth = rows.shape[0] // 2, rows.shape[1]
    columns = w_keyval.shape[1]
    vmem_spec = pl.BlockSpec(memory_space=pltpu.VMEM)
    half = jax.ShapeDtypeStruct((count // 2, columns), F32)
    return pl.pallas_call(
        keyval_kernel,
        out_shape=[half, half],
        in_specs=[pl.BlockSpec(memory_space=pltpu.SMEM)] + [vmem_spec] * 2,
        out_specs=[vmem_spec] * 2,
        scratch_shapes=[pltpu.VMEM((count, columns), F32)],
        compiler_params=pltpu.CompilerParams(vmem_limit_bytes=12 * 2**20),
        cost_estimate=pl.CostEstimate(
            flops=2 * count * depth * columns, bytes_accessed=3 * 2**20, transcendentals=0
        ),
        name="keyval_projection",
    )(place, rows, w_keyval)


def query_kernel(pair, place, *refs):
    pieces, (w_ref, away_ref, keep_ref, rows_ref) = refs[:8], refs[8:]
    x, y, z, core = place[0], place[1], place[2], place[3]
    for index, piece in enumerate(pieces):
        for part in range(2):
            outer = (0, 3, 1, 2)[index % 4]
            inner = ((0, 3), (1, 2))[index // 4][part]
            at_y = lax.rem(y + jnp.where(core == 0, outer, inner), RING)
            at_z = lax.rem(z + jnp.where(core == 0, inner, outer), RING)
            to_core = at_z // 2
            ahead = lax.rem(at_y - x + RING, RING)
            slot = jnp.where(to_core == 0, ahead, lax.rem(RING - ahead, RING))
            mine = jnp.where(to_core == core, 4, 0)
            position = mine + lax.rem(slot, 2) * 2 + lax.rem(at_z, 2)

            @pl.when(slot // 2 == pair)
            def _():
                rows_ref[position] = piece[part * 64 : (part + 1) * 64, :]

    rows = rows_ref[...].reshape(512, w_ref.shape[0])
    result = jnp.dot(rows, w_ref[...], preferred_element_type=F32)
    away_ref[...] = result[:256]
    keep_ref[...] = result[256:]


def project_query(place, pieces, w_query, pair):
    depth, columns = w_query.shape
    vmem_spec = pl.BlockSpec(memory_space=pltpu.VMEM)
    half = jax.ShapeDtypeStruct((256, columns), F32)
    return pl.pallas_call(
        functools.partial(query_kernel, pair),
        out_shape=[half, half],
        in_specs=[pl.BlockSpec(memory_space=pltpu.SMEM)] + [vmem_spec] * 9,
        out_specs=[vmem_spec] * 2,
        scratch_shapes=[pltpu.VMEM((8, 64, depth), BF16)],
        compiler_params=pltpu.CompilerParams(vmem_limit_bytes=20 * 2**20),
        cost_estimate=pl.CostEstimate(
            flops=2 * 512 * depth * columns, bytes_accessed=8 * 2**20, transcendentals=0
        ),
        name="query_projection",
    )(place, *pieces, w_query)


def attend_kernel(lengths, q_ref, cos_ref, sin_ref, kv_ref, k_ref, v_ref, out_ref, new_ref, acc_ref):
    seqs = k_ref.shape[0]
    half = HEAD // 2
    rows = q_ref.shape[0]
    scale = HEAD ** (-0.5)
    contract_last = (((1,), (1,)), ((), ()))
    pick_row = lax.broadcasted_iota(jnp.int32, (32, rows), 0)
    pick_col = lax.broadcasted_iota(jnp.int32, (32, rows), 1)
    odd = lax.rem(lax.broadcasted_iota(jnp.int32, (32, half), 0), 2) == 1
    second_step = lax.rem(lax.broadcasted_iota(jnp.int32, (96, 1), 0), 2) == 1
    first = kv_ref[:, :half].astype(F32)
    second = kv_ref[:, half:HEAD].astype(F32)
    cosine, sine = cos_ref[...], sin_ref[...]
    new_ref[:, :half] = (first * cosine - second * sine).astype(BF16)
    new_ref[:, half:HEAD] = (second * cosine + first * sine).astype(BF16)
    new_ref[:, HEAD:] = kv_ref[:, HEAD:]
    new_rows = new_ref[...].astype(F32)

    def pick_of(r):
        return (pick_col == (pick_row // 2) * 8 + 2 * r + lax.rem(pick_row, 2)).astype(BF16)

    def query_of(r):
        pick = pick_of(r)
        cosine = jnp.where(odd, cos_ref[2 * r + 1 : 2 * r + 2, :], cos_ref[2 * r : 2 * r + 1, :])
        sine = jnp.where(odd, sin_ref[2 * r + 1 : 2 * r + 2, :], sin_ref[2 * r : 2 * r + 1, :])
        parts = []
        for h in range(3):
            chosen = jnp.dot(pick, q_ref[:, h * HEAD : (h + 1) * HEAD], preferred_element_type=F32)
            first, second = chosen[:, :half], chosen[:, half:]
            parts.append(
                jnp.concatenate([first * cosine - second * sine, second * cosine + first * sine], 1)
            )
        return jnp.concatenate(parts, 0).astype(BF16)

    def scores_of(r, query):
        return lax.dot_general(query, k_ref[r], contract_last, preferred_element_type=F32) * scale

    query = query_of(0)
    scores = scores_of(0, query)
    for r in range(seqs):
        if r + 1 < seqs:
            next_query = query_of(r + 1)
            next_scores = scores_of(r + 1, next_query)
        valid = lax.broadcasted_iota(jnp.int32, scores.shape, 1) < lengths[r]
        cached = jnp.where(valid, scores, -jnp.inf)
        new = new_rows[2 * r : 2 * r + 2, :]
        wide = query.astype(F32)
        fresh0 = jnp.sum(wide * new[0:1, :HEAD], -1, keepdims=True) * scale
        fresh1 = jnp.sum(wide * new[1:2, :HEAD], -1, keepdims=True) * scale
        fresh1 = jnp.where(second_step, fresh1, -jnp.inf)
        top = jnp.maximum(jnp.max(cached, -1, keepdims=True), jnp.maximum(fresh0, fresh1))
        exp_cached = jnp.exp(cached - top)
        exp0 = jnp.exp(fresh0 - top)
        exp1 = jnp.exp(fresh1 - top)
        inverse = 1.0 / (jnp.sum(exp_cached, -1, keepdims=True) + exp0 + exp1)
        weights = (exp_cached * inverse).astype(BF16)
        weight0 = (exp0 * inverse).astype(BF16).astype(F32)
        weight1 = (exp1 * inverse).astype(BF16).astype(F32)
        result = jnp.dot(weights, v_ref[r], preferred_element_type=F32)
        result = result + weight0 * new[0:1, HEAD:] + weight1 * new[1:2, HEAD:]
        result = result.astype(BF16)
        pick = pick_of(r)
        for h in range(3):
            spread = lax.dot_general(
                pick,
                result[h * 32 : (h + 1) * 32],
                (((0,), (0,)), ((), ())),
                preferred_element_type=F32,
            )
            columns = slice(h * HEAD, (h + 1) * HEAD)
            if r == 0:
                acc_ref[:, columns] = spread
            else:
                acc_ref[:, columns] += spread
        if r + 1 < seqs:
            query, scores = next_query, next_scores
    out_ref[...] = acc_ref[...].astype(BF16)


def attend(lengths, query, cosine, sine, keyval, keys, values):
    seqs, context, _ = keys.shape
    rows, columns = query.shape
    vmem_spec = pl.BlockSpec(memory_space=pltpu.VMEM)
    return pl.pallas_call(
        attend_kernel,
        out_shape=[
            jax.ShapeDtypeStruct((rows, columns), BF16),
            jax.ShapeDtypeStruct(keyval.shape, BF16),
        ],
        in_specs=[pl.BlockSpec(memory_space=pltpu.SMEM)] + [vmem_spec] * 6,
        out_specs=[vmem_spec] * 2,
        scratch_shapes=[pltpu.VMEM((rows, columns), F32)],
        compiler_params=pltpu.CompilerParams(vmem_limit_bytes=20 * 2**20),
        cost_estimate=pl.CostEstimate(
            flops=4 * seqs * 96 * context * HEAD,
            bytes_accessed=4 * seqs * context * HEAD,
            transcendentals=seqs * 96 * context,
        ),
        name="attention",
    )(lengths, query, cosine, sine, keyval, keys, values)


def output_kernel(groups, place, *refs):
    pieces, (w_ref, *outs), rows_ref = refs[:8], refs[8:-1], refs[-1]
    x, y, z, core = place[0], place[1], place[2], place[3]
    for index, piece in enumerate(pieces):
        at_core = core if index < 4 else 1 - core
        slot = (0, 3, 1, 2)[index % 4]
        ahead = jnp.where(at_core == 0, slot, (RING - slot) % RING)
        dy = lax.rem(x + ahead - y + RING, RING)
        for part in range(2):
            dz = lax.rem(2 * at_core + part - z + RING, RING)
            outer, inner = jnp.where(core == 0, dy, dz), jnp.where(core == 0, dz, dy)
            for position, group in enumerate(groups):

                @pl.when(outer == group)
                def _():
                    rows_ref[position * RING + inner] = piece[part * 64 : (part + 1) * 64, :]

    outs = list(outs)
    for position, group in enumerate(groups):
        rows = rows_ref[RING * position : RING * position + RING].reshape(256, w_ref.shape[0])
        targets = [outs.pop(0)] if group == 0 else [outs.pop(0), outs.pop(0)]
        for start in range(0, w_ref.shape[1], 768):
            columns = slice(start, start + 768)
            result = jnp.dot(rows, w_ref[:, columns], preferred_element_type=F32)
            if group == 0:
                targets[0][:, columns] = result
            else:
                targets[0][:, columns] = result[:128].astype(BF16)
                targets[1][:, columns] = result[128:].astype(BF16)


def project_output(place, pieces, w_out, groups):
    depth, columns = w_out.shape
    vmem_spec = pl.BlockSpec(memory_space=pltpu.VMEM)
    shapes = []
    for group in groups:
        if group == 0:
            shapes.append(jax.ShapeDtypeStruct((256, columns), F32))
        else:
            shapes += [jax.ShapeDtypeStruct((128, columns), BF16)] * 2
    return pl.pallas_call(
        functools.partial(output_kernel, groups),
        out_shape=shapes,
        in_specs=[pl.BlockSpec(memory_space=pltpu.SMEM)] + [vmem_spec] * 9,
        out_specs=[vmem_spec] * len(shapes),
        scratch_shapes=[pltpu.VMEM((RING * len(groups), 64, depth), BF16)],
        compiler_params=pltpu.CompilerParams(vmem_limit_bytes=20 * 2**20),
        cost_estimate=pl.CostEstimate(
            flops=2 * 256 * len(groups) * depth * columns,
            bytes_accessed=8 * 2**20,
            transcendentals=0,
        ),
        name="output_projection",
    )(place, *pieces, w_out)


def body(tokens, gain, w_query, w_keyval, w_out, key_cache, value_cache, lengths):
    seqs = lengths.shape[0]
    gx, yz = lax.axis_index("gx"), lax.axis_index("yz")
    place = jnp.stack([gx // 2, yz // RING, lax.rem(yz, RING), lax.rem(gx, 2)]).astype(jnp.int32)
    positions = jnp.repeat(lengths, 2) + lax.rem(jnp.arange(2 * seqs, dtype=jnp.int32), 2)
    cosine, sine = rotation_tables(positions)

    count = tokens.shape[0] * 2
    features = tokens.shape[2]
    raw = lax.optimization_barrier(tokens.reshape(count, features))
    sums = row_sums(raw)
    before, after = send_inner(raw, 1), send_inner(raw, -1)
    sums = sums + send_core(sums)
    sums, cosine, sine, place = lax.optimization_barrier((sums, cosine, sine, place))
    sums = sums + send_x(sums, 1) + send_x(sums, 2) + send_x(sums, 3)
    sums, before, after = lax.optimization_barrier((sums, before, after))
    far = send_inner(before, 1)
    scale = gain.reshape(1, features)
    near = normalize(raw, before, sums, send_inner(sums, 1), scale)
    near, far = lax.optimization_barrier((near, far))
    wide = normalize(after, far, send_inner(sums, -1), send_inner(sums, 2), scale)

    keyval_away, keyval_keep = project_keyval(place, near, w_keyval)

    near_before, near_after = send_outer(near, 1), send_outer(near, -1)
    near_before, near_after = lax.optimization_barrier((near_before, near_after))
    wide_after = send_outer(wide, -1)
    near_far = send_outer(near_before, 1)
    near_far, wide_again = lax.optimization_barrier((near_far, wide))
    wide_before = send_outer(wide_again, 1)
    wide_far = send_outer(wide_after, -1)

    kept = (keyval_keep + send_core(keyval_away)).reshape(RING, count // 8, 2 * HEAD)
    keyval = kept[0] + send_ahead(kept[1], 1) + send_ahead(kept[2], 2) + send_ahead(kept[3], 3)
    keyval = keyval.astype(BF16)

    pieces = [near, near_before, near_after, near_far, wide, wide_before, wide_after, wide_far]
    columns = w_query.shape[1]
    pieces, keyval = lax.optimization_barrier((pieces, keyval))
    away, keep = project_query(place, pieces, w_query, 1)
    summed = (keep + send_core(away)).reshape(2, 128, columns)
    far, behind = send_x(summed[0], 1), send_x(summed[1], -1)
    away, keep = project_query(place, pieces, w_query, 0)
    summed = (keep + send_core(away)).reshape(2, 128, columns)
    ahead = send_x(summed[1] + far, 1)
    query = (summed[0] + ahead + behind).astype(BF16).reshape(16, 8, columns)
    moves = [
        (g * 16 + j, (j // 2) * 16 + (j % 2) * 8 + g) for g in range(8) for j in range(16)
    ]
    keyval = lax.ppermute(keyval, ("gx", "yz"), moves)
    query, keyval = lax.optimization_barrier((query, keyval))
    query = lax.all_to_all(query, "yz", split_axis=0, concat_axis=0)

    heads_out, new_keyval = attend(
        lengths, query.reshape(128, columns), cosine, sine, keyval, key_cache, value_cache
    )
    heads_out = lax.all_to_all(
        heads_out.reshape(16, 8, columns), "yz", split_axis=0, concat_axis=0
    ).reshape(128, columns)
    before = send_x(heads_out, 1)
    after = send_x(heads_out, -1)
    pieces = [heads_out, before, after, send_x(before, 1)]
    pieces = pieces + [send_core(p) for p in pieces]
    two_low, two_high = project_output(place, pieces, w_out, (2,))
    one_low, one_high, three_low, three_high, own = project_output(
        place, pieces, w_out, (1, 3, 0)
    )

    far_low, far_high = send_outer(two_low, 1), send_outer(two_high, -1)
    far_low, far_high = lax.optimization_barrier((far_low, far_high))
    early_high, early_low = send_outer(one_high, 1), send_outer(three_low, -1)
    late_low = send_outer((one_low.astype(F32) + far_low.astype(F32)).astype(BF16), 1)
    late_high = send_outer((three_high.astype(F32) + far_high.astype(F32)).astype(BF16), -1)
    low = own[:128] + early_low.astype(F32) + late_low.astype(F32)
    high = own[128:] + early_high.astype(F32) + late_high.astype(F32)
    here, one, two, three = low[:64], low[64:], high[:64], high[64:]
    far_low, far_high = send_inner(two[:32], 1), send_inner(two[32:], -1)
    one = jnp.concatenate([one[:32] + far_low, one[32:]], 0)
    three = jnp.concatenate([three[:32], three[32:] + far_high], 0)
    branch = here + send_inner(one, 1) + send_inner(three, -1)
    mixed = (raw.astype(F32) + branch).astype(BF16).reshape(tokens.shape)
    return (mixed, new_keyval.reshape(seqs, 2, 2 * HEAD))


def solution(mesh):
    return jax.shard_map(
        body,
        mesh=mesh,
        in_specs=(
            P("yz", None, "gx"),
            P("gx"),
            P("gx", "yz"),
            P("gx", None),
            P("yz", "gx"),
            P(("gx", "yz"), None, None),
            P(("gx", "yz"), None, None),
            P(("gx", "yz")),
        ),
        out_specs=(P("yz", None, "gx"), P(("gx", "yz"), None, None)),
        check_vma=False,
    )
```

```python
import functools

import jax
import jax.numpy as jnp
from jax import lax
from jax.experimental import pallas as pl
from jax.experimental.pallas import tpu as pltpu
from jax.sharding import PartitionSpec as P

D = 18432
HEADS = 48
HEAD = 256
RING = 4
F32 = jnp.float32
BF16 = jnp.bfloat16


def shift(value, move):
    pairs = []
    for x in range(RING):
        for core in range(2):
            for y in range(RING):
                for z in range(RING):
                    dx, dy, dz = move(core)
                    target = (2 * ((x + dx) % RING) + core) * 16
                    target += RING * ((y + dy) % RING) + (z + dz) % RING
                    pairs.append(((2 * x + core) * 16 + RING * y + z, target))
    return lax.ppermute(value, ("gx", "yz"), pairs)


def send_core(value):
    pairs = [(2 * x + c, 2 * x + 1 - c) for x in range(RING) for c in range(2)]
    return lax.ppermute(value, "gx", pairs)


def send_x(value, step):
    return shift(value, lambda core: ((1 - 2 * core) * step, 0, 0))


def send_ahead(value, step):
    return shift(value, lambda core: (step, 0, 0))


def send_inner(value, step):
    return shift(value, lambda core: (0, core * step, (1 - core) * step))


def send_outer(value, step):
    return shift(value, lambda core: (0, (1 - core) * step, core * step))


def rotation_tables(positions):
    half = HEAD // 2
    freq = 10000.0 ** (-jnp.arange(half, dtype=F32) * 2.0 / HEAD)
    angle = positions.astype(F32)[..., None] * freq
    return jnp.cos(angle), jnp.sin(angle)


def sums_kernel(rows_ref, out_ref):
    rows = rows_ref[...].astype(F32)
    total = jnp.sum(rows, -1, keepdims=True)
    squares = jnp.sum(rows * rows, -1, keepdims=True)
    out_ref[...] = jnp.concatenate([total, squares], 1)


def row_sums(rows):
    vmem_spec = pl.BlockSpec(memory_space=pltpu.VMEM)
    return pl.pallas_call(
        sums_kernel,
        out_shape=jax.ShapeDtypeStruct((rows.shape[0], 2), F32),
        in_specs=[vmem_spec],
        out_specs=vmem_spec,
        compiler_params=pltpu.CompilerParams(vmem_limit_bytes=12 * 2**20),
        name="row_sums",
    )(rows)


def normalize_kernel(one_ref, two_ref, one_sums, two_sums, gain_ref, out_ref):
    count = one_ref.shape[0]
    for index, (rows_ref, sums_ref) in enumerate(((one_ref, one_sums), (two_ref, two_sums))):
        mean = sums_ref[:, 0:1] / D
        var = sums_ref[:, 1:2] / D - mean * mean
        rows = rows_ref[...].astype(F32)
        normed = (rows - mean) * lax.rsqrt(var + 1e-05) * gain_ref[...]
        out_ref[index * count : (index + 1) * count, :] = normed.astype(BF16)


def normalize(one, two, one_sums, two_sums, gain):
    vmem_spec = pl.BlockSpec(memory_space=pltpu.VMEM)
    return pl.pallas_call(
        normalize_kernel,
        out_shape=jax.ShapeDtypeStruct((2 * one.shape[0], one.shape[1]), BF16),
        in_specs=[vmem_spec] * 5,
        out_specs=vmem_spec,
        compiler_params=pltpu.CompilerParams(vmem_limit_bytes=12 * 2**20),
        name="normalize",
    )(one, two, one_sums, two_sums, gain)


def keyval_kernel(place, rows_ref, w_ref, away_ref, keep_ref, sums_ref):
    x, core = place[0], place[3]
    rows = rows_ref[: sums_ref.shape[0], :]
    sums_ref[...] = jnp.dot(rows, w_ref[...], preferred_element_type=F32)
    for slot in range(RING):
        block = 2 * lax.rem(x + slot, RING)
        target = pl.ds(8 * slot, 8)
        keep_ref[target, :] = sums_ref[pl.ds(pl.multiple_of(8 * (block + core), 8), 8), :]
        away_ref[target, :] = sums_ref[pl.ds(pl.multiple_of(8 * (block + 1 - core), 8), 8), :]


def project_keyval(place, rows, w_keyval):
    count, depth = rows.shape[0] // 2, rows.shape[1]
    columns = w_keyval.shape[1]
    vmem_spec = pl.BlockSpec(memory_space=pltpu.VMEM)
    half = jax.ShapeDtypeStruct((count // 2, columns), F32)
    return pl.pallas_call(
        keyval_kernel,
        out_shape=[half, half],
        in_specs=[pl.BlockSpec(memory_space=pltpu.SMEM)] + [vmem_spec] * 2,
        out_specs=[vmem_spec] * 2,
        scratch_shapes=[pltpu.VMEM((count, columns), F32)],
        compiler_params=pltpu.CompilerParams(vmem_limit_bytes=12 * 2**20),
        cost_estimate=pl.CostEstimate(
            flops=2 * count * depth * columns, bytes_accessed=3 * 2**20, transcendentals=0
        ),
        name="keyval_projection",
    )(place, rows, w_keyval)


def query_kernel(pair, place, *refs):
    pieces, (w_ref, away_ref, keep_ref, rows_ref) = refs[:8], refs[8:]
    x, y, z, core = place[0], place[1], place[2], place[3]
    for index, piece in enumerate(pieces):
        for part in range(2):
            outer = (0, 3, 1, 2)[index % 4]
            inner = ((0, 3), (1, 2))[index // 4][part]
            at_y = lax.rem(y + jnp.where(core == 0, outer, inner), RING)
            at_z = lax.rem(z + jnp.where(core == 0, inner, outer), RING)
            to_core = at_z // 2
            ahead = lax.rem(at_y - x + RING, RING)
            slot = jnp.where(to_core == 0, ahead, lax.rem(RING - ahead, RING))
            mine = jnp.where(to_core == core, 4, 0)
            position = mine + lax.rem(slot, 2) * 2 + lax.rem(at_z, 2)

            @pl.when(slot // 2 == pair)
            def _():
                rows_ref[position] = piece[part * 64 : (part + 1) * 64, :]

    rows = rows_ref[...].reshape(512, w_ref.shape[0])
    result = jnp.dot(rows, w_ref[...], preferred_element_type=F32)
    away_ref[...] = result[:256]
    keep_ref[...] = result[256:]


def project_query(place, pieces, w_query, pair):
    depth, columns = w_query.shape
    vmem_spec = pl.BlockSpec(memory_space=pltpu.VMEM)
    half = jax.ShapeDtypeStruct((256, columns), F32)
    return pl.pallas_call(
        functools.partial(query_kernel, pair),
        out_shape=[half, half],
        in_specs=[pl.BlockSpec(memory_space=pltpu.SMEM)] + [vmem_spec] * 9,
        out_specs=[vmem_spec] * 2,
        scratch_shapes=[pltpu.VMEM((8, 64, depth), BF16)],
        compiler_params=pltpu.CompilerParams(vmem_limit_bytes=20 * 2**20),
        cost_estimate=pl.CostEstimate(
            flops=2 * 512 * depth * columns, bytes_accessed=8 * 2**20, transcendentals=0
        ),
        name="query_projection",
    )(place, *pieces, w_query)


def attend_kernel(lengths, q_ref, cos_ref, sin_ref, kv_ref, k_ref, v_ref, out_ref, new_ref, acc_ref):
    seqs = k_ref.shape[0]
    half = HEAD // 2
    rows = q_ref.shape[0]
    scale = HEAD ** (-0.5)
    contract_last = (((1,), (1,)), ((), ()))
    pick_row = lax.broadcasted_iota(jnp.int32, (32, rows), 0)
    pick_col = lax.broadcasted_iota(jnp.int32, (32, rows), 1)
    odd = lax.rem(lax.broadcasted_iota(jnp.int32, (32, half), 0), 2) == 1
    second_step = lax.rem(lax.broadcasted_iota(jnp.int32, (96, 1), 0), 2) == 1
    first = kv_ref[:, :half].astype(F32)
    second = kv_ref[:, half:HEAD].astype(F32)
    cosine, sine = cos_ref[...], sin_ref[...]
    new_ref[:, :half] = (first * cosine - second * sine).astype(BF16)
    new_ref[:, half:HEAD] = (second * cosine + first * sine).astype(BF16)
    new_ref[:, HEAD:] = kv_ref[:, HEAD:]
    new_rows = new_ref[...].astype(F32)

    def pick_of(r):
        return (pick_col == (pick_row // 2) * 8 + 2 * r + lax.rem(pick_row, 2)).astype(BF16)

    def query_of(r):
        pick = pick_of(r)
        cosine = jnp.where(odd, cos_ref[2 * r + 1 : 2 * r + 2, :], cos_ref[2 * r : 2 * r + 1, :])
        sine = jnp.where(odd, sin_ref[2 * r + 1 : 2 * r + 2, :], sin_ref[2 * r : 2 * r + 1, :])
        parts = []
        for h in range(3):
            chosen = jnp.dot(pick, q_ref[:, h * HEAD : (h + 1) * HEAD], preferred_element_type=F32)
            first, second = chosen[:, :half], chosen[:, half:]
            parts.append(
                jnp.concatenate([first * cosine - second * sine, second * cosine + first * sine], 1)
            )
        return jnp.concatenate(parts, 0).astype(BF16)

    def scores_of(r, query):
        return lax.dot_general(query, k_ref[r], contract_last, preferred_element_type=F32) * scale

    query = query_of(0)
    scores = scores_of(0, query)
    for r in range(seqs):
        if r + 1 < seqs:
            next_query = query_of(r + 1)
            next_scores = scores_of(r + 1, next_query)
        valid = lax.broadcasted_iota(jnp.int32, scores.shape, 1) < lengths[r]
        cached = jnp.where(valid, scores, -jnp.inf)
        new = new_rows[2 * r : 2 * r + 2, :]
        wide = query.astype(F32)
        fresh0 = jnp.sum(wide * new[0:1, :HEAD], -1, keepdims=True) * scale
        fresh1 = jnp.sum(wide * new[1:2, :HEAD], -1, keepdims=True) * scale
        fresh1 = jnp.where(second_step, fresh1, -jnp.inf)
        top = jnp.maximum(jnp.max(cached, -1, keepdims=True), jnp.maximum(fresh0, fresh1))
        exp_cached = jnp.exp(cached - top)
        exp0 = jnp.exp(fresh0 - top)
        exp1 = jnp.exp(fresh1 - top)
        inverse = 1.0 / (jnp.sum(exp_cached, -1, keepdims=True) + exp0 + exp1)
        weights = (exp_cached * inverse).astype(BF16)
        weight0 = (exp0 * inverse).astype(BF16).astype(F32)
        weight1 = (exp1 * inverse).astype(BF16).astype(F32)
        result = jnp.dot(weights, v_ref[r], preferred_element_type=F32)
        result = result + weight0 * new[0:1, HEAD:] + weight1 * new[1:2, HEAD:]
        result = result.astype(BF16)
        pick = pick_of(r)
        for h in range(3):
            spread = lax.dot_general(
                pick,
                result[h * 32 : (h + 1) * 32],
                (((0,), (0,)), ((), ())),
                preferred_element_type=F32,
            )
            columns = slice(h * HEAD, (h + 1) * HEAD)
            if r == 0:
                acc_ref[:, columns] = spread
            else:
                acc_ref[:, columns] += spread
        if r + 1 < seqs:
            query, scores = next_query, next_scores
    out_ref[...] = acc_ref[...].astype(BF16)


def attend(lengths, query, cosine, sine, keyval, keys, values):
    seqs, context, _ = keys.shape
    rows, columns = query.shape
    vmem_spec = pl.BlockSpec(memory_space=pltpu.VMEM)
    return pl.pallas_call(
        attend_kernel,
        out_shape=[
            jax.ShapeDtypeStruct((rows, columns), BF16),
            jax.ShapeDtypeStruct(keyval.shape, BF16),
        ],
        in_specs=[pl.BlockSpec(memory_space=pltpu.SMEM)] + [vmem_spec] * 6,
        out_specs=[vmem_spec] * 2,
        scratch_shapes=[pltpu.VMEM((rows, columns), F32)],
        compiler_params=pltpu.CompilerParams(vmem_limit_bytes=20 * 2**20),
        cost_estimate=pl.CostEstimate(
            flops=4 * seqs * 96 * context * HEAD,
            bytes_accessed=4 * seqs * context * HEAD,
            transcendentals=seqs * 96 * context,
        ),
        name="attention",
    )(lengths, query, cosine, sine, keyval, keys, values)


def output_kernel(groups, place, *refs):
    pieces, (w_ref, *outs), rows_ref = refs[:8], refs[8:-1], refs[-1]
    x, y, z, core = place[0], place[1], place[2], place[3]
    for index, piece in enumerate(pieces):
        at_core = core if index < 4 else 1 - core
        slot = (0, 3, 1, 2)[index % 4]
        ahead = jnp.where(at_core == 0, slot, (RING - slot) % RING)
        dy = lax.rem(x + ahead - y + RING, RING)
        for part in range(2):
            dz = lax.rem(2 * at_core + part - z + RING, RING)
            outer, inner = jnp.where(core == 0, dy, dz), jnp.where(core == 0, dz, dy)
            for position, group in enumerate(groups):

                @pl.when(outer == group)
                def _():
                    rows_ref[position * RING + inner] = piece[part * 64 : (part + 1) * 64, :]

    outs = list(outs)
    for position, group in enumerate(groups):
        rows = rows_ref[RING * position : RING * position + RING].reshape(256, w_ref.shape[0])
        targets = [outs.pop(0)] if group == 0 else [outs.pop(0), outs.pop(0)]
        for start in range(0, w_ref.shape[1], 768):
            columns = slice(start, start + 768)
            result = jnp.dot(rows, w_ref[:, columns], preferred_element_type=F32)
            if group == 0:
                targets[0][:, columns] = result
            else:
                targets[0][:, columns] = result[:128].astype(BF16)
                targets[1][:, columns] = result[128:].astype(BF16)


def project_output(place, pieces, w_out, groups):
    depth, columns = w_out.shape
    vmem_spec = pl.BlockSpec(memory_space=pltpu.VMEM)
    shapes = []
    for group in groups:
        if group == 0:
            shapes.append(jax.ShapeDtypeStruct((256, columns), F32))
        else:
            shapes += [jax.ShapeDtypeStruct((128, columns), BF16)] * 2
    return pl.pallas_call(
        functools.partial(output_kernel, groups),
        out_shape=shapes,
        in_specs=[pl.BlockSpec(memory_space=pltpu.SMEM)] + [vmem_spec] * 9,
        out_specs=[vmem_spec] * len(shapes),
        scratch_shapes=[pltpu.VMEM((RING * len(groups), 64, depth), BF16)],
        compiler_params=pltpu.CompilerParams(vmem_limit_bytes=20 * 2**20),
        cost_estimate=pl.CostEstimate(
            flops=2 * 256 * len(groups) * depth * columns,
            bytes_accessed=8 * 2**20,
            transcendentals=0,
        ),
        name="output_projection",
    )(place, *pieces, w_out)


def body(tokens, gain, w_query, w_keyval, w_out, key_cache, value_cache, lengths):
    seqs = lengths.shape[0]
    gx, yz = lax.axis_index("gx"), lax.axis_index("yz")
    place = jnp.stack([gx // 2, yz // RING, lax.rem(yz, RING), lax.rem(gx, 2)]).astype(jnp.int32)
    positions = jnp.repeat(lengths, 2) + lax.rem(jnp.arange(2 * seqs, dtype=jnp.int32), 2)
    cosine, sine = rotation_tables(positions)

    count = tokens.shape[0] * 2
    features = tokens.shape[2]
    raw = lax.optimization_barrier(tokens.reshape(count, features))
    sums = row_sums(raw)
    sums = sums + send_core(sums)
    sums, cosine, sine, place, raw = lax.optimization_barrier((sums, cosine, sine, place, raw))
    before, after = send_inner(raw, 1), send_inner(raw, -1)
    sums = sums + send_x(sums, 1) + send_x(sums, 2) + send_x(sums, 3)
    sums, before, after = lax.optimization_barrier((sums, before, after))
    before_sums, after_sums = send_inner(sums, 1), send_inner(sums, -1)
    before, before_sums = lax.optimization_barrier((before, before_sums))
    far, far_sums = send_inner(before, 1), send_inner(sums, 2)
    scale = gain.reshape(1, features)
    near = normalize(raw, before, sums, before_sums, scale)
    wide = normalize(after, far, after_sums, far_sums, scale)

    keyval_away, keyval_keep = project_keyval(place, near, w_keyval)
    kept = keyval_keep + send_core(keyval_away)

    near_before, near_after = send_outer(near, 1), send_outer(near, -1)
    near_before, near_after, wide, kept = lax.optimization_barrier(
        (near_before, near_after, wide, kept)
    )
    wide_after = send_outer(wide, -1)
    near_far = send_outer(near_before, 1)
    near_far, wide_again = lax.optimization_barrier((near_far, wide))
    wide_before = send_outer(wide_again, 1)
    wide_far = send_outer(wide_after, -1)

    kept = kept.reshape(RING, count // 8, 2 * HEAD)
    keyval = kept[0] + send_ahead(kept[1], 1) + send_ahead(kept[2], 2) + send_ahead(kept[3], 3)
    keyval = keyval.astype(BF16)

    pieces = [near, near_before, near_after, near_far, wide, wide_before, wide_after, wide_far]
    columns = w_query.shape[1]
    pieces, keyval = lax.optimization_barrier((pieces, keyval))
    away, keep = project_query(place, pieces, w_query, 1)
    summed = (keep + send_core(away)).reshape(2, 128, columns)
    far, behind = send_x(summed[0], 1), send_x(summed[1], -1)
    away, keep = project_query(place, pieces, w_query, 0)
    summed = (keep + send_core(away)).reshape(2, 128, columns)
    moves = [
        (g * 16 + j, (j // 2) * 16 + (j % 2) * 8 + g) for g in range(8) for j in range(16)
    ]
    keyval = lax.ppermute(keyval, ("gx", "yz"), moves)
    far, keyval = lax.optimization_barrier((far, keyval))
    ahead = send_x(summed[1] + far, 1)
    query = (summed[0] + ahead + behind).astype(BF16).reshape(16, 8, columns)
    query = lax.all_to_all(query, "yz", split_axis=0, concat_axis=0)

    heads_out, new_keyval = attend(
        lengths, query.reshape(128, columns), cosine, sine, keyval, key_cache, value_cache
    )
    heads_out = lax.all_to_all(
        heads_out.reshape(16, 8, columns), "yz", split_axis=0, concat_axis=0
    ).reshape(128, columns)
    before = send_x(heads_out, 1)
    after = send_x(heads_out, -1)
    pieces = [heads_out, before, after, send_x(before, 1)]
    pieces = pieces + [send_core(p) for p in pieces]
    two_low, two_high = project_output(place, pieces, w_out, (2,))
    one_low, one_high, three_low, three_high, own = project_output(
        place, pieces, w_out, (1, 3, 0)
    )

    far_low, far_high = send_outer(two_low, 1), send_outer(two_high, -1)
    far_low, far_high = lax.optimization_barrier((far_low, far_high))
    early_high, early_low = send_outer(one_high, 1), send_outer(three_low, -1)
    late_low = send_outer((one_low.astype(F32) + far_low.astype(F32)).astype(BF16), 1)
    late_high = send_outer((three_high.astype(F32) + far_high.astype(F32)).astype(BF16), -1)
    low = own[:128] + early_low.astype(F32) + late_low.astype(F32)
    high = own[128:] + early_high.astype(F32) + late_high.astype(F32)
    here, one, two, three = low[:64], low[64:], high[:64], high[64:]
    far_low, far_high = send_inner(two[:32], 1), send_inner(two[32:], -1)
    one = jnp.concatenate([one[:32] + far_low, one[32:]], 0)
    three = jnp.concatenate([three[:32], three[32:] + far_high], 0)
    branch = here + send_inner(one, 1) + send_inner(three, -1)
    mixed = (raw.astype(F32) + branch).astype(BF16).reshape(tokens.shape)
    return (mixed, new_keyval.reshape(seqs, 2, 2 * HEAD))


def solution(mesh):
    return jax.shard_map(
        body,
        mesh=mesh,
        in_specs=(
            P("yz", None, "gx"),
            P("gx"),
            P("gx", "yz"),
            P("gx", None),
            P("yz", "gx"),
            P(("gx", "yz"), None, None),
            P(("gx", "yz"), None, None),
            P(("gx", "yz")),
        ),
        out_specs=(P("yz", None, "gx"), P(("gx", "yz"), None, None)),
        check_vma=False,
    )
```

```python
import functools

import jax
import jax.numpy as jnp
from jax import lax
from jax.experimental import pallas as pl
from jax.experimental.pallas import tpu as pltpu
from jax.sharding import PartitionSpec as P

D = 18432
HEADS = 48
HEAD = 256
RING = 4
F32 = jnp.float32
BF16 = jnp.bfloat16


def shift(value, move):
    pairs = []
    for x in range(RING):
        for core in range(2):
            for y in range(RING):
                for z in range(RING):
                    dx, dy, dz = move(core)
                    target = (2 * ((x + dx) % RING) + core) * 16
                    target += RING * ((y + dy) % RING) + (z + dz) % RING
                    pairs.append(((2 * x + core) * 16 + RING * y + z, target))
    return lax.ppermute(value, ("gx", "yz"), pairs)


def send_core(value):
    pairs = [(2 * x + c, 2 * x + 1 - c) for x in range(RING) for c in range(2)]
    return lax.ppermute(value, "gx", pairs)


def send_x(value, step):
    return shift(value, lambda core: ((1 - 2 * core) * step, 0, 0))


def send_ahead(value, step):
    return shift(value, lambda core: (step, 0, 0))


def send_inner(value, step):
    return shift(value, lambda core: (0, core * step, (1 - core) * step))


def send_outer(value, step):
    return shift(value, lambda core: (0, (1 - core) * step, core * step))


def rotation_tables(positions):
    half = HEAD // 2
    freq = 10000.0 ** (-jnp.arange(half, dtype=F32) * 2.0 / HEAD)
    angle = positions.astype(F32)[..., None] * freq
    return jnp.cos(angle), jnp.sin(angle)


def sums_kernel(rows_ref, out_ref):
    rows = rows_ref[...].astype(F32)
    total = jnp.sum(rows, -1, keepdims=True)
    squares = jnp.sum(rows * rows, -1, keepdims=True)
    out_ref[...] = jnp.concatenate([total, squares], 1)


def row_sums(rows):
    vmem_spec = pl.BlockSpec(memory_space=pltpu.VMEM)
    return pl.pallas_call(
        sums_kernel,
        out_shape=jax.ShapeDtypeStruct((rows.shape[0], 2), F32),
        in_specs=[vmem_spec],
        out_specs=vmem_spec,
        compiler_params=pltpu.CompilerParams(vmem_limit_bytes=12 * 2**20),
        name="row_sums",
    )(rows)


def normalize_kernel(one_ref, two_ref, one_sums, two_sums, gain_ref, out_ref):
    count = one_ref.shape[0]
    for index, (rows_ref, sums_ref) in enumerate(((one_ref, one_sums), (two_ref, two_sums))):
        mean = sums_ref[:, 0:1] / D
        var = sums_ref[:, 1:2] / D - mean * mean
        rows = rows_ref[...].astype(F32)
        normed = (rows - mean) * lax.rsqrt(var + 1e-05) * gain_ref[...]
        out_ref[index * count : (index + 1) * count, :] = normed.astype(BF16)


def normalize(one, two, one_sums, two_sums, gain):
    vmem_spec = pl.BlockSpec(memory_space=pltpu.VMEM)
    return pl.pallas_call(
        normalize_kernel,
        out_shape=jax.ShapeDtypeStruct((2 * one.shape[0], one.shape[1]), BF16),
        in_specs=[vmem_spec] * 5,
        out_specs=vmem_spec,
        compiler_params=pltpu.CompilerParams(vmem_limit_bytes=12 * 2**20),
        name="normalize",
    )(one, two, one_sums, two_sums, gain)


def keyval_kernel(place, rows_ref, w_ref, away_ref, keep_ref, sums_ref):
    x, core = place[0], place[3]
    rows = rows_ref[: sums_ref.shape[0], :]
    sums_ref[...] = jnp.dot(rows, w_ref[...], preferred_element_type=F32)
    for slot in range(RING):
        block = 2 * lax.rem(x + slot, RING)
        target = pl.ds(8 * slot, 8)
        keep_ref[target, :] = sums_ref[pl.ds(pl.multiple_of(8 * (block + core), 8), 8), :]
        away_ref[target, :] = sums_ref[pl.ds(pl.multiple_of(8 * (block + 1 - core), 8), 8), :]


def project_keyval(place, rows, w_keyval):
    count, depth = rows.shape[0] // 2, rows.shape[1]
    columns = w_keyval.shape[1]
    vmem_spec = pl.BlockSpec(memory_space=pltpu.VMEM)
    half = jax.ShapeDtypeStruct((count // 2, columns), F32)
    return pl.pallas_call(
        keyval_kernel,
        out_shape=[half, half],
        in_specs=[pl.BlockSpec(memory_space=pltpu.SMEM)] + [vmem_spec] * 2,
        out_specs=[vmem_spec] * 2,
        scratch_shapes=[pltpu.VMEM((count, columns), F32)],
        compiler_params=pltpu.CompilerParams(vmem_limit_bytes=12 * 2**20),
        cost_estimate=pl.CostEstimate(
            flops=2 * count * depth * columns, bytes_accessed=3 * 2**20, transcendentals=0
        ),
        name="keyval_projection",
    )(place, rows, w_keyval)


def query_kernel(pair, place, *refs):
    pieces, (w_ref, away_ref, keep_ref, rows_ref) = refs[:8], refs[8:]
    x, y, z, core = place[0], place[1], place[2], place[3]
    for index, piece in enumerate(pieces):
        for part in range(2):
            outer = (0, 3, 1, 2)[index % 4]
            inner = ((0, 3), (1, 2))[index // 4][part]
            at_y = lax.rem(y + jnp.where(core == 0, outer, inner), RING)
            at_z = lax.rem(z + jnp.where(core == 0, inner, outer), RING)
            to_core = at_z // 2
            ahead = lax.rem(at_y - x + RING, RING)
            slot = jnp.where(to_core == 0, ahead, lax.rem(RING - ahead, RING))
            mine = jnp.where(to_core == core, 4, 0)
            position = mine + lax.rem(slot, 2) * 2 + lax.rem(at_z, 2)

            @pl.when(slot // 2 == pair)
            def _():
                rows_ref[position] = piece[part * 64 : (part + 1) * 64, :]

    rows = rows_ref[...].reshape(512, w_ref.shape[0])
    result = jnp.dot(rows, w_ref[...], preferred_element_type=F32)
    away_ref[...] = result[:256]
    keep_ref[...] = result[256:]


def project_query(place, pieces, w_query, pair):
    depth, columns = w_query.shape
    vmem_spec = pl.BlockSpec(memory_space=pltpu.VMEM)
    half = jax.ShapeDtypeStruct((256, columns), F32)
    return pl.pallas_call(
        functools.partial(query_kernel, pair),
        out_shape=[half, half],
        in_specs=[pl.BlockSpec(memory_space=pltpu.SMEM)] + [vmem_spec] * 9,
        out_specs=[vmem_spec] * 2,
        scratch_shapes=[pltpu.VMEM((8, 64, depth), BF16)],
        compiler_params=pltpu.CompilerParams(vmem_limit_bytes=20 * 2**20),
        cost_estimate=pl.CostEstimate(
            flops=2 * 512 * depth * columns, bytes_accessed=8 * 2**20, transcendentals=0
        ),
        name="query_projection",
    )(place, *pieces, w_query)


def attend_kernel(lengths, q_ref, cos_ref, sin_ref, kv_ref, k_ref, v_ref, out_ref, new_ref, acc_ref):
    seqs = k_ref.shape[0]
    half = HEAD // 2
    rows = q_ref.shape[0]
    scale = HEAD ** (-0.5)
    contract_last = (((1,), (1,)), ((), ()))
    pick_row = lax.broadcasted_iota(jnp.int32, (32, rows), 0)
    pick_col = lax.broadcasted_iota(jnp.int32, (32, rows), 1)
    odd = lax.rem(lax.broadcasted_iota(jnp.int32, (32, half), 0), 2) == 1
    second_step = lax.rem(lax.broadcasted_iota(jnp.int32, (96, 1), 0), 2) == 1
    first = kv_ref[:, :half].astype(F32)
    second = kv_ref[:, half:HEAD].astype(F32)
    cosine, sine = cos_ref[...], sin_ref[...]
    new_ref[:, :half] = (first * cosine - second * sine).astype(BF16)
    new_ref[:, half:HEAD] = (second * cosine + first * sine).astype(BF16)
    new_ref[:, HEAD:] = kv_ref[:, HEAD:]
    new_rows = new_ref[...].astype(F32)

    def pick_of(r):
        return (pick_col == (pick_row // 2) * 8 + 2 * r + lax.rem(pick_row, 2)).astype(BF16)

    def query_of(r):
        pick = pick_of(r)
        cosine = jnp.where(odd, cos_ref[2 * r + 1 : 2 * r + 2, :], cos_ref[2 * r : 2 * r + 1, :])
        sine = jnp.where(odd, sin_ref[2 * r + 1 : 2 * r + 2, :], sin_ref[2 * r : 2 * r + 1, :])
        parts = []
        for h in range(3):
            chosen = jnp.dot(pick, q_ref[:, h * HEAD : (h + 1) * HEAD], preferred_element_type=F32)
            first, second = chosen[:, :half], chosen[:, half:]
            parts.append(
                jnp.concatenate([first * cosine - second * sine, second * cosine + first * sine], 1)
            )
        return jnp.concatenate(parts, 0).astype(BF16)

    def scores_of(r, query):
        return lax.dot_general(query, k_ref[r], contract_last, preferred_element_type=F32) * scale

    query = query_of(0)
    scores = scores_of(0, query)
    for r in range(seqs):
        if r + 1 < seqs:
            next_query = query_of(r + 1)
            next_scores = scores_of(r + 1, next_query)
        valid = lax.broadcasted_iota(jnp.int32, scores.shape, 1) < lengths[r]
        cached = jnp.where(valid, scores, -jnp.inf)
        new = new_rows[2 * r : 2 * r + 2, :]
        wide = query.astype(F32)
        fresh0 = jnp.sum(wide * new[0:1, :HEAD], -1, keepdims=True) * scale
        fresh1 = jnp.sum(wide * new[1:2, :HEAD], -1, keepdims=True) * scale
        fresh1 = jnp.where(second_step, fresh1, -jnp.inf)
        top = jnp.maximum(jnp.max(cached, -1, keepdims=True), jnp.maximum(fresh0, fresh1))
        exp_cached = jnp.exp(cached - top)
        exp0 = jnp.exp(fresh0 - top)
        exp1 = jnp.exp(fresh1 - top)
        inverse = 1.0 / (jnp.sum(exp_cached, -1, keepdims=True) + exp0 + exp1)
        weights = (exp_cached * inverse).astype(BF16)
        weight0 = (exp0 * inverse).astype(BF16).astype(F32)
        weight1 = (exp1 * inverse).astype(BF16).astype(F32)
        result = jnp.dot(weights, v_ref[r], preferred_element_type=F32)
        result = result + weight0 * new[0:1, HEAD:] + weight1 * new[1:2, HEAD:]
        result = result.astype(BF16)
        pick = pick_of(r)
        for h in range(3):
            spread = lax.dot_general(
                pick,
                result[h * 32 : (h + 1) * 32],
                (((0,), (0,)), ((), ())),
                preferred_element_type=F32,
            )
            columns = slice(h * HEAD, (h + 1) * HEAD)
            if r == 0:
                acc_ref[:, columns] = spread
            else:
                acc_ref[:, columns] += spread
        if r + 1 < seqs:
            query, scores = next_query, next_scores
    out_ref[...] = acc_ref[...].astype(BF16)


def attend(lengths, query, cosine, sine, keyval, keys, values):
    seqs, context, _ = keys.shape
    rows, columns = query.shape
    vmem_spec = pl.BlockSpec(memory_space=pltpu.VMEM)
    return pl.pallas_call(
        attend_kernel,
        out_shape=[
            jax.ShapeDtypeStruct((rows, columns), BF16),
            jax.ShapeDtypeStruct(keyval.shape, BF16),
        ],
        in_specs=[pl.BlockSpec(memory_space=pltpu.SMEM)] + [vmem_spec] * 6,
        out_specs=[vmem_spec] * 2,
        scratch_shapes=[pltpu.VMEM((rows, columns), F32)],
        compiler_params=pltpu.CompilerParams(vmem_limit_bytes=20 * 2**20),
        cost_estimate=pl.CostEstimate(
            flops=4 * seqs * 96 * context * HEAD,
            bytes_accessed=4 * seqs * context * HEAD,
            transcendentals=seqs * 96 * context,
        ),
        name="attention",
    )(lengths, query, cosine, sine, keyval, keys, values)


def output_kernel(groups, place, *refs):
    pieces, (w_ref, *outs), rows_ref = refs[:8], refs[8:-1], refs[-1]
    x, y, z, core = place[0], place[1], place[2], place[3]
    for index, piece in enumerate(pieces):
        at_core = core if index < 4 else 1 - core
        slot = (0, 3, 1, 2)[index % 4]
        ahead = jnp.where(at_core == 0, slot, (RING - slot) % RING)
        dy = lax.rem(x + ahead - y + RING, RING)
        for part in range(2):
            dz = lax.rem(2 * at_core + part - z + RING, RING)
            outer, inner = jnp.where(core == 0, dy, dz), jnp.where(core == 0, dz, dy)
            for position, group in enumerate(groups):

                @pl.when(outer == group)
                def _():
                    rows_ref[position * RING + inner] = piece[part * 64 : (part + 1) * 64, :]

    outs = list(outs)
    for position, group in enumerate(groups):
        rows = rows_ref[RING * position : RING * position + RING].reshape(256, w_ref.shape[0])
        targets = [outs.pop(0)] if group == 0 else [outs.pop(0), outs.pop(0)]
        for start in range(0, w_ref.shape[1], 768):
            columns = slice(start, start + 768)
            result = jnp.dot(rows, w_ref[:, columns], preferred_element_type=F32)
            if group == 0:
                targets[0][:, columns] = result
            else:
                targets[0][:, columns] = result[:128].astype(targets[0].dtype)
                targets[1][:, columns] = result[128:].astype(targets[1].dtype)


def project_output(place, pieces, w_out, groups):
    depth, columns = w_out.shape
    vmem_spec = pl.BlockSpec(memory_space=pltpu.VMEM)
    shapes = []
    for group in groups:
        if group == 0:
            shapes.append(jax.ShapeDtypeStruct((256, columns), F32))
        else:
            for added in (group == 1, group == 3):
                shapes.append(jax.ShapeDtypeStruct((128, columns), F32 if added else BF16))
    return pl.pallas_call(
        functools.partial(output_kernel, groups),
        out_shape=shapes,
        in_specs=[pl.BlockSpec(memory_space=pltpu.SMEM)] + [vmem_spec] * 9,
        out_specs=[vmem_spec] * len(shapes),
        scratch_shapes=[pltpu.VMEM((RING * len(groups), 64, depth), BF16)],
        compiler_params=pltpu.CompilerParams(vmem_limit_bytes=20 * 2**20),
        cost_estimate=pl.CostEstimate(
            flops=2 * 256 * len(groups) * depth * columns,
            bytes_accessed=8 * 2**20,
            transcendentals=0,
        ),
        name="output_projection",
    )(place, *pieces, w_out)


def body(tokens, gain, w_query, w_keyval, w_out, key_cache, value_cache, lengths):
    seqs = lengths.shape[0]
    gx, yz = lax.axis_index("gx"), lax.axis_index("yz")
    place = jnp.stack([gx // 2, yz // RING, lax.rem(yz, RING), lax.rem(gx, 2)]).astype(jnp.int32)
    positions = jnp.repeat(lengths, 2) + lax.rem(jnp.arange(2 * seqs, dtype=jnp.int32), 2)
    cosine, sine = rotation_tables(positions)

    count = tokens.shape[0] * 2
    features = tokens.shape[2]
    raw = lax.optimization_barrier(tokens.reshape(count, features))
    sums = row_sums(raw)
    sums = sums + send_core(sums)
    sums, cosine, sine, place, raw = lax.optimization_barrier((sums, cosine, sine, place, raw))
    before, after = send_inner(raw, 1), send_inner(raw, -1)
    sums = sums + send_x(sums, 1) + send_x(sums, 2) + send_x(sums, 3)
    sums, before, after = lax.optimization_barrier((sums, before, after))
    before_sums, after_sums = send_inner(sums, 1), send_inner(sums, -1)
    before, before_sums = lax.optimization_barrier((before, before_sums))
    far, far_sums = send_inner(before, 1), send_inner(sums, 2)
    scale = gain.reshape(1, features)
    near = normalize(raw, before, sums, before_sums, scale)
    wide = normalize(after, far, after_sums, far_sums, scale)

    keyval_away, keyval_keep = project_keyval(place, near, w_keyval)
    kept = keyval_keep + send_core(keyval_away)

    near_before, near_after = send_outer(near, 1), send_outer(near, -1)
    near_before, near_after, wide, kept = lax.optimization_barrier(
        (near_before, near_after, wide, kept)
    )
    wide_after = send_outer(wide, -1)
    near_far = send_outer(near_before, 1)
    near_far, wide_again = lax.optimization_barrier((near_far, wide))
    wide_before = send_outer(wide_again, 1)
    wide_far = send_outer(wide_after, -1)

    kept = kept.reshape(RING, count // 8, 2 * HEAD)
    keyval = kept[0] + send_ahead(kept[1], 1) + send_ahead(kept[2], 2) + send_ahead(kept[3], 3)
    keyval = keyval.astype(BF16)

    pieces = [near, near_before, near_after, near_far, wide, wide_before, wide_after, wide_far]
    columns = w_query.shape[1]
    pieces, keyval = lax.optimization_barrier((pieces, keyval))
    away, keep = project_query(place, pieces, w_query, 1)
    summed = (keep + send_core(away)).reshape(2, 128, columns)
    far, behind = send_x(summed[0], 1), send_x(summed[1], -1)
    away, keep = project_query(place, pieces, w_query, 0)
    summed = (keep + send_core(away)).reshape(2, 128, columns)
    moves = [
        (g * 16 + j, (j // 2) * 16 + (j % 2) * 8 + g) for g in range(8) for j in range(16)
    ]
    keyval = lax.ppermute(keyval, ("gx", "yz"), moves)
    far, keyval = lax.optimization_barrier((far, keyval))
    ahead = send_x(summed[1] + far, 1)
    query = (summed[0] + ahead + behind).astype(BF16).reshape(16, 8, columns)
    query = lax.all_to_all(query, "yz", split_axis=0, concat_axis=0)

    heads_out, new_keyval = attend(
        lengths, query.reshape(128, columns), cosine, sine, keyval, key_cache, value_cache
    )
    heads_out = lax.all_to_all(
        heads_out.reshape(16, 8, columns), "yz", split_axis=0, concat_axis=0
    ).reshape(128, columns)
    before = send_x(heads_out, 1)
    after = send_x(heads_out, -1)
    pieces = [heads_out, before, after, send_x(before, 1)]
    pieces = pieces + [send_core(p) for p in pieces]
    two_low, two_high = project_output(place, pieces, w_out, (2,))
    one_low, one_high, three_low, three_high, own = project_output(
        place, pieces, w_out, (1, 3, 0)
    )

    far_low, far_high = send_outer(two_low, 1), send_outer(two_high, -1)
    far_low, far_high = lax.optimization_barrier((far_low, far_high))
    early_high, early_low = send_outer(one_high, 1), send_outer(three_low, -1)
    late_low = send_outer((one_low + far_low.astype(F32)).astype(BF16), 1)
    late_high = send_outer((three_high + far_high.astype(F32)).astype(BF16), -1)
    low = own[:128] + early_low.astype(F32) + late_low.astype(F32)
    high = own[128:] + early_high.astype(F32) + late_high.astype(F32)
    halves = []
    for columns in (slice(0, features // 2), slice(features // 2, features)):
        here, one = low[:64, columns], low[64:, columns]
        two, three = high[:64, columns], high[64:, columns]
        far_low, far_high = send_inner(two[:32], 1), send_inner(two[32:], -1)
        one = jnp.concatenate([one[:32] + far_low, one[32:]], 0)
        three = jnp.concatenate([three[:32], three[32:] + far_high], 0)
        halves.append(here + send_inner(one, 1) + send_inner(three, -1))
    branch = jnp.concatenate(halves, 1)
    mixed = (raw.astype(F32) + branch).astype(BF16).reshape(tokens.shape)
    return (mixed, new_keyval.reshape(seqs, 2, 2 * HEAD))


def solution(mesh):
    return jax.shard_map(
        body,
        mesh=mesh,
        in_specs=(
            P("yz", None, "gx"),
            P("gx"),
            P("gx", "yz"),
            P("gx", None),
            P("yz", "gx"),
            P(("gx", "yz"), None, None),
            P(("gx", "yz"), None, None),
            P(("gx", "yz")),
        ),
        out_specs=(P("yz", None, "gx"), P(("gx", "yz"), None, None)),
        check_vma=False,
    )
```

```python
import functools

import jax
import jax.numpy as jnp
from jax import lax
from jax.experimental import pallas as pl
from jax.experimental.pallas import tpu as pltpu
from jax.sharding import PartitionSpec as P

D = 18432
HEADS = 48
HEAD = 256
RING = 4
F32 = jnp.float32
BF16 = jnp.bfloat16


def shift(value, move):
    pairs = []
    for x in range(RING):
        for core in range(2):
            for y in range(RING):
                for z in range(RING):
                    dx, dy, dz = move(core)
                    target = (2 * ((x + dx) % RING) + core) * 16
                    target += RING * ((y + dy) % RING) + (z + dz) % RING
                    pairs.append(((2 * x + core) * 16 + RING * y + z, target))
    return lax.ppermute(value, ("gx", "yz"), pairs)


def send_core(value):
    pairs = [(2 * x + c, 2 * x + 1 - c) for x in range(RING) for c in range(2)]
    return lax.ppermute(value, "gx", pairs)


def send_x(value, step):
    return shift(value, lambda core: ((1 - 2 * core) * step, 0, 0))


def send_ahead(value, step):
    return shift(value, lambda core: (step, 0, 0))


def send_inner(value, step):
    return shift(value, lambda core: (0, core * step, (1 - core) * step))


def send_outer(value, step):
    return shift(value, lambda core: (0, (1 - core) * step, core * step))


def rotation_tables(positions):
    half = HEAD // 2
    freq = 10000.0 ** (-jnp.arange(half, dtype=F32) * 2.0 / HEAD)
    angle = positions.astype(F32)[..., None] * freq
    return jnp.cos(angle), jnp.sin(angle)


def sums_kernel(rows_ref, out_ref):
    rows = rows_ref[...].astype(F32)
    total = jnp.sum(rows, -1, keepdims=True)
    squares = jnp.sum(rows * rows, -1, keepdims=True)
    out_ref[...] = jnp.concatenate([total, squares], 1)


def row_sums(rows):
    vmem_spec = pl.BlockSpec(memory_space=pltpu.VMEM)
    return pl.pallas_call(
        sums_kernel,
        out_shape=jax.ShapeDtypeStruct((rows.shape[0], 2), F32),
        in_specs=[vmem_spec],
        out_specs=vmem_spec,
        compiler_params=pltpu.CompilerParams(vmem_limit_bytes=12 * 2**20),
        name="row_sums",
    )(rows)


def normalize_kernel(one_ref, two_ref, one_sums, two_sums, gain_ref, out_ref):
    count = one_ref.shape[0]
    for index, (rows_ref, sums_ref) in enumerate(((one_ref, one_sums), (two_ref, two_sums))):
        mean = sums_ref[:, 0:1] / D
        var = sums_ref[:, 1:2] / D - mean * mean
        rows = rows_ref[...].astype(F32)
        normed = (rows - mean) * lax.rsqrt(var + 1e-05) * gain_ref[...]
        out_ref[index * count : (index + 1) * count, :] = normed.astype(BF16)


def normalize(one, two, one_sums, two_sums, gain):
    vmem_spec = pl.BlockSpec(memory_space=pltpu.VMEM)
    return pl.pallas_call(
        normalize_kernel,
        out_shape=jax.ShapeDtypeStruct((2 * one.shape[0], one.shape[1]), BF16),
        in_specs=[vmem_spec] * 5,
        out_specs=vmem_spec,
        compiler_params=pltpu.CompilerParams(vmem_limit_bytes=12 * 2**20),
        name="normalize",
    )(one, two, one_sums, two_sums, gain)


def keyval_kernel(place, rows_ref, w_ref, away_ref, keep_ref, sums_ref):
    x, core = place[0], place[3]
    rows = rows_ref[: sums_ref.shape[0], :]
    sums_ref[...] = jnp.dot(rows, w_ref[...], preferred_element_type=F32)
    for slot in range(RING):
        block = 2 * lax.rem(x + slot, RING)
        target = pl.ds(8 * slot, 8)
        keep_ref[target, :] = sums_ref[pl.ds(pl.multiple_of(8 * (block + core), 8), 8), :]
        away_ref[target, :] = sums_ref[pl.ds(pl.multiple_of(8 * (block + 1 - core), 8), 8), :]


def project_keyval(place, rows, w_keyval):
    count, depth = rows.shape[0] // 2, rows.shape[1]
    columns = w_keyval.shape[1]
    vmem_spec = pl.BlockSpec(memory_space=pltpu.VMEM)
    half = jax.ShapeDtypeStruct((count // 2, columns), F32)
    return pl.pallas_call(
        keyval_kernel,
        out_shape=[half, half],
        in_specs=[pl.BlockSpec(memory_space=pltpu.SMEM)] + [vmem_spec] * 2,
        out_specs=[vmem_spec] * 2,
        scratch_shapes=[pltpu.VMEM((count, columns), F32)],
        compiler_params=pltpu.CompilerParams(vmem_limit_bytes=12 * 2**20),
        cost_estimate=pl.CostEstimate(
            flops=2 * count * depth * columns, bytes_accessed=3 * 2**20, transcendentals=0
        ),
        name="keyval_projection",
    )(place, rows, w_keyval)


def query_kernel(pair, place, *refs):
    pieces, (w_ref, away_ref, keep_ref, rows_ref) = refs[:8], refs[8:]
    x, y, z, core = place[0], place[1], place[2], place[3]
    for index, piece in enumerate(pieces):
        for part in range(2):
            outer = (0, 3, 1, 2)[index % 4]
            inner = ((0, 3), (1, 2))[index // 4][part]
            at_y = lax.rem(y + jnp.where(core == 0, outer, inner), RING)
            at_z = lax.rem(z + jnp.where(core == 0, inner, outer), RING)
            to_core = at_z // 2
            ahead = lax.rem(at_y - x + RING, RING)
            slot = jnp.where(to_core == 0, ahead, lax.rem(RING - ahead, RING))
            mine = jnp.where(to_core == core, 4, 0)
            position = mine + lax.rem(slot, 2) * 2 + lax.rem(at_z, 2)

            @pl.when(slot // 2 == pair)
            def _():
                rows_ref[position] = piece[part * 64 : (part + 1) * 64, :]

    rows = rows_ref[...].reshape(512, w_ref.shape[0])
    result = jnp.dot(rows, w_ref[...], preferred_element_type=F32)
    away_ref[...] = result[:256]
    keep_ref[...] = result[256:]


def project_query(place, pieces, w_query, pair):
    depth, columns = w_query.shape
    vmem_spec = pl.BlockSpec(memory_space=pltpu.VMEM)
    half = jax.ShapeDtypeStruct((256, columns), F32)
    return pl.pallas_call(
        functools.partial(query_kernel, pair),
        out_shape=[half, half],
        in_specs=[pl.BlockSpec(memory_space=pltpu.SMEM)] + [vmem_spec] * 9,
        out_specs=[vmem_spec] * 2,
        scratch_shapes=[pltpu.VMEM((8, 64, depth), BF16)],
        compiler_params=pltpu.CompilerParams(vmem_limit_bytes=20 * 2**20),
        cost_estimate=pl.CostEstimate(
            flops=2 * 512 * depth * columns, bytes_accessed=8 * 2**20, transcendentals=0
        ),
        name="query_projection",
    )(place, *pieces, w_query)


def attend_kernel(lengths, q_ref, cos_ref, sin_ref, kv_ref, k_ref, v_ref, out_ref, new_ref, acc_ref):
    seqs = k_ref.shape[0]
    half = HEAD // 2
    rows = q_ref.shape[0]
    scale = HEAD ** (-0.5)
    contract_last = (((1,), (1,)), ((), ()))
    pick_row = lax.broadcasted_iota(jnp.int32, (32, rows), 0)
    pick_col = lax.broadcasted_iota(jnp.int32, (32, rows), 1)
    odd = lax.rem(lax.broadcasted_iota(jnp.int32, (32, half), 0), 2) == 1
    second_step = lax.rem(lax.broadcasted_iota(jnp.int32, (96, 1), 0), 2) == 1
    first = kv_ref[:, :half].astype(F32)
    second = kv_ref[:, half:HEAD].astype(F32)
    cosine, sine = cos_ref[...], sin_ref[...]
    new_ref[:, :half] = (first * cosine - second * sine).astype(BF16)
    new_ref[:, half:HEAD] = (second * cosine + first * sine).astype(BF16)
    new_ref[:, HEAD:] = kv_ref[:, HEAD:]
    new_rows = new_ref[...].astype(F32)

    def pick_of(r):
        return (pick_col == (pick_row // 2) * 8 + 2 * r + lax.rem(pick_row, 2)).astype(BF16)

    def query_of(r):
        pick = pick_of(r)
        cosine = jnp.where(odd, cos_ref[2 * r + 1 : 2 * r + 2, :], cos_ref[2 * r : 2 * r + 1, :])
        sine = jnp.where(odd, sin_ref[2 * r + 1 : 2 * r + 2, :], sin_ref[2 * r : 2 * r + 1, :])
        parts = []
        for h in range(3):
            chosen = jnp.dot(pick, q_ref[:, h * HEAD : (h + 1) * HEAD], preferred_element_type=F32)
            first, second = chosen[:, :half], chosen[:, half:]
            parts.append(
                jnp.concatenate([first * cosine - second * sine, second * cosine + first * sine], 1)
            )
        return jnp.concatenate(parts, 0).astype(BF16)

    def scores_of(r, query):
        return lax.dot_general(query, k_ref[r], contract_last, preferred_element_type=F32) * scale

    query = query_of(0)
    scores = scores_of(0, query)
    for r in range(seqs):
        if r + 1 < seqs:
            next_query = query_of(r + 1)
            next_scores = scores_of(r + 1, next_query)
        valid = lax.broadcasted_iota(jnp.int32, scores.shape, 1) < lengths[r]
        cached = jnp.where(valid, scores, -jnp.inf)
        new = new_rows[2 * r : 2 * r + 2, :]
        wide = query.astype(F32)
        fresh0 = jnp.sum(wide * new[0:1, :HEAD], -1, keepdims=True) * scale
        fresh1 = jnp.sum(wide * new[1:2, :HEAD], -1, keepdims=True) * scale
        fresh1 = jnp.where(second_step, fresh1, -jnp.inf)
        top = jnp.maximum(jnp.max(cached, -1, keepdims=True), jnp.maximum(fresh0, fresh1))
        exp_cached = jnp.exp(cached - top)
        exp0 = jnp.exp(fresh0 - top)
        exp1 = jnp.exp(fresh1 - top)
        inverse = 1.0 / (jnp.sum(exp_cached, -1, keepdims=True) + exp0 + exp1)
        weights = (exp_cached * inverse).astype(BF16)
        weight0 = (exp0 * inverse).astype(BF16).astype(F32)
        weight1 = (exp1 * inverse).astype(BF16).astype(F32)
        result = jnp.dot(weights, v_ref[r], preferred_element_type=F32)
        result = result + weight0 * new[0:1, HEAD:] + weight1 * new[1:2, HEAD:]
        result = result.astype(BF16)
        pick = pick_of(r)
        for h in range(3):
            spread = lax.dot_general(
                pick,
                result[h * 32 : (h + 1) * 32],
                (((0,), (0,)), ((), ())),
                preferred_element_type=F32,
            )
            columns = slice(h * HEAD, (h + 1) * HEAD)
            if r == 0:
                acc_ref[:, columns] = spread
            else:
                acc_ref[:, columns] += spread
        if r + 1 < seqs:
            query, scores = next_query, next_scores
    out_ref[...] = acc_ref[...].astype(BF16)


def attend(lengths, query, cosine, sine, keyval, keys, values):
    seqs, context, _ = keys.shape
    rows, columns = query.shape
    vmem_spec = pl.BlockSpec(memory_space=pltpu.VMEM)
    return pl.pallas_call(
        attend_kernel,
        out_shape=[
            jax.ShapeDtypeStruct((rows, columns), BF16),
            jax.ShapeDtypeStruct(keyval.shape, BF16),
        ],
        in_specs=[pl.BlockSpec(memory_space=pltpu.SMEM)] + [vmem_spec] * 6,
        out_specs=[vmem_spec] * 2,
        scratch_shapes=[pltpu.VMEM((rows, columns), F32)],
        compiler_params=pltpu.CompilerParams(vmem_limit_bytes=20 * 2**20),
        cost_estimate=pl.CostEstimate(
            flops=4 * seqs * 96 * context * HEAD,
            bytes_accessed=4 * seqs * context * HEAD,
            transcendentals=seqs * 96 * context,
        ),
        name="attention",
    )(lengths, query, cosine, sine, keyval, keys, values)


def output_kernel(groups, place, *refs):
    pieces, (w_ref, *outs), rows_ref = refs[:8], refs[8:-1], refs[-1]
    x, y, z, core = place[0], place[1], place[2], place[3]
    for index, piece in enumerate(pieces):
        at_core = core if index < 4 else 1 - core
        slot = (0, 3, 1, 2)[index % 4]
        ahead = jnp.where(at_core == 0, slot, (RING - slot) % RING)
        dy = lax.rem(x + ahead - y + RING, RING)
        for part in range(2):
            dz = lax.rem(2 * at_core + part - z + RING, RING)
            outer, inner = jnp.where(core == 0, dy, dz), jnp.where(core == 0, dz, dy)
            for position, group in enumerate(groups):

                @pl.when(outer == group)
                def _():
                    rows_ref[position * RING + inner] = piece[part * 64 : (part + 1) * 64, :]

    outs = list(outs)
    for position, group in enumerate(groups):
        rows = rows_ref[RING * position : RING * position + RING].reshape(256, w_ref.shape[0])
        targets = [outs.pop(0)] if group == 0 else [outs.pop(0), outs.pop(0)]
        for start in range(0, w_ref.shape[1], 768):
            columns = slice(start, start + 768)
            result = jnp.dot(rows, w_ref[:, columns], preferred_element_type=F32)
            if group == 0:
                targets[0][:, columns] = result
            else:
                targets[0][:, columns] = result[:128].astype(targets[0].dtype)
                targets[1][:, columns] = result[128:].astype(targets[1].dtype)


def project_output(place, pieces, w_out, groups):
    depth, columns = w_out.shape
    vmem_spec = pl.BlockSpec(memory_space=pltpu.VMEM)
    shapes = []
    for group in groups:
        if group == 0:
            shapes.append(jax.ShapeDtypeStruct((256, columns), F32))
        else:
            for added in (group == 1, group == 3):
                shapes.append(jax.ShapeDtypeStruct((128, columns), F32 if added else BF16))
    return pl.pallas_call(
        functools.partial(output_kernel, groups),
        out_shape=shapes,
        in_specs=[pl.BlockSpec(memory_space=pltpu.SMEM)] + [vmem_spec] * 9,
        out_specs=[vmem_spec] * len(shapes),
        scratch_shapes=[pltpu.VMEM((RING * len(groups), 64, depth), BF16)],
        compiler_params=pltpu.CompilerParams(vmem_limit_bytes=20 * 2**20),
        cost_estimate=pl.CostEstimate(
            flops=2 * 256 * len(groups) * depth * columns,
            bytes_accessed=8 * 2**20,
            transcendentals=0,
        ),
        name="output_projection",
    )(place, *pieces, w_out)


def body(tokens, gain, w_query, w_keyval, w_out, key_cache, value_cache, lengths):
    seqs = lengths.shape[0]
    gx, yz = lax.axis_index("gx"), lax.axis_index("yz")
    place = jnp.stack([gx // 2, yz // RING, lax.rem(yz, RING), lax.rem(gx, 2)]).astype(jnp.int32)
    positions = jnp.repeat(lengths, 2) + lax.rem(jnp.arange(2 * seqs, dtype=jnp.int32), 2)
    cosine, sine = rotation_tables(positions)

    count = tokens.shape[0] * 2
    features = tokens.shape[2]
    raw = lax.optimization_barrier(tokens.reshape(count, features))
    sums = row_sums(raw)
    sums = sums + send_core(sums)
    sums, cosine, sine, place, raw = lax.optimization_barrier((sums, cosine, sine, place, raw))
    before, after = send_inner(raw, 1), send_inner(raw, -1)
    sums = sums + send_x(sums, 1) + send_x(sums, 2) + send_x(sums, 3)
    sums, before, after = lax.optimization_barrier((sums, before, after))
    before_sums, after_sums = send_inner(sums, 1), send_inner(sums, -1)
    before, before_sums = lax.optimization_barrier((before, before_sums))
    far, far_sums = send_inner(before, 1), send_inner(sums, 2)
    scale = gain.reshape(1, features)
    near = normalize(raw, before, sums, before_sums, scale)
    wide = normalize(after, far, after_sums, far_sums, scale)

    keyval_away, keyval_keep = project_keyval(place, near, w_keyval)
    kept = keyval_keep + send_core(keyval_away)

    near_before, near_after = send_outer(near, 1), send_outer(near, -1)
    near_before, near_after, wide, kept = lax.optimization_barrier(
        (near_before, near_after, wide, kept)
    )
    kept = kept.reshape(RING, count // 8, 2 * HEAD)
    keyval = kept[0] + send_ahead(kept[1], 1) + send_ahead(kept[2], 2) + send_ahead(kept[3], 3)
    keyval = keyval.astype(BF16)

    wide_after = send_outer(wide, -1)
    near_far = send_outer(near_before, 1)
    near_far, wide_again, keyval = lax.optimization_barrier((near_far, wide, keyval))
    wide_before = send_outer(wide_again, 1)
    wide_far = send_outer(wide_after, -1)

    moves = [
        (g * 16 + j, (j // 2) * 16 + (j % 2) * 8 + g) for g in range(8) for j in range(16)
    ]
    keyval = lax.ppermute(keyval, ("gx", "yz"), moves)

    pieces = [near, near_before, near_after, near_far, wide, wide_before, wide_after, wide_far]
    columns = w_query.shape[1]
    pieces, keyval = lax.optimization_barrier((pieces, keyval))
    away, keep = project_query(place, pieces, w_query, 1)
    summed = (keep + send_core(away)).reshape(2, 128, columns)
    far, behind = send_x(summed[0], 1), send_x(summed[1], -1)
    away, keep = project_query(place, pieces, w_query, 0)
    summed = (keep + send_core(away)).reshape(2, 128, columns)
    ahead = send_x(summed[1] + far, 1)
    query = (summed[0] + ahead + behind).astype(BF16).reshape(16, 8, columns)
    query = lax.all_to_all(query, "yz", split_axis=0, concat_axis=0)

    heads_out, new_keyval = attend(
        lengths, query.reshape(128, columns), cosine, sine, keyval, key_cache, value_cache
    )
    heads_out = lax.all_to_all(
        heads_out.reshape(16, 8, columns), "yz", split_axis=0, concat_axis=0
    ).reshape(128, columns)
    before = send_x(heads_out, 1)
    after = send_x(heads_out, -1)
    pieces = [heads_out, before, after, send_x(before, 1)]
    pieces = pieces + [send_core(p) for p in pieces]
    two_low, two_high = project_output(place, pieces, w_out, (2,))
    one_low, one_high, three_low, three_high, own = project_output(
        place, pieces, w_out, (1, 3, 0)
    )

    far_low, far_high = send_outer(two_low, 1), send_outer(two_high, -1)
    far_low, far_high = lax.optimization_barrier((far_low, far_high))
    early_high, early_low = send_outer(one_high, 1), send_outer(three_low, -1)
    late_low = send_outer((one_low + far_low.astype(F32)).astype(BF16), 1)
    late_high = send_outer((three_high + far_high.astype(F32)).astype(BF16), -1)
    low = own[:128] + early_low.astype(F32) + late_low.astype(F32)
    high = own[128:] + early_high.astype(F32) + late_high.astype(F32)
    here, one, two, three = low[:64], low[64:], high[:64], high[64:]
    two = two.astype(BF16)
    far_low, far_high = send_inner(two[:32], 1), send_inner(two[32:], -1)
    one = jnp.concatenate([one[:32] + far_low.astype(F32), one[32:]], 0)
    three = jnp.concatenate([three[:32], three[32:] + far_high.astype(F32)], 0)
    branch = here + send_inner(one, 1) + send_inner(three, -1)
    mixed = (raw.astype(F32) + branch).astype(BF16).reshape(tokens.shape)
    return (mixed, new_keyval.reshape(seqs, 2, 2 * HEAD))


def solution(mesh):
    return jax.shard_map(
        body,
        mesh=mesh,
        in_specs=(
            P("yz", None, "gx"),
            P("gx"),
            P("gx", "yz"),
            P("gx", None),
            P("yz", "gx"),
            P(("gx", "yz"), None, None),
            P(("gx", "yz"), None, None),
            P(("gx", "yz")),
        ),
        out_specs=(P("yz", None, "gx"), P(("gx", "yz"), None, None)),
        check_vma=False,
    )
```

```python
import functools

import jax
import jax.numpy as jnp
from jax import lax
from jax.experimental import pallas as pl
from jax.experimental.pallas import tpu as pltpu
from jax.sharding import PartitionSpec as P

D = 18432
HEADS = 48
HEAD = 256
RING = 4
F32 = jnp.float32
BF16 = jnp.bfloat16


def shift(value, move):
    pairs = []
    for x in range(RING):
        for core in range(2):
            for y in range(RING):
                for z in range(RING):
                    dx, dy, dz = move(core)
                    target = (2 * ((x + dx) % RING) + core) * 16
                    target += RING * ((y + dy) % RING) + (z + dz) % RING
                    pairs.append(((2 * x + core) * 16 + RING * y + z, target))
    return lax.ppermute(value, ("gx", "yz"), pairs)


def send_core(value):
    pairs = [(2 * x + c, 2 * x + 1 - c) for x in range(RING) for c in range(2)]
    return lax.ppermute(value, "gx", pairs)


def send_x(value, step):
    return shift(value, lambda core: ((1 - 2 * core) * step, 0, 0))


def send_ahead(value, step):
    return shift(value, lambda core: (step, 0, 0))


def send_inner(value, step):
    return shift(value, lambda core: (0, core * step, (1 - core) * step))


def send_outer(value, step):
    return shift(value, lambda core: (0, (1 - core) * step, core * step))


def rotation_tables(positions):
    half = HEAD // 2
    freq = 10000.0 ** (-jnp.arange(half, dtype=F32) * 2.0 / HEAD)
    angle = positions.astype(F32)[..., None] * freq
    return jnp.cos(angle), jnp.sin(angle)


def sums_kernel(rows_ref, out_ref):
    rows = rows_ref[...].astype(F32)
    total = jnp.sum(rows, -1, keepdims=True)
    squares = jnp.sum(rows * rows, -1, keepdims=True)
    out_ref[...] = jnp.concatenate([total, squares], 1)


def row_sums(rows):
    vmem_spec = pl.BlockSpec(memory_space=pltpu.VMEM)
    return pl.pallas_call(
        sums_kernel,
        out_shape=jax.ShapeDtypeStruct((rows.shape[0], 2), F32),
        in_specs=[vmem_spec],
        out_specs=vmem_spec,
        compiler_params=pltpu.CompilerParams(vmem_limit_bytes=12 * 2**20),
        name="row_sums",
    )(rows)


def normalize_kernel(one_ref, two_ref, one_sums, two_sums, gain_ref, out_ref):
    count = one_ref.shape[0]
    for index, (rows_ref, sums_ref) in enumerate(((one_ref, one_sums), (two_ref, two_sums))):
        mean = sums_ref[:, 0:1] / D
        var = sums_ref[:, 1:2] / D - mean * mean
        rows = rows_ref[...].astype(F32)
        normed = (rows - mean) * lax.rsqrt(var + 1e-05) * gain_ref[...]
        out_ref[index * count : (index + 1) * count, :] = normed.astype(BF16)


def normalize(one, two, one_sums, two_sums, gain):
    vmem_spec = pl.BlockSpec(memory_space=pltpu.VMEM)
    return pl.pallas_call(
        normalize_kernel,
        out_shape=jax.ShapeDtypeStruct((2 * one.shape[0], one.shape[1]), BF16),
        in_specs=[vmem_spec] * 5,
        out_specs=vmem_spec,
        compiler_params=pltpu.CompilerParams(vmem_limit_bytes=12 * 2**20),
        name="normalize",
    )(one, two, one_sums, two_sums, gain)


def keyval_kernel(place, rows_ref, w_ref, away_ref, keep_ref, sums_ref):
    x, core = place[0], place[3]
    rows = rows_ref[: sums_ref.shape[0], :]
    sums_ref[...] = jnp.dot(rows, w_ref[...], preferred_element_type=F32)
    for slot in range(RING):
        block = 2 * lax.rem(x + slot, RING)
        target = pl.ds(8 * slot, 8)
        keep_ref[target, :] = sums_ref[pl.ds(pl.multiple_of(8 * (block + core), 8), 8), :]
        away_ref[target, :] = sums_ref[pl.ds(pl.multiple_of(8 * (block + 1 - core), 8), 8), :]


def project_keyval(place, rows, w_keyval):
    count, depth = rows.shape[0] // 2, rows.shape[1]
    columns = w_keyval.shape[1]
    vmem_spec = pl.BlockSpec(memory_space=pltpu.VMEM)
    half = jax.ShapeDtypeStruct((count // 2, columns), F32)
    return pl.pallas_call(
        keyval_kernel,
        out_shape=[half, half],
        in_specs=[pl.BlockSpec(memory_space=pltpu.SMEM)] + [vmem_spec] * 2,
        out_specs=[vmem_spec] * 2,
        scratch_shapes=[pltpu.VMEM((count, columns), F32)],
        compiler_params=pltpu.CompilerParams(vmem_limit_bytes=12 * 2**20),
        cost_estimate=pl.CostEstimate(
            flops=2 * count * depth * columns, bytes_accessed=3 * 2**20, transcendentals=0
        ),
        name="keyval_projection",
    )(place, rows, w_keyval)


def query_kernel(pair, place, *refs):
    pieces, (w_ref, away_ref, keep_ref, rows_ref) = refs[:8], refs[8:]
    x, y, z, core = place[0], place[1], place[2], place[3]
    for index, piece in enumerate(pieces):
        for part in range(2):
            outer = (0, 3, 1, 2)[index % 4]
            inner = ((0, 3), (1, 2))[index // 4][part]
            at_y = lax.rem(y + jnp.where(core == 0, outer, inner), RING)
            at_z = lax.rem(z + jnp.where(core == 0, inner, outer), RING)
            to_core = at_z // 2
            ahead = lax.rem(at_y - x + RING, RING)
            slot = jnp.where(to_core == 0, ahead, lax.rem(RING - ahead, RING))
            mine = jnp.where(to_core == core, 4, 0)
            position = mine + lax.rem(slot, 2) * 2 + lax.rem(at_z, 2)

            @pl.when(slot // 2 == pair)
            def _():
                rows_ref[position] = piece[part * 64 : (part + 1) * 64, :]

    rows = rows_ref[...].reshape(512, w_ref.shape[0])
    result = jnp.dot(rows, w_ref[...], preferred_element_type=F32)
    away_ref[...] = result[:256]
    keep_ref[...] = result[256:]


def project_query(place, pieces, w_query, pair):
    depth, columns = w_query.shape
    vmem_spec = pl.BlockSpec(memory_space=pltpu.VMEM)
    half = jax.ShapeDtypeStruct((256, columns), F32)
    return pl.pallas_call(
        functools.partial(query_kernel, pair),
        out_shape=[half, half],
        in_specs=[pl.BlockSpec(memory_space=pltpu.SMEM)] + [vmem_spec] * 9,
        out_specs=[vmem_spec] * 2,
        scratch_shapes=[pltpu.VMEM((8, 64, depth), BF16)],
        compiler_params=pltpu.CompilerParams(vmem_limit_bytes=20 * 2**20),
        cost_estimate=pl.CostEstimate(
            flops=2 * 512 * depth * columns, bytes_accessed=8 * 2**20, transcendentals=0
        ),
        name="query_projection",
    )(place, *pieces, w_query)


def attend_kernel(lengths, q_ref, cos_ref, sin_ref, kv_ref, k_ref, v_ref, out_ref, new_ref, acc_ref):
    seqs = k_ref.shape[0]
    half = HEAD // 2
    rows = q_ref.shape[0]
    scale = HEAD ** (-0.5)
    contract_last = (((1,), (1,)), ((), ()))
    pick_row = lax.broadcasted_iota(jnp.int32, (32, rows), 0)
    pick_col = lax.broadcasted_iota(jnp.int32, (32, rows), 1)
    odd = lax.rem(lax.broadcasted_iota(jnp.int32, (32, half), 0), 2) == 1
    second_step = lax.rem(lax.broadcasted_iota(jnp.int32, (96, 1), 0), 2) == 1
    first = kv_ref[:, :half].astype(F32)
    second = kv_ref[:, half:HEAD].astype(F32)
    cosine, sine = cos_ref[...], sin_ref[...]
    new_ref[:, :half] = (first * cosine - second * sine).astype(BF16)
    new_ref[:, half:HEAD] = (second * cosine + first * sine).astype(BF16)
    new_ref[:, HEAD:] = kv_ref[:, HEAD:]
    new_rows = new_ref[...].astype(F32)

    def pick_of(r):
        return (pick_col == (pick_row // 2) * 8 + 2 * r + lax.rem(pick_row, 2)).astype(BF16)

    def query_of(r):
        pick = pick_of(r)
        cosine = jnp.where(odd, cos_ref[2 * r + 1 : 2 * r + 2, :], cos_ref[2 * r : 2 * r + 1, :])
        sine = jnp.where(odd, sin_ref[2 * r + 1 : 2 * r + 2, :], sin_ref[2 * r : 2 * r + 1, :])
        parts = []
        for h in range(3):
            chosen = jnp.dot(pick, q_ref[:, h * HEAD : (h + 1) * HEAD], preferred_element_type=F32)
            first, second = chosen[:, :half], chosen[:, half:]
            parts.append(
                jnp.concatenate([first * cosine - second * sine, second * cosine + first * sine], 1)
            )
        return jnp.concatenate(parts, 0).astype(BF16)

    def scores_of(r, query):
        return lax.dot_general(query, k_ref[r], contract_last, preferred_element_type=F32) * scale

    query = query_of(0)
    scores = scores_of(0, query)
    for r in range(seqs):
        if r + 1 < seqs:
            next_query = query_of(r + 1)
            next_scores = scores_of(r + 1, next_query)
        valid = lax.broadcasted_iota(jnp.int32, scores.shape, 1) < lengths[r]
        cached = jnp.where(valid, scores, -jnp.inf)
        new = new_rows[2 * r : 2 * r + 2, :]
        wide = query.astype(F32)
        fresh0 = jnp.sum(wide * new[0:1, :HEAD], -1, keepdims=True) * scale
        fresh1 = jnp.sum(wide * new[1:2, :HEAD], -1, keepdims=True) * scale
        fresh1 = jnp.where(second_step, fresh1, -jnp.inf)
        top = jnp.maximum(jnp.max(cached, -1, keepdims=True), jnp.maximum(fresh0, fresh1))
        exp_cached = jnp.exp(cached - top)
        exp0 = jnp.exp(fresh0 - top)
        exp1 = jnp.exp(fresh1 - top)
        inverse = 1.0 / (jnp.sum(exp_cached, -1, keepdims=True) + exp0 + exp1)
        weights = (exp_cached * inverse).astype(BF16)
        weight0 = (exp0 * inverse).astype(BF16).astype(F32)
        weight1 = (exp1 * inverse).astype(BF16).astype(F32)
        result = jnp.dot(weights, v_ref[r], preferred_element_type=F32)
        result = result + weight0 * new[0:1, HEAD:] + weight1 * new[1:2, HEAD:]
        result = result.astype(BF16)
        pick = pick_of(r)
        for h in range(3):
            spread = lax.dot_general(
                pick,
                result[h * 32 : (h + 1) * 32],
                (((0,), (0,)), ((), ())),
                preferred_element_type=F32,
            )
            columns = slice(h * HEAD, (h + 1) * HEAD)
            if r == 0:
                acc_ref[:, columns] = spread
            else:
                acc_ref[:, columns] += spread
        if r + 1 < seqs:
            query, scores = next_query, next_scores
    out_ref[...] = acc_ref[...].astype(BF16)


def attend(lengths, query, cosine, sine, keyval, keys, values):
    seqs, context, _ = keys.shape
    rows, columns = query.shape
    vmem_spec = pl.BlockSpec(memory_space=pltpu.VMEM)
    return pl.pallas_call(
        attend_kernel,
        out_shape=[
            jax.ShapeDtypeStruct((rows, columns), BF16),
            jax.ShapeDtypeStruct(keyval.shape, BF16),
        ],
        in_specs=[pl.BlockSpec(memory_space=pltpu.SMEM)] + [vmem_spec] * 6,
        out_specs=[vmem_spec] * 2,
        scratch_shapes=[pltpu.VMEM((rows, columns), F32)],
        compiler_params=pltpu.CompilerParams(vmem_limit_bytes=20 * 2**20),
        cost_estimate=pl.CostEstimate(
            flops=4 * seqs * 96 * context * HEAD,
            bytes_accessed=4 * seqs * context * HEAD,
            transcendentals=seqs * 96 * context,
        ),
        name="attention",
    )(lengths, query, cosine, sine, keyval, keys, values)


def output_kernel(groups, place, *refs):
    pieces, (w_ref, *outs), rows_ref = refs[:8], refs[8:-1], refs[-1]
    x, y, z, core = place[0], place[1], place[2], place[3]
    for index, piece in enumerate(pieces):
        at_core = core if index < 4 else 1 - core
        slot = (0, 3, 1, 2)[index % 4]
        ahead = jnp.where(at_core == 0, slot, (RING - slot) % RING)
        dy = lax.rem(x + ahead - y + RING, RING)
        for part in range(2):
            dz = lax.rem(2 * at_core + part - z + RING, RING)
            outer, inner = jnp.where(core == 0, dy, dz), jnp.where(core == 0, dz, dy)
            for position, group in enumerate(groups):

                @pl.when(outer == group)
                def _():
                    rows_ref[position * RING + inner] = piece[part * 64 : (part + 1) * 64, :]

    outs = list(outs)
    for position, group in enumerate(groups):
        rows = rows_ref[RING * position : RING * position + RING].reshape(256, w_ref.shape[0])
        targets = [outs.pop(0)] if group == 0 else [outs.pop(0), outs.pop(0)]
        for start in range(0, w_ref.shape[1], 768):
            columns = slice(start, start + 768)
            result = jnp.dot(rows, w_ref[:, columns], preferred_element_type=F32)
            if group == 0:
                targets[0][:, columns] = result
            else:
                targets[0][:, columns] = result[:128].astype(targets[0].dtype)
                targets[1][:, columns] = result[128:].astype(targets[1].dtype)


def project_output(place, pieces, w_out, groups):
    depth, columns = w_out.shape
    vmem_spec = pl.BlockSpec(memory_space=pltpu.VMEM)
    shapes = []
    for group in groups:
        if group == 0:
            shapes.append(jax.ShapeDtypeStruct((256, columns), F32))
        else:
            for added in (group == 1, group == 3):
                shapes.append(jax.ShapeDtypeStruct((128, columns), F32 if added else BF16))
    return pl.pallas_call(
        functools.partial(output_kernel, groups),
        out_shape=shapes,
        in_specs=[pl.BlockSpec(memory_space=pltpu.SMEM)] + [vmem_spec] * 9,
        out_specs=[vmem_spec] * len(shapes),
        scratch_shapes=[pltpu.VMEM((RING * len(groups), 64, depth), BF16)],
        compiler_params=pltpu.CompilerParams(vmem_limit_bytes=20 * 2**20),
        cost_estimate=pl.CostEstimate(
            flops=2 * 256 * len(groups) * depth * columns,
            bytes_accessed=8 * 2**20,
            transcendentals=0,
        ),
        name="output_projection",
    )(place, *pieces, w_out)


def body(tokens, gain, w_query, w_keyval, w_out, key_cache, value_cache, lengths):
    seqs = lengths.shape[0]
    gx, yz = lax.axis_index("gx"), lax.axis_index("yz")
    place = jnp.stack([gx // 2, yz // RING, lax.rem(yz, RING), lax.rem(gx, 2)]).astype(jnp.int32)
    positions = jnp.repeat(lengths, 2) + lax.rem(jnp.arange(2 * seqs, dtype=jnp.int32), 2)
    cosine, sine = rotation_tables(positions)

    count = tokens.shape[0] * 2
    features = tokens.shape[2]
    raw = lax.optimization_barrier(tokens.reshape(count, features))
    sums = row_sums(raw)
    sums = sums + send_core(sums)
    sums, cosine, sine, place, raw = lax.optimization_barrier((sums, cosine, sine, place, raw))
    before, after = send_inner(raw, 1), send_inner(raw, -1)
    sums = sums + send_x(sums, 1) + send_x(sums, 2) + send_x(sums, 3)
    sums, before, after = lax.optimization_barrier((sums, before, after))
    before_sums, after_sums = send_inner(sums, 1), send_inner(sums, -1)
    before, before_sums = lax.optimization_barrier((before, before_sums))
    far, far_sums = send_inner(before, 1), send_inner(sums, 2)
    scale = gain.reshape(1, features)
    near = normalize(raw, before, sums, before_sums, scale)
    wide = normalize(after, far, after_sums, far_sums, scale)

    keyval_away, keyval_keep = project_keyval(place, near, w_keyval)
    kept = keyval_keep + send_core(keyval_away)

    near_before, near_after = send_outer(near, 1), send_outer(near, -1)
    near_before, near_after, wide, kept = lax.optimization_barrier(
        (near_before, near_after, wide, kept)
    )
    wide_after = send_outer(wide, -1)
    near_far = send_outer(near_before, 1)
    near_far, wide_again = lax.optimization_barrier((near_far, wide))
    wide_before = send_outer(wide_again, 1)
    wide_far = send_outer(wide_after, -1)

    kept = kept.reshape(RING, count // 8, 2 * HEAD)
    keyval = kept[0] + send_ahead(kept[1], 1) + send_ahead(kept[2], 2) + send_ahead(kept[3], 3)
    keyval = keyval.astype(BF16)

    pieces = [near, near_before, near_after, near_far, wide, wide_before, wide_after, wide_far]
    columns = w_query.shape[1]
    pieces, keyval = lax.optimization_barrier((pieces, keyval))
    away, keep = project_query(place, pieces, w_query, 1)
    summed = (keep + send_core(away)).reshape(2, 128, columns)
    far, behind = send_x(summed[0], 1), send_x(summed[1], -1)
    away, keep = project_query(place, pieces, w_query, 0)
    summed = (keep + send_core(away)).reshape(2, 128, columns)
    moves = [
        (g * 16 + j, (j // 2) * 16 + (j % 2) * 8 + g) for g in range(8) for j in range(16)
    ]
    keyval = lax.ppermute(keyval, ("gx", "yz"), moves)
    far, keyval = lax.optimization_barrier((far, keyval))
    ahead = send_x(summed[1] + far, 1)
    query = (summed[0] + ahead + behind).astype(BF16).reshape(16, 8, columns)
    query = lax.all_to_all(query, "yz", split_axis=0, concat_axis=0)

    heads_out, new_keyval = attend(
        lengths, query.reshape(128, columns), cosine, sine, keyval, key_cache, value_cache
    )
    heads_out = lax.all_to_all(
        heads_out.reshape(16, 8, columns), "yz", split_axis=0, concat_axis=0
    ).reshape(128, columns)
    before = send_x(heads_out, 1)
    after = send_x(heads_out, -1)
    pieces = [heads_out, before, after, send_x(before, 1)]
    pieces = pieces + [send_core(p) for p in pieces]
    two_low, two_high = project_output(place, pieces, w_out, (2,))
    one_low, one_high, three_low, three_high, own = project_output(
        place, pieces, w_out, (1, 3, 0)
    )

    far_low, far_high = send_outer(two_low, 1), send_outer(two_high, -1)
    far_low, far_high = lax.optimization_barrier((far_low, far_high))
    early_high, early_low = send_outer(one_high, 1), send_outer(three_low, -1)
    late_low = send_outer((one_low + far_low.astype(F32)).astype(BF16), 1)
    late_high = send_outer((three_high + far_high.astype(F32)).astype(BF16), -1)
    low = own[:128] + early_low.astype(F32) + late_low.astype(F32)
    high = own[128:] + early_high.astype(F32) + late_high.astype(F32)
    here, one, two, three = low[:64], low[64:], high[:64], high[64:]
    two = two.astype(BF16)
    far_low, far_high = send_inner(two[:32], 1), send_inner(two[32:], -1)
    one = jnp.concatenate([one[:32] + far_low.astype(F32), one[32:]], 0)
    three = jnp.concatenate([three[:32], three[32:] + far_high.astype(F32)], 0)
    branch = here + send_inner(one, 1) + send_inner(three, -1)
    mixed = (raw.astype(F32) + branch).astype(BF16).reshape(tokens.shape)
    return (mixed, new_keyval.reshape(seqs, 2, 2 * HEAD))


def solution(mesh):
    return jax.shard_map(
        body,
        mesh=mesh,
        in_specs=(
            P("yz", None, "gx"),
            P("gx"),
            P("gx", "yz"),
            P("gx", None),
            P("yz", "gx"),
            P(("gx", "yz"), None, None),
            P(("gx", "yz"), None, None),
            P(("gx", "yz")),
        ),
        out_specs=(P("yz", None, "gx"), P(("gx", "yz"), None, None)),
        check_vma=False,
    )
```

```python
import functools

import jax
import jax.numpy as jnp
from jax import lax
from jax.experimental import pallas as pl
from jax.experimental.pallas import tpu as pltpu
from jax.sharding import PartitionSpec as P

D = 18432
HEADS = 48
HEAD = 256
RING = 4
F32 = jnp.float32
BF16 = jnp.bfloat16


def shift(value, move):
    pairs = []
    for x in range(RING):
        for core in range(2):
            for y in range(RING):
                for z in range(RING):
                    dx, dy, dz = move(core)
                    target = (2 * ((x + dx) % RING) + core) * 16
                    target += RING * ((y + dy) % RING) + (z + dz) % RING
                    pairs.append(((2 * x + core) * 16 + RING * y + z, target))
    return lax.ppermute(value, ("gx", "yz"), pairs)


def send_core(value):
    pairs = [(2 * x + c, 2 * x + 1 - c) for x in range(RING) for c in range(2)]
    return lax.ppermute(value, "gx", pairs)


def send_x(value, step):
    return shift(value, lambda core: ((1 - 2 * core) * step, 0, 0))


def send_ahead(value, step):
    return shift(value, lambda core: (step, 0, 0))


def send_inner(value, step):
    return shift(value, lambda core: (0, core * step, (1 - core) * step))


def send_outer(value, step):
    return shift(value, lambda core: (0, (1 - core) * step, core * step))


def rotation_tables(positions):
    half = HEAD // 2
    freq = 10000.0 ** (-jnp.arange(half, dtype=F32) * 2.0 / HEAD)
    angle = positions.astype(F32)[..., None] * freq
    return jnp.cos(angle), jnp.sin(angle)


def sums_kernel(rows_ref, out_ref):
    rows = rows_ref[...].astype(F32)
    total = jnp.sum(rows, -1, keepdims=True)
    squares = jnp.sum(rows * rows, -1, keepdims=True)
    out_ref[...] = jnp.concatenate([total, squares], 1)


def row_sums(rows):
    vmem_spec = pl.BlockSpec(memory_space=pltpu.VMEM)
    return pl.pallas_call(
        sums_kernel,
        out_shape=jax.ShapeDtypeStruct((rows.shape[0], 2), F32),
        in_specs=[vmem_spec],
        out_specs=vmem_spec,
        compiler_params=pltpu.CompilerParams(vmem_limit_bytes=12 * 2**20),
        name="row_sums",
    )(rows)


def normalize_kernel(one_ref, two_ref, one_sums, two_sums, gain_ref, out_ref):
    count = one_ref.shape[0]
    for index, (rows_ref, sums_ref) in enumerate(((one_ref, one_sums), (two_ref, two_sums))):
        mean = sums_ref[:, 0:1] / D
        var = sums_ref[:, 1:2] / D - mean * mean
        rows = rows_ref[...].astype(F32)
        normed = (rows - mean) * lax.rsqrt(var + 1e-05) * gain_ref[...]
        out_ref[index * count : (index + 1) * count, :] = normed.astype(BF16)


def normalize(one, two, one_sums, two_sums, gain):
    vmem_spec = pl.BlockSpec(memory_space=pltpu.VMEM)
    return pl.pallas_call(
        normalize_kernel,
        out_shape=jax.ShapeDtypeStruct((2 * one.shape[0], one.shape[1]), BF16),
        in_specs=[vmem_spec] * 5,
        out_specs=vmem_spec,
        compiler_params=pltpu.CompilerParams(vmem_limit_bytes=12 * 2**20),
        name="normalize",
    )(one, two, one_sums, two_sums, gain)


def keyval_kernel(place, rows_ref, w_ref, away_ref, keep_ref, sums_ref):
    x, core = place[0], place[3]
    rows = rows_ref[: sums_ref.shape[0], :]
    sums_ref[...] = jnp.dot(rows, w_ref[...], preferred_element_type=F32)
    for slot in range(RING):
        block = 2 * lax.rem(x + slot, RING)
        target = pl.ds(8 * slot, 8)
        keep_ref[target, :] = sums_ref[pl.ds(pl.multiple_of(8 * (block + core), 8), 8), :]
        away_ref[target, :] = sums_ref[pl.ds(pl.multiple_of(8 * (block + 1 - core), 8), 8), :]


def project_keyval(place, rows, w_keyval):
    count, depth = rows.shape[0] // 2, rows.shape[1]
    columns = w_keyval.shape[1]
    vmem_spec = pl.BlockSpec(memory_space=pltpu.VMEM)
    half = jax.ShapeDtypeStruct((count // 2, columns), F32)
    return pl.pallas_call(
        keyval_kernel,
        out_shape=[half, half],
        in_specs=[pl.BlockSpec(memory_space=pltpu.SMEM)] + [vmem_spec] * 2,
        out_specs=[vmem_spec] * 2,
        scratch_shapes=[pltpu.VMEM((count, columns), F32)],
        compiler_params=pltpu.CompilerParams(vmem_limit_bytes=12 * 2**20),
        cost_estimate=pl.CostEstimate(
            flops=2 * count * depth * columns, bytes_accessed=3 * 2**20, transcendentals=0
        ),
        name="keyval_projection",
    )(place, rows, w_keyval)


def query_kernel(pair, place, *refs):
    pieces, (w_ref, away_ref, keep_ref, rows_ref) = refs[:8], refs[8:]
    x, y, z, core = place[0], place[1], place[2], place[3]
    for index, piece in enumerate(pieces):
        for part in range(2):
            outer = (0, 3, 1, 2)[index % 4]
            inner = ((0, 3), (1, 2))[index // 4][part]
            at_y = lax.rem(y + jnp.where(core == 0, outer, inner), RING)
            at_z = lax.rem(z + jnp.where(core == 0, inner, outer), RING)
            to_core = at_z // 2
            ahead = lax.rem(at_y - x + RING, RING)
            slot = jnp.where(to_core == 0, ahead, lax.rem(RING - ahead, RING))
            mine = jnp.where(to_core == core, 4, 0)
            position = mine + lax.rem(slot, 2) * 2 + lax.rem(at_z, 2)

            @pl.when(slot // 2 == pair)
            def _():
                rows_ref[position] = piece[part * 64 : (part + 1) * 64, :]

    rows = rows_ref[...].reshape(512, w_ref.shape[0])
    result = jnp.dot(rows, w_ref[...], preferred_element_type=F32)
    away_ref[...] = result[:256]
    keep_ref[...] = result[256:]


def project_query(place, pieces, w_query, pair):
    depth, columns = w_query.shape
    vmem_spec = pl.BlockSpec(memory_space=pltpu.VMEM)
    half = jax.ShapeDtypeStruct((256, columns), F32)
    return pl.pallas_call(
        functools.partial(query_kernel, pair),
        out_shape=[half, half],
        in_specs=[pl.BlockSpec(memory_space=pltpu.SMEM)] + [vmem_spec] * 9,
        out_specs=[vmem_spec] * 2,
        scratch_shapes=[pltpu.VMEM((8, 64, depth), BF16)],
        compiler_params=pltpu.CompilerParams(vmem_limit_bytes=20 * 2**20),
        cost_estimate=pl.CostEstimate(
            flops=2 * 512 * depth * columns, bytes_accessed=8 * 2**20, transcendentals=0
        ),
        name="query_projection",
    )(place, *pieces, w_query)


def attend_kernel(lengths, q_ref, cos_ref, sin_ref, kv_ref, k_ref, v_ref, out_ref, new_ref, acc_ref):
    seqs = k_ref.shape[0]
    half = HEAD // 2
    rows = q_ref.shape[0]
    scale = HEAD ** (-0.5)
    contract_last = (((1,), (1,)), ((), ()))
    pick_row = lax.broadcasted_iota(jnp.int32, (32, rows), 0)
    pick_col = lax.broadcasted_iota(jnp.int32, (32, rows), 1)
    odd = lax.rem(lax.broadcasted_iota(jnp.int32, (32, half), 0), 2) == 1
    second_step = lax.rem(lax.broadcasted_iota(jnp.int32, (96, 1), 0), 2) == 1
    first = kv_ref[:, :half].astype(F32)
    second = kv_ref[:, half:HEAD].astype(F32)
    cosine, sine = cos_ref[...], sin_ref[...]
    new_ref[:, :half] = (first * cosine - second * sine).astype(BF16)
    new_ref[:, half:HEAD] = (second * cosine + first * sine).astype(BF16)
    new_ref[:, HEAD:] = kv_ref[:, HEAD:]
    new_rows = new_ref[...].astype(F32)

    def pick_of(r):
        return (pick_col == (pick_row // 2) * 8 + 2 * r + lax.rem(pick_row, 2)).astype(BF16)

    def query_of(r):
        pick = pick_of(r)
        cosine = jnp.where(odd, cos_ref[2 * r + 1 : 2 * r + 2, :], cos_ref[2 * r : 2 * r + 1, :])
        sine = jnp.where(odd, sin_ref[2 * r + 1 : 2 * r + 2, :], sin_ref[2 * r : 2 * r + 1, :])
        parts = []
        for h in range(3):
            chosen = jnp.dot(pick, q_ref[:, h * HEAD : (h + 1) * HEAD], preferred_element_type=F32)
            first, second = chosen[:, :half], chosen[:, half:]
            parts.append(
                jnp.concatenate([first * cosine - second * sine, second * cosine + first * sine], 1)
            )
        return jnp.concatenate(parts, 0).astype(BF16)

    def scores_of(r, query):
        return lax.dot_general(query, k_ref[r], contract_last, preferred_element_type=F32) * scale

    query = query_of(0)
    scores = scores_of(0, query)
    for r in range(seqs):
        if r + 1 < seqs:
            next_query = query_of(r + 1)
            next_scores = scores_of(r + 1, next_query)
        valid = lax.broadcasted_iota(jnp.int32, scores.shape, 1) < lengths[r]
        cached = jnp.where(valid, scores, -jnp.inf)
        new = new_rows[2 * r : 2 * r + 2, :]
        wide = query.astype(F32)
        fresh0 = jnp.sum(wide * new[0:1, :HEAD], -1, keepdims=True) * scale
        fresh1 = jnp.sum(wide * new[1:2, :HEAD], -1, keepdims=True) * scale
        fresh1 = jnp.where(second_step, fresh1, -jnp.inf)
        top = jnp.maximum(jnp.max(cached, -1, keepdims=True), jnp.maximum(fresh0, fresh1))
        exp_cached = jnp.exp(cached - top)
        exp0 = jnp.exp(fresh0 - top)
        exp1 = jnp.exp(fresh1 - top)
        inverse = 1.0 / (jnp.sum(exp_cached, -1, keepdims=True) + exp0 + exp1)
        weights = (exp_cached * inverse).astype(BF16)
        weight0 = (exp0 * inverse).astype(BF16).astype(F32)
        weight1 = (exp1 * inverse).astype(BF16).astype(F32)
        result = jnp.dot(weights, v_ref[r], preferred_element_type=F32)
        result = result + weight0 * new[0:1, HEAD:] + weight1 * new[1:2, HEAD:]
        result = result.astype(BF16)
        pick = pick_of(r)
        for h in range(3):
            spread = lax.dot_general(
                pick,
                result[h * 32 : (h + 1) * 32],
                (((0,), (0,)), ((), ())),
                preferred_element_type=F32,
            )
            columns = slice(h * HEAD, (h + 1) * HEAD)
            if r == 0:
                acc_ref[:, columns] = spread
            else:
                acc_ref[:, columns] += spread
        if r + 1 < seqs:
            query, scores = next_query, next_scores
    out_ref[...] = acc_ref[...].astype(BF16)


def attend(lengths, query, cosine, sine, keyval, keys, values):
    seqs, context, _ = keys.shape
    rows, columns = query.shape
    vmem_spec = pl.BlockSpec(memory_space=pltpu.VMEM)
    return pl.pallas_call(
        attend_kernel,
        out_shape=[
            jax.ShapeDtypeStruct((rows, columns), BF16),
            jax.ShapeDtypeStruct(keyval.shape, BF16),
        ],
        in_specs=[pl.BlockSpec(memory_space=pltpu.SMEM)] + [vmem_spec] * 6,
        out_specs=[vmem_spec] * 2,
        scratch_shapes=[pltpu.VMEM((rows, columns), F32)],
        compiler_params=pltpu.CompilerParams(vmem_limit_bytes=20 * 2**20),
        cost_estimate=pl.CostEstimate(
            flops=4 * seqs * 96 * context * HEAD,
            bytes_accessed=4 * seqs * context * HEAD,
            transcendentals=seqs * 96 * context,
        ),
        name="attention",
    )(lengths, query, cosine, sine, keyval, keys, values)


def output_kernel(groups, place, *refs):
    pieces, (w_ref, *outs), rows_ref = refs[:8], refs[8:-1], refs[-1]
    x, y, z, core = place[0], place[1], place[2], place[3]
    for index, piece in enumerate(pieces):
        at_core = core if index < 4 else 1 - core
        slot = (0, 3, 1, 2)[index % 4]
        ahead = jnp.where(at_core == 0, slot, (RING - slot) % RING)
        dy = lax.rem(x + ahead - y + RING, RING)
        for part in range(2):
            dz = lax.rem(2 * at_core + part - z + RING, RING)
            outer, inner = jnp.where(core == 0, dy, dz), jnp.where(core == 0, dz, dy)
            for position, group in enumerate(groups):

                @pl.when(outer == group)
                def _():
                    rows_ref[position * RING + inner] = piece[part * 64 : (part + 1) * 64, :]

    outs = list(outs)
    for position, group in enumerate(groups):
        rows = rows_ref[RING * position : RING * position + RING].reshape(256, w_ref.shape[0])
        targets = [outs.pop(0)] if group == 0 else [outs.pop(0), outs.pop(0)]
        for start in range(0, w_ref.shape[1], 768):
            columns = slice(start, start + 768)
            result = jnp.dot(rows, w_ref[:, columns], preferred_element_type=F32)
            if group == 0:
                targets[0][:, columns] = result
            else:
                targets[0][:, columns] = result[:128].astype(targets[0].dtype)
                targets[1][:, columns] = result[128:].astype(targets[1].dtype)


def project_output(place, pieces, w_out, groups):
    depth, columns = w_out.shape
    vmem_spec = pl.BlockSpec(memory_space=pltpu.VMEM)
    shapes = []
    for group in groups:
        if group == 0:
            shapes.append(jax.ShapeDtypeStruct((256, columns), F32))
        else:
            for added in (group == 1, group == 3):
                shapes.append(jax.ShapeDtypeStruct((128, columns), F32 if added else BF16))
    return pl.pallas_call(
        functools.partial(output_kernel, groups),
        out_shape=shapes,
        in_specs=[pl.BlockSpec(memory_space=pltpu.SMEM)] + [vmem_spec] * 9,
        out_specs=[vmem_spec] * len(shapes),
        scratch_shapes=[pltpu.VMEM((RING * len(groups), 64, depth), BF16)],
        compiler_params=pltpu.CompilerParams(vmem_limit_bytes=20 * 2**20),
        cost_estimate=pl.CostEstimate(
            flops=2 * 256 * len(groups) * depth * columns,
            bytes_accessed=8 * 2**20,
            transcendentals=0,
        ),
        name="output_projection",
    )(place, *pieces, w_out)


def body(tokens, gain, w_query, w_keyval, w_out, key_cache, value_cache, lengths):
    seqs = lengths.shape[0]
    gx, yz = lax.axis_index("gx"), lax.axis_index("yz")
    place = jnp.stack([gx // 2, yz // RING, lax.rem(yz, RING), lax.rem(gx, 2)]).astype(jnp.int32)
    positions = jnp.repeat(lengths, 2) + lax.rem(jnp.arange(2 * seqs, dtype=jnp.int32), 2)
    cosine, sine = rotation_tables(positions)

    count = tokens.shape[0] * 2
    features = tokens.shape[2]
    raw = lax.optimization_barrier(tokens.reshape(count, features))
    sums = row_sums(raw)
    sums = sums + send_core(sums)
    sums, cosine, sine, place, raw = lax.optimization_barrier((sums, cosine, sine, place, raw))
    before = send_inner(raw, 1)
    sums = sums + send_x(sums, 1) + send_x(sums, 2) + send_x(sums, 3)
    sums, before, raw = lax.optimization_barrier((sums, before, raw))
    after = send_inner(raw, -1)
    before_sums, after_sums = send_inner(sums, 1), send_inner(sums, -1)
    before, before_sums = lax.optimization_barrier((before, before_sums))
    far, far_sums = send_inner(before, 1), send_inner(sums, 2)
    scale = gain.reshape(1, features)
    near = normalize(raw, before, sums, before_sums, scale)
    wide = normalize(after, far, after_sums, far_sums, scale)

    keyval_away, keyval_keep = project_keyval(place, near, w_keyval)
    kept = keyval_keep + send_core(keyval_away)

    near_before, near_after = send_outer(near, 1), send_outer(near, -1)
    near_before, near_after, wide, kept = lax.optimization_barrier(
        (near_before, near_after, wide, kept)
    )
    wide_after = send_outer(wide, -1)
    near_far = send_outer(near_before, 1)
    near_far, wide_again = lax.optimization_barrier((near_far, wide))
    wide_before = send_outer(wide_again, 1)
    wide_far = send_outer(wide_after, -1)

    kept = kept.reshape(RING, count // 8, 2 * HEAD)
    keyval = kept[0] + send_ahead(kept[1], 1) + send_ahead(kept[2], 2) + send_ahead(kept[3], 3)
    keyval = keyval.astype(BF16)

    pieces = [near, near_before, near_after, near_far, wide, wide_before, wide_after, wide_far]
    columns = w_query.shape[1]
    pieces, keyval = lax.optimization_barrier((pieces, keyval))
    away, keep = project_query(place, pieces, w_query, 1)
    summed = (keep + send_core(away)).reshape(2, 128, columns)
    far, behind = send_x(summed[0], 1), send_x(summed[1], -1)
    away, keep = project_query(place, pieces, w_query, 0)
    summed = (keep + send_core(away)).reshape(2, 128, columns)
    moves = [
        (g * 16 + j, (j // 2) * 16 + (j % 2) * 8 + g) for g in range(8) for j in range(16)
    ]
    keyval = lax.ppermute(keyval, ("gx", "yz"), moves)
    far, keyval = lax.optimization_barrier((far, keyval))
    ahead = send_x(summed[1] + far, 1)
    query = (summed[0] + ahead + behind).astype(BF16).reshape(16, 8, columns)
    query = lax.all_to_all(query, "yz", split_axis=0, concat_axis=0)

    heads_out, new_keyval = attend(
        lengths, query.reshape(128, columns), cosine, sine, keyval, key_cache, value_cache
    )
    heads_out = lax.all_to_all(
        heads_out.reshape(16, 8, columns), "yz", split_axis=0, concat_axis=0
    ).reshape(128, columns)
    before = send_x(heads_out, 1)
    after = send_x(heads_out, -1)
    pieces = [heads_out, before, after, send_x(before, 1)]
    pieces = pieces + [send_core(p) for p in pieces]
    two_low, two_high = project_output(place, pieces, w_out, (2,))
    one_low, one_high, three_low, three_high, own = project_output(
        place, pieces, w_out, (1, 3, 0)
    )

    far_low, far_high = send_outer(two_low, 1), send_outer(two_high, -1)
    far_low, far_high = lax.optimization_barrier((far_low, far_high))
    early_high, early_low = send_outer(one_high, 1), send_outer(three_low, -1)
    late_low = send_outer((one_low + far_low.astype(F32)).astype(BF16), 1)
    late_high = send_outer((three_high + far_high.astype(F32)).astype(BF16), -1)
    low = own[:128] + early_low.astype(F32) + late_low.astype(F32)
    high = own[128:] + early_high.astype(F32) + late_high.astype(F32)
    here, one, two, three = low[:64], low[64:], high[:64], high[64:]
    two = two.astype(BF16)
    far_low, far_high = send_inner(two[:32], 1), send_inner(two[32:], -1)
    one = jnp.concatenate([one[:32] + far_low.astype(F32), one[32:]], 0)
    three = jnp.concatenate([three[:32], three[32:] + far_high.astype(F32)], 0)
    branch = here + send_inner(one, 1) + send_inner(three, -1)
    mixed = (raw.astype(F32) + branch).astype(BF16).reshape(tokens.shape)
    return (mixed, new_keyval.reshape(seqs, 2, 2 * HEAD))


def solution(mesh):
    return jax.shard_map(
        body,
        mesh=mesh,
        in_specs=(
            P("yz", None, "gx"),
            P("gx"),
            P("gx", "yz"),
            P("gx", None),
            P("yz", "gx"),
            P(("gx", "yz"), None, None),
            P(("gx", "yz"), None, None),
            P(("gx", "yz")),
        ),
        out_specs=(P("yz", None, "gx"), P(("gx", "yz"), None, None)),
        check_vma=False,
    )
```

```python
import functools

import jax
import jax.numpy as jnp
from jax import lax
from jax.experimental import pallas as pl
from jax.experimental.pallas import tpu as pltpu
from jax.sharding import PartitionSpec as P

D = 18432
HEADS = 48
HEAD = 256
RING = 4
F32 = jnp.float32
BF16 = jnp.bfloat16


def shift(value, move):
    pairs = []
    for x in range(RING):
        for core in range(2):
            for y in range(RING):
                for z in range(RING):
                    dx, dy, dz = move(core)
                    target = (2 * ((x + dx) % RING) + core) * 16
                    target += RING * ((y + dy) % RING) + (z + dz) % RING
                    pairs.append(((2 * x + core) * 16 + RING * y + z, target))
    return lax.ppermute(value, ("gx", "yz"), pairs)


def send_core(value):
    pairs = [(2 * x + c, 2 * x + 1 - c) for x in range(RING) for c in range(2)]
    return lax.ppermute(value, "gx", pairs)


def send_x(value, step):
    return shift(value, lambda core: ((1 - 2 * core) * step, 0, 0))


def send_ahead(value, step):
    return shift(value, lambda core: (step, 0, 0))


def send_inner(value, step):
    return shift(value, lambda core: (0, core * step, (1 - core) * step))


def send_outer(value, step):
    return shift(value, lambda core: (0, (1 - core) * step, core * step))


def rotation_tables(positions):
    half = HEAD // 2
    freq = 10000.0 ** (-jnp.arange(half, dtype=F32) * 2.0 / HEAD)
    angle = positions.astype(F32)[..., None] * freq
    return jnp.cos(angle), jnp.sin(angle)


def sums_kernel(rows_ref, out_ref):
    rows = rows_ref[...].astype(F32)
    total = jnp.sum(rows, -1, keepdims=True)
    squares = jnp.sum(rows * rows, -1, keepdims=True)
    out_ref[...] = jnp.concatenate([total, squares], 1)


def row_sums(rows):
    vmem_spec = pl.BlockSpec(memory_space=pltpu.VMEM)
    return pl.pallas_call(
        sums_kernel,
        out_shape=jax.ShapeDtypeStruct((rows.shape[0], 2), F32),
        in_specs=[vmem_spec],
        out_specs=vmem_spec,
        compiler_params=pltpu.CompilerParams(vmem_limit_bytes=12 * 2**20),
        name="row_sums",
    )(rows)


def normalize_kernel(one_ref, two_ref, one_sums, two_sums, gain_ref, out_ref):
    count = one_ref.shape[0]
    for index, (rows_ref, sums_ref) in enumerate(((one_ref, one_sums), (two_ref, two_sums))):
        mean = sums_ref[:, 0:1] / D
        var = sums_ref[:, 1:2] / D - mean * mean
        rows = rows_ref[...].astype(F32)
        normed = (rows - mean) * lax.rsqrt(var + 1e-05) * gain_ref[...]
        out_ref[index * count : (index + 1) * count, :] = normed.astype(BF16)


def normalize(one, two, one_sums, two_sums, gain):
    vmem_spec = pl.BlockSpec(memory_space=pltpu.VMEM)
    return pl.pallas_call(
        normalize_kernel,
        out_shape=jax.ShapeDtypeStruct((2 * one.shape[0], one.shape[1]), BF16),
        in_specs=[vmem_spec] * 5,
        out_specs=vmem_spec,
        compiler_params=pltpu.CompilerParams(vmem_limit_bytes=12 * 2**20),
        name="normalize",
    )(one, two, one_sums, two_sums, gain)


def keyval_kernel(place, rows_ref, w_ref, away_ref, keep_ref, sums_ref):
    x, core = place[0], place[3]
    rows = rows_ref[: sums_ref.shape[0], :]
    sums_ref[...] = jnp.dot(rows, w_ref[...], preferred_element_type=F32)
    for slot in range(RING):
        block = 2 * lax.rem(x + slot, RING)
        target = pl.ds(8 * slot, 8)
        keep_ref[target, :] = sums_ref[pl.ds(pl.multiple_of(8 * (block + core), 8), 8), :]
        away_ref[target, :] = sums_ref[pl.ds(pl.multiple_of(8 * (block + 1 - core), 8), 8), :]


def project_keyval(place, rows, w_keyval):
    count, depth = rows.shape[0] // 2, rows.shape[1]
    columns = w_keyval.shape[1]
    vmem_spec = pl.BlockSpec(memory_space=pltpu.VMEM)
    half = jax.ShapeDtypeStruct((count // 2, columns), F32)
    return pl.pallas_call(
        keyval_kernel,
        out_shape=[half, half],
        in_specs=[pl.BlockSpec(memory_space=pltpu.SMEM)] + [vmem_spec] * 2,
        out_specs=[vmem_spec] * 2,
        scratch_shapes=[pltpu.VMEM((count, columns), F32)],
        compiler_params=pltpu.CompilerParams(vmem_limit_bytes=12 * 2**20),
        cost_estimate=pl.CostEstimate(
            flops=2 * count * depth * columns, bytes_accessed=3 * 2**20, transcendentals=0
        ),
        name="keyval_projection",
    )(place, rows, w_keyval)


def query_kernel(pair, place, *refs):
    pieces, (w_ref, away_ref, keep_ref, rows_ref) = refs[:8], refs[8:]
    x, y, z, core = place[0], place[1], place[2], place[3]
    for index, piece in enumerate(pieces):
        for part in range(2):
            outer = (0, 3, 1, 2)[index % 4]
            inner = ((0, 3), (1, 2))[index // 4][part]
            at_y = lax.rem(y + jnp.where(core == 0, outer, inner), RING)
            at_z = lax.rem(z + jnp.where(core == 0, inner, outer), RING)
            to_core = at_z // 2
            ahead = lax.rem(at_y - x + RING, RING)
            slot = jnp.where(to_core == 0, ahead, lax.rem(RING - ahead, RING))
            mine = jnp.where(to_core == core, 4, 0)
            position = mine + lax.rem(slot, 2) * 2 + lax.rem(at_z, 2)

            @pl.when(slot // 2 == pair)
            def _():
                rows_ref[position] = piece[part * 64 : (part + 1) * 64, :]

    rows = rows_ref[...].reshape(512, w_ref.shape[0])
    result = jnp.dot(rows, w_ref[...], preferred_element_type=F32)
    away_ref[...] = result[:256]
    keep_ref[...] = result[256:]


def project_query(place, pieces, w_query, pair):
    depth, columns = w_query.shape
    vmem_spec = pl.BlockSpec(memory_space=pltpu.VMEM)
    half = jax.ShapeDtypeStruct((256, columns), F32)
    return pl.pallas_call(
        functools.partial(query_kernel, pair),
        out_shape=[half, half],
        in_specs=[pl.BlockSpec(memory_space=pltpu.SMEM)] + [vmem_spec] * 9,
        out_specs=[vmem_spec] * 2,
        scratch_shapes=[pltpu.VMEM((8, 64, depth), BF16)],
        compiler_params=pltpu.CompilerParams(vmem_limit_bytes=20 * 2**20),
        cost_estimate=pl.CostEstimate(
            flops=2 * 512 * depth * columns, bytes_accessed=8 * 2**20, transcendentals=0
        ),
        name="query_projection",
    )(place, *pieces, w_query)


def attend_kernel(lengths, q_ref, cos_ref, sin_ref, kv_ref, k_ref, v_ref, out_ref, new_ref, acc_ref):
    seqs = k_ref.shape[0]
    half = HEAD // 2
    rows = q_ref.shape[0]
    scale = HEAD ** (-0.5)
    contract_last = (((1,), (1,)), ((), ()))
    pick_row = lax.broadcasted_iota(jnp.int32, (32, rows), 0)
    pick_col = lax.broadcasted_iota(jnp.int32, (32, rows), 1)
    odd = lax.rem(lax.broadcasted_iota(jnp.int32, (32, half), 0), 2) == 1
    second_step = lax.rem(lax.broadcasted_iota(jnp.int32, (96, 1), 0), 2) == 1
    first = kv_ref[:, :half].astype(F32)
    second = kv_ref[:, half:HEAD].astype(F32)
    cosine, sine = cos_ref[...], sin_ref[...]
    new_ref[:, :half] = (first * cosine - second * sine).astype(BF16)
    new_ref[:, half:HEAD] = (second * cosine + first * sine).astype(BF16)
    new_ref[:, HEAD:] = kv_ref[:, HEAD:]
    new_rows = new_ref[...].astype(F32)

    def pick_of(r):
        return (pick_col == (pick_row // 2) * 8 + 2 * r + lax.rem(pick_row, 2)).astype(BF16)

    def query_of(r):
        pick = pick_of(r)
        cosine = jnp.where(odd, cos_ref[2 * r + 1 : 2 * r + 2, :], cos_ref[2 * r : 2 * r + 1, :])
        sine = jnp.where(odd, sin_ref[2 * r + 1 : 2 * r + 2, :], sin_ref[2 * r : 2 * r + 1, :])
        parts = []
        for h in range(3):
            chosen = jnp.dot(pick, q_ref[:, h * HEAD : (h + 1) * HEAD], preferred_element_type=F32)
            first, second = chosen[:, :half], chosen[:, half:]
            parts.append(
                jnp.concatenate([first * cosine - second * sine, second * cosine + first * sine], 1)
            )
        return jnp.concatenate(parts, 0).astype(BF16)

    def scores_of(r, query):
        return lax.dot_general(query, k_ref[r], contract_last, preferred_element_type=F32) * scale

    query = query_of(0)
    scores = scores_of(0, query)
    for r in range(seqs):
        if r + 1 < seqs:
            next_query = query_of(r + 1)
            next_scores = scores_of(r + 1, next_query)
        valid = lax.broadcasted_iota(jnp.int32, scores.shape, 1) < lengths[r]
        cached = jnp.where(valid, scores, -jnp.inf)
        new = new_rows[2 * r : 2 * r + 2, :]
        wide = query.astype(F32)
        fresh0 = jnp.sum(wide * new[0:1, :HEAD], -1, keepdims=True) * scale
        fresh1 = jnp.sum(wide * new[1:2, :HEAD], -1, keepdims=True) * scale
        fresh1 = jnp.where(second_step, fresh1, -jnp.inf)
        top = jnp.maximum(jnp.max(cached, -1, keepdims=True), jnp.maximum(fresh0, fresh1))
        exp_cached = jnp.exp(cached - top)
        exp0 = jnp.exp(fresh0 - top)
        exp1 = jnp.exp(fresh1 - top)
        inverse = 1.0 / (jnp.sum(exp_cached, -1, keepdims=True) + exp0 + exp1)
        weights = (exp_cached * inverse).astype(BF16)
        weight0 = (exp0 * inverse).astype(BF16).astype(F32)
        weight1 = (exp1 * inverse).astype(BF16).astype(F32)
        result = jnp.dot(weights, v_ref[r], preferred_element_type=F32)
        result = result + weight0 * new[0:1, HEAD:] + weight1 * new[1:2, HEAD:]
        result = result.astype(BF16)
        pick = pick_of(r)
        for h in range(3):
            spread = lax.dot_general(
                pick,
                result[h * 32 : (h + 1) * 32],
                (((0,), (0,)), ((), ())),
                preferred_element_type=F32,
            )
            columns = slice(h * HEAD, (h + 1) * HEAD)
            if r == 0:
                acc_ref[:, columns] = spread
            else:
                acc_ref[:, columns] += spread
        if r + 1 < seqs:
            query, scores = next_query, next_scores
    out_ref[...] = acc_ref[...].astype(BF16)


def attend(lengths, query, cosine, sine, keyval, keys, values):
    seqs, context, _ = keys.shape
    rows, columns = query.shape
    vmem_spec = pl.BlockSpec(memory_space=pltpu.VMEM)
    return pl.pallas_call(
        attend_kernel,
        out_shape=[
            jax.ShapeDtypeStruct((rows, columns), BF16),
            jax.ShapeDtypeStruct(keyval.shape, BF16),
        ],
        in_specs=[pl.BlockSpec(memory_space=pltpu.SMEM)] + [vmem_spec] * 6,
        out_specs=[vmem_spec] * 2,
        scratch_shapes=[pltpu.VMEM((rows, columns), F32)],
        compiler_params=pltpu.CompilerParams(vmem_limit_bytes=20 * 2**20),
        cost_estimate=pl.CostEstimate(
            flops=4 * seqs * 96 * context * HEAD,
            bytes_accessed=4 * seqs * context * HEAD,
            transcendentals=seqs * 96 * context,
        ),
        name="attention",
    )(lengths, query, cosine, sine, keyval, keys, values)


def output_kernel(groups, place, *refs):
    pieces, (w_ref, *outs), rows_ref = refs[:8], refs[8:-1], refs[-1]
    x, y, z, core = place[0], place[1], place[2], place[3]
    for index, piece in enumerate(pieces):
        at_core = core if index < 4 else 1 - core
        slot = (0, 3, 1, 2)[index % 4]
        ahead = jnp.where(at_core == 0, slot, (RING - slot) % RING)
        dy = lax.rem(x + ahead - y + RING, RING)
        for part in range(2):
            dz = lax.rem(2 * at_core + part - z + RING, RING)
            outer, inner = jnp.where(core == 0, dy, dz), jnp.where(core == 0, dz, dy)
            for position, group in enumerate(groups):

                @pl.when(outer == group)
                def _():
                    rows_ref[position * RING + inner] = piece[part * 64 : (part + 1) * 64, :]

    outs = list(outs)
    for position, group in enumerate(groups):
        rows = rows_ref[RING * position : RING * position + RING].reshape(256, w_ref.shape[0])
        targets = [outs.pop(0)] if group == 0 else [outs.pop(0), outs.pop(0)]
        for start in range(0, w_ref.shape[1], 768):
            columns = slice(start, start + 768)
            result = jnp.dot(rows, w_ref[:, columns], preferred_element_type=F32)
            if group == 0:
                targets[0][:, columns] = result
            else:
                targets[0][:, columns] = result[:128].astype(targets[0].dtype)
                targets[1][:, columns] = result[128:].astype(targets[1].dtype)


def project_output(place, pieces, w_out, groups):
    depth, columns = w_out.shape
    vmem_spec = pl.BlockSpec(memory_space=pltpu.VMEM)
    shapes = []
    for group in groups:
        if group == 0:
            shapes.append(jax.ShapeDtypeStruct((256, columns), F32))
        else:
            for added in (group == 1, group == 3):
                shapes.append(jax.ShapeDtypeStruct((128, columns), F32 if added else BF16))
    return pl.pallas_call(
        functools.partial(output_kernel, groups),
        out_shape=shapes,
        in_specs=[pl.BlockSpec(memory_space=pltpu.SMEM)] + [vmem_spec] * 9,
        out_specs=[vmem_spec] * len(shapes),
        scratch_shapes=[pltpu.VMEM((RING * len(groups), 64, depth), BF16)],
        compiler_params=pltpu.CompilerParams(vmem_limit_bytes=20 * 2**20),
        cost_estimate=pl.CostEstimate(
            flops=2 * 256 * len(groups) * depth * columns,
            bytes_accessed=8 * 2**20,
            transcendentals=0,
        ),
        name="output_projection",
    )(place, *pieces, w_out)


def body(tokens, gain, w_query, w_keyval, w_out, key_cache, value_cache, lengths):
    seqs = lengths.shape[0]
    gx, yz = lax.axis_index("gx"), lax.axis_index("yz")
    place = jnp.stack([gx // 2, yz // RING, lax.rem(yz, RING), lax.rem(gx, 2)]).astype(jnp.int32)
    positions = jnp.repeat(lengths, 2) + lax.rem(jnp.arange(2 * seqs, dtype=jnp.int32), 2)
    cosine, sine = rotation_tables(positions)

    count = tokens.shape[0] * 2
    features = tokens.shape[2]
    raw = lax.optimization_barrier(tokens.reshape(count, features))
    sums = row_sums(raw)
    sums = sums + send_core(sums)
    sums, cosine, sine, place, raw = lax.optimization_barrier((sums, cosine, sine, place, raw))
    before, after = send_inner(raw, 1), send_inner(raw, -1)
    sums = sums + send_x(sums, 1) + send_x(sums, 2) + send_x(sums, 3)
    sums, before, after = lax.optimization_barrier((sums, before, after))
    before_sums, after_sums = send_inner(sums, 1), send_inner(sums, -1)
    far, far_sums = send_inner(after, -1), send_inner(sums, 2)
    scale = gain.reshape(1, features)
    near = normalize(raw, before, sums, before_sums, scale)
    near, far = lax.optimization_barrier((near, far))
    wide = normalize(after, far, after_sums, far_sums, scale)

    keyval_away, keyval_keep = project_keyval(place, near, w_keyval)
    kept = keyval_keep + send_core(keyval_away)

    near_before, near_after = send_outer(near, 1), send_outer(near, -1)
    near_before, near_after, wide = lax.optimization_barrier((near_before, near_after, wide))
    wide_after = send_outer(wide, -1)
    near_far = send_outer(near_before, 1)
    near_far, wide_again, kept = lax.optimization_barrier((near_far, wide, kept))
    wide_before = send_outer(wide_again, 1)
    wide_far = send_outer(wide_after, -1)

    kept = kept.reshape(RING, count // 8, 2 * HEAD)
    keyval = kept[0] + send_ahead(kept[1], 1) + send_ahead(kept[2], 2) + send_ahead(kept[3], 3)
    keyval = keyval.astype(BF16)

    pieces = [near, near_before, near_after, near_far, wide, wide_before, wide_after, wide_far]
    columns = w_query.shape[1]
    pieces, keyval = lax.optimization_barrier((pieces, keyval))
    away, keep = project_query(place, pieces, w_query, 1)
    summed = (keep + send_core(away)).reshape(2, 128, columns)
    far, behind = send_x(summed[0], 1), send_x(summed[1], -1)
    away, keep = project_query(place, pieces, w_query, 0)
    summed = (keep + send_core(away)).reshape(2, 128, columns)
    moves = [
        (g * 16 + j, (j // 2) * 16 + (j % 2) * 8 + g) for g in range(8) for j in range(16)
    ]
    keyval = lax.ppermute(keyval, ("gx", "yz"), moves)
    far, keyval = lax.optimization_barrier((far, keyval))
    ahead = send_x(summed[1] + far, 1)
    query = (summed[0] + ahead + behind).astype(BF16).reshape(16, 8, columns)
    query = lax.all_to_all(query, "yz", split_axis=0, concat_axis=0)

    heads_out, new_keyval = attend(
        lengths, query.reshape(128, columns), cosine, sine, keyval, key_cache, value_cache
    )
    heads_out = lax.all_to_all(
        heads_out.reshape(16, 8, columns), "yz", split_axis=0, concat_axis=0
    ).reshape(128, columns)
    before = send_x(heads_out, 1)
    after = send_x(heads_out, -1)
    pieces = [heads_out, before, after, send_x(before, 1)]
    pieces = pieces + [send_core(p) for p in pieces]
    two_low, two_high = project_output(place, pieces, w_out, (2,))
    one_low, one_high, three_low, three_high, own = project_output(
        place, pieces, w_out, (1, 3, 0)
    )

    far_low, far_high = send_outer(two_low, 1), send_outer(two_high, -1)
    far_low, far_high = lax.optimization_barrier((far_low, far_high))
    early_high, early_low = send_outer(one_high, 1), send_outer(three_low, -1)
    late_low = send_outer((one_low + far_low.astype(F32)).astype(BF16), 1)
    late_high = send_outer((three_high + far_high.astype(F32)).astype(BF16), -1)
    low = own[:128] + early_low.astype(F32) + late_low.astype(F32)
    high = own[128:] + early_high.astype(F32) + late_high.astype(F32)
    here, one, two, three = low[:64], low[64:], high[:64], high[64:]
    two = two.astype(BF16)
    far_low, far_high = send_inner(two[:32], 1), send_inner(two[32:], -1)
    one = jnp.concatenate([one[:32] + far_low.astype(F32), one[32:]], 0)
    three = jnp.concatenate([three[:32], three[32:] + far_high.astype(F32)], 0)
    branch = here + send_inner(one, 1) + send_inner(three, -1)
    mixed = (raw.astype(F32) + branch).astype(BF16).reshape(tokens.shape)
    return (mixed, new_keyval.reshape(seqs, 2, 2 * HEAD))


def solution(mesh):
    return jax.shard_map(
        body,
        mesh=mesh,
        in_specs=(
            P("yz", None, "gx"),
            P("gx"),
            P("gx", "yz"),
            P("gx", None),
            P("yz", "gx"),
            P(("gx", "yz"), None, None),
            P(("gx", "yz"), None, None),
            P(("gx", "yz")),
        ),
        out_specs=(P("yz", None, "gx"), P(("gx", "yz"), None, None)),
        check_vma=False,
    )
```

```python
import functools

import jax
import jax.numpy as jnp
from jax import lax
from jax.experimental import pallas as pl
from jax.experimental.pallas import tpu as pltpu
from jax.sharding import PartitionSpec as P

D = 18432
HEADS = 48
HEAD = 256
RING = 4
F32 = jnp.float32
BF16 = jnp.bfloat16


def shift(value, move):
    pairs = []
    for x in range(RING):
        for core in range(2):
            for y in range(RING):
                for z in range(RING):
                    dx, dy, dz = move(core)
                    target = (2 * ((x + dx) % RING) + core) * 16
                    target += RING * ((y + dy) % RING) + (z + dz) % RING
                    pairs.append(((2 * x + core) * 16 + RING * y + z, target))
    return lax.ppermute(value, ("gx", "yz"), pairs)


def send_core(value):
    pairs = [(2 * x + c, 2 * x + 1 - c) for x in range(RING) for c in range(2)]
    return lax.ppermute(value, "gx", pairs)


def send_x(value, step):
    return shift(value, lambda core: ((1 - 2 * core) * step, 0, 0))


def send_ahead(value, step):
    return shift(value, lambda core: (step, 0, 0))


def send_inner(value, step):
    return shift(value, lambda core: (0, core * step, (1 - core) * step))


def send_outer(value, step):
    return shift(value, lambda core: (0, (1 - core) * step, core * step))


def rotation_tables(positions):
    half = HEAD // 2
    freq = 10000.0 ** (-jnp.arange(half, dtype=F32) * 2.0 / HEAD)
    angle = positions.astype(F32)[..., None] * freq
    return jnp.cos(angle), jnp.sin(angle)


def sums_kernel(rows_ref, out_ref):
    rows = rows_ref[...].astype(F32)
    total = jnp.sum(rows, -1, keepdims=True)
    squares = jnp.sum(rows * rows, -1, keepdims=True)
    out_ref[...] = jnp.concatenate([total, squares], 1)


def row_sums(rows):
    vmem_spec = pl.BlockSpec(memory_space=pltpu.VMEM)
    return pl.pallas_call(
        sums_kernel,
        out_shape=jax.ShapeDtypeStruct((rows.shape[0], 2), F32),
        in_specs=[vmem_spec],
        out_specs=vmem_spec,
        compiler_params=pltpu.CompilerParams(vmem_limit_bytes=12 * 2**20),
        name="row_sums",
    )(rows)


def normalize_kernel(one_ref, two_ref, one_sums, two_sums, gain_ref, out_ref):
    count = one_ref.shape[0]
    for index, (rows_ref, sums_ref) in enumerate(((one_ref, one_sums), (two_ref, two_sums))):
        mean = sums_ref[:, 0:1] / D
        var = sums_ref[:, 1:2] / D - mean * mean
        rows = rows_ref[...].astype(F32)
        normed = (rows - mean) * lax.rsqrt(var + 1e-05) * gain_ref[...]
        out_ref[index * count : (index + 1) * count, :] = normed.astype(BF16)


def normalize(one, two, one_sums, two_sums, gain):
    vmem_spec = pl.BlockSpec(memory_space=pltpu.VMEM)
    return pl.pallas_call(
        normalize_kernel,
        out_shape=jax.ShapeDtypeStruct((2 * one.shape[0], one.shape[1]), BF16),
        in_specs=[vmem_spec] * 5,
        out_specs=vmem_spec,
        compiler_params=pltpu.CompilerParams(vmem_limit_bytes=12 * 2**20),
        name="normalize",
    )(one, two, one_sums, two_sums, gain)


def keyval_kernel(place, rows_ref, w_ref, away_ref, keep_ref, sums_ref):
    x, core = place[0], place[3]
    rows = rows_ref[: sums_ref.shape[0], :]
    sums_ref[...] = jnp.dot(rows, w_ref[...], preferred_element_type=F32)
    for slot in range(RING):
        block = 2 * lax.rem(x + slot, RING)
        target = pl.ds(8 * slot, 8)
        keep_ref[target, :] = sums_ref[pl.ds(pl.multiple_of(8 * (block + core), 8), 8), :]
        away_ref[target, :] = sums_ref[pl.ds(pl.multiple_of(8 * (block + 1 - core), 8), 8), :]


def project_keyval(place, rows, w_keyval):
    count, depth = rows.shape[0] // 2, rows.shape[1]
    columns = w_keyval.shape[1]
    vmem_spec = pl.BlockSpec(memory_space=pltpu.VMEM)
    half = jax.ShapeDtypeStruct((count // 2, columns), F32)
    return pl.pallas_call(
        keyval_kernel,
        out_shape=[half, half],
        in_specs=[pl.BlockSpec(memory_space=pltpu.SMEM)] + [vmem_spec] * 2,
        out_specs=[vmem_spec] * 2,
        scratch_shapes=[pltpu.VMEM((count, columns), F32)],
        compiler_params=pltpu.CompilerParams(vmem_limit_bytes=12 * 2**20),
        cost_estimate=pl.CostEstimate(
            flops=2 * count * depth * columns, bytes_accessed=3 * 2**20, transcendentals=0
        ),
        name="keyval_projection",
    )(place, rows, w_keyval)


def query_kernel(pair, place, *refs):
    pieces, (w_ref, away_ref, keep_ref, rows_ref) = refs[:8], refs[8:]
    x, y, z, core = place[0], place[1], place[2], place[3]
    for index, piece in enumerate(pieces):
        for part in range(2):
            outer = (0, 3, 1, 2)[index % 4]
            inner = ((0, 3), (1, 2))[index // 4][part]
            at_y = lax.rem(y + jnp.where(core == 0, outer, inner), RING)
            at_z = lax.rem(z + jnp.where(core == 0, inner, outer), RING)
            to_core = at_z // 2
            ahead = lax.rem(at_y - x + RING, RING)
            slot = jnp.where(to_core == 0, ahead, lax.rem(RING - ahead, RING))
            mine = jnp.where(to_core == core, 4, 0)
            position = mine + lax.rem(slot, 2) * 2 + lax.rem(at_z, 2)

            @pl.when(slot // 2 == pair)
            def _():
                rows_ref[position] = piece[part * 64 : (part + 1) * 64, :]

    rows = rows_ref[...].reshape(512, w_ref.shape[0])
    result = jnp.dot(rows, w_ref[...], preferred_element_type=F32)
    away_ref[...] = result[:256]
    keep_ref[...] = result[256:]


def project_query(place, pieces, w_query, pair):
    depth, columns = w_query.shape
    vmem_spec = pl.BlockSpec(memory_space=pltpu.VMEM)
    half = jax.ShapeDtypeStruct((256, columns), F32)
    return pl.pallas_call(
        functools.partial(query_kernel, pair),
        out_shape=[half, half],
        in_specs=[pl.BlockSpec(memory_space=pltpu.SMEM)] + [vmem_spec] * 9,
        out_specs=[vmem_spec] * 2,
        scratch_shapes=[pltpu.VMEM((8, 64, depth), BF16)],
        compiler_params=pltpu.CompilerParams(vmem_limit_bytes=20 * 2**20),
        cost_estimate=pl.CostEstimate(
            flops=2 * 512 * depth * columns, bytes_accessed=8 * 2**20, transcendentals=0
        ),
        name="query_projection",
    )(place, *pieces, w_query)


def attend_kernel(lengths, q_ref, cos_ref, sin_ref, kv_ref, k_ref, v_ref, out_ref, new_ref, acc_ref):
    seqs = k_ref.shape[0]
    half = HEAD // 2
    rows = q_ref.shape[0]
    scale = HEAD ** (-0.5)
    contract_last = (((1,), (1,)), ((), ()))
    pick_row = lax.broadcasted_iota(jnp.int32, (32, rows), 0)
    pick_col = lax.broadcasted_iota(jnp.int32, (32, rows), 1)
    odd = lax.rem(lax.broadcasted_iota(jnp.int32, (32, half), 0), 2) == 1
    second_step = lax.rem(lax.broadcasted_iota(jnp.int32, (96, 1), 0), 2) == 1
    first = kv_ref[:, :half].astype(F32)
    second = kv_ref[:, half:HEAD].astype(F32)
    cosine, sine = cos_ref[...], sin_ref[...]
    new_ref[:, :half] = (first * cosine - second * sine).astype(BF16)
    new_ref[:, half:HEAD] = (second * cosine + first * sine).astype(BF16)
    new_ref[:, HEAD:] = kv_ref[:, HEAD:]
    new_rows = new_ref[...].astype(F32)

    def pick_of(r):
        return (pick_col == (pick_row // 2) * 8 + 2 * r + lax.rem(pick_row, 2)).astype(BF16)

    def query_of(r):
        pick = pick_of(r)
        cosine = jnp.where(odd, cos_ref[2 * r + 1 : 2 * r + 2, :], cos_ref[2 * r : 2 * r + 1, :])
        sine = jnp.where(odd, sin_ref[2 * r + 1 : 2 * r + 2, :], sin_ref[2 * r : 2 * r + 1, :])
        parts = []
        for h in range(3):
            chosen = jnp.dot(pick, q_ref[:, h * HEAD : (h + 1) * HEAD], preferred_element_type=F32)
            first, second = chosen[:, :half], chosen[:, half:]
            parts.append(
                jnp.concatenate([first * cosine - second * sine, second * cosine + first * sine], 1)
            )
        return jnp.concatenate(parts, 0).astype(BF16)

    def scores_of(r, query):
        return lax.dot_general(query, k_ref[r], contract_last, preferred_element_type=F32) * scale

    query = query_of(0)
    scores = scores_of(0, query)
    for r in range(seqs):
        if r + 1 < seqs:
            next_query = query_of(r + 1)
            next_scores = scores_of(r + 1, next_query)
        valid = lax.broadcasted_iota(jnp.int32, scores.shape, 1) < lengths[r]
        cached = jnp.where(valid, scores, -jnp.inf)
        new = new_rows[2 * r : 2 * r + 2, :]
        wide = query.astype(F32)
        fresh0 = jnp.sum(wide * new[0:1, :HEAD], -1, keepdims=True) * scale
        fresh1 = jnp.sum(wide * new[1:2, :HEAD], -1, keepdims=True) * scale
        fresh1 = jnp.where(second_step, fresh1, -jnp.inf)
        top = jnp.maximum(jnp.max(cached, -1, keepdims=True), jnp.maximum(fresh0, fresh1))
        exp_cached = jnp.exp(cached - top)
        exp0 = jnp.exp(fresh0 - top)
        exp1 = jnp.exp(fresh1 - top)
        inverse = 1.0 / (jnp.sum(exp_cached, -1, keepdims=True) + exp0 + exp1)
        weights = (exp_cached * inverse).astype(BF16)
        weight0 = (exp0 * inverse).astype(BF16).astype(F32)
        weight1 = (exp1 * inverse).astype(BF16).astype(F32)
        result = jnp.dot(weights, v_ref[r], preferred_element_type=F32)
        result = result + weight0 * new[0:1, HEAD:] + weight1 * new[1:2, HEAD:]
        result = result.astype(BF16)
        pick = pick_of(r)
        for h in range(3):
            spread = lax.dot_general(
                pick,
                result[h * 32 : (h + 1) * 32],
                (((0,), (0,)), ((), ())),
                preferred_element_type=F32,
            )
            columns = slice(h * HEAD, (h + 1) * HEAD)
            if r == 0:
                acc_ref[:, columns] = spread
            else:
                acc_ref[:, columns] += spread
        if r + 1 < seqs:
            query, scores = next_query, next_scores
    out_ref[...] = acc_ref[...].astype(BF16)


def attend(lengths, query, cosine, sine, keyval, keys, values):
    seqs, context, _ = keys.shape
    rows, columns = query.shape
    vmem_spec = pl.BlockSpec(memory_space=pltpu.VMEM)
    return pl.pallas_call(
        attend_kernel,
        out_shape=[
            jax.ShapeDtypeStruct((rows, columns), BF16),
            jax.ShapeDtypeStruct(keyval.shape, BF16),
        ],
        in_specs=[pl.BlockSpec(memory_space=pltpu.SMEM)] + [vmem_spec] * 6,
        out_specs=[vmem_spec] * 2,
        scratch_shapes=[pltpu.VMEM((rows, columns), F32)],
        compiler_params=pltpu.CompilerParams(vmem_limit_bytes=20 * 2**20),
        cost_estimate=pl.CostEstimate(
            flops=4 * seqs * 96 * context * HEAD,
            bytes_accessed=4 * seqs * context * HEAD,
            transcendentals=seqs * 96 * context,
        ),
        name="attention",
    )(lengths, query, cosine, sine, keyval, keys, values)


def output_kernel(groups, place, *refs):
    pieces, (w_ref, *outs), rows_ref = refs[:8], refs[8:-1], refs[-1]
    x, y, z, core = place[0], place[1], place[2], place[3]
    for index, piece in enumerate(pieces):
        at_core = core if index < 4 else 1 - core
        slot = (0, 3, 1, 2)[index % 4]
        ahead = jnp.where(at_core == 0, slot, (RING - slot) % RING)
        dy = lax.rem(x + ahead - y + RING, RING)
        for part in range(2):
            dz = lax.rem(2 * at_core + part - z + RING, RING)
            outer, inner = jnp.where(core == 0, dy, dz), jnp.where(core == 0, dz, dy)
            for position, group in enumerate(groups):

                @pl.when(outer == group)
                def _():
                    rows_ref[position * RING + inner] = piece[part * 64 : (part + 1) * 64, :]

    outs = list(outs)
    for position, group in enumerate(groups):
        rows = rows_ref[RING * position : RING * position + RING].reshape(256, w_ref.shape[0])
        targets = [outs.pop(0)] if group == 0 else [outs.pop(0), outs.pop(0)]
        width = w_ref.shape[1] if len(groups) == 1 else 768
        for start in range(0, w_ref.shape[1], width):
            columns = slice(start, start + width)
            result = jnp.dot(rows, w_ref[:, columns], preferred_element_type=F32)
            if group == 0:
                targets[0][:, columns] = result
            else:
                targets[0][:, columns] = result[:128].astype(targets[0].dtype)
                targets[1][:, columns] = result[128:].astype(targets[1].dtype)


def project_output(place, pieces, w_out, groups):
    depth, columns = w_out.shape
    vmem_spec = pl.BlockSpec(memory_space=pltpu.VMEM)
    shapes = []
    for group in groups:
        if group == 0:
            shapes.append(jax.ShapeDtypeStruct((256, columns), F32))
        else:
            for added in (group == 1, group == 3):
                shapes.append(jax.ShapeDtypeStruct((128, columns), F32 if added else BF16))
    return pl.pallas_call(
        functools.partial(output_kernel, groups),
        out_shape=shapes,
        in_specs=[pl.BlockSpec(memory_space=pltpu.SMEM)] + [vmem_spec] * 9,
        out_specs=[vmem_spec] * len(shapes),
        scratch_shapes=[pltpu.VMEM((RING * len(groups), 64, depth), BF16)],
        compiler_params=pltpu.CompilerParams(vmem_limit_bytes=20 * 2**20),
        cost_estimate=pl.CostEstimate(
            flops=2 * 256 * len(groups) * depth * columns,
            bytes_accessed=8 * 2**20,
            transcendentals=0,
        ),
        name="output_projection",
    )(place, *pieces, w_out)


def finish_kernel(rows_ref, here_ref, one_ref, two_ref, out_ref):
    total = here_ref[...] + one_ref[...] + two_ref[...]
    out_ref[...] = (rows_ref[...].astype(F32) + total).astype(BF16)


def finish(rows, here, one, two):
    vmem_spec = pl.BlockSpec(memory_space=pltpu.VMEM)
    return pl.pallas_call(
        finish_kernel,
        out_shape=jax.ShapeDtypeStruct(rows.shape, BF16),
        in_specs=[vmem_spec] * 4,
        out_specs=vmem_spec,
        compiler_params=pltpu.CompilerParams(vmem_limit_bytes=12 * 2**20),
        name="finish",
    )(rows, here, one, two)


def body(tokens, gain, w_query, w_keyval, w_out, key_cache, value_cache, lengths):
    seqs = lengths.shape[0]
    gx, yz = lax.axis_index("gx"), lax.axis_index("yz")
    place = jnp.stack([gx // 2, yz // RING, lax.rem(yz, RING), lax.rem(gx, 2)]).astype(jnp.int32)
    positions = jnp.repeat(lengths, 2) + lax.rem(jnp.arange(2 * seqs, dtype=jnp.int32), 2)
    cosine, sine = rotation_tables(positions)

    count = tokens.shape[0] * 2
    features = tokens.shape[2]
    raw = lax.optimization_barrier(tokens.reshape(count, features))
    sums = row_sums(raw)
    sums = sums + send_core(sums)
    sums, cosine, sine, place, raw = lax.optimization_barrier((sums, cosine, sine, place, raw))
    after, before = send_inner(raw, -1), send_inner(raw, 1)
    sums = sums + send_x(sums, 1) + send_x(sums, 2) + send_x(sums, 3)
    sums, before, after = lax.optimization_barrier((sums, before, after))
    before_sums, after_sums = send_inner(sums, 1), send_inner(sums, -1)
    before, before_sums = lax.optimization_barrier((before, before_sums))
    far, far_sums = send_inner(before, 1), send_inner(sums, 2)
    scale = gain.reshape(1, features)
    near = normalize(raw, before, sums, before_sums, scale)
    wide = normalize(after, far, after_sums, far_sums, scale)

    keyval_away, keyval_keep = project_keyval(place, near, w_keyval)
    kept = keyval_keep + send_core(keyval_away)

    near_before, near_after = send_outer(near, 1), send_outer(near, -1)
    near_before, near_after, wide, kept = lax.optimization_barrier(
        (near_before, near_after, wide, kept)
    )
    wide_after = send_outer(wide, -1)
    near_far = send_outer(near_before, 1)
    near_far, wide_again = lax.optimization_barrier((near_far, wide))
    wide_before = send_outer(wide_again, 1)
    wide_far = send_outer(wide_after, -1)

    kept = kept.reshape(RING, count // 8, 2 * HEAD)
    keyval = kept[0] + send_ahead(kept[1], 1) + send_ahead(kept[2], 2) + send_ahead(kept[3], 3)
    keyval = keyval.astype(BF16)

    pieces = [near, near_before, near_after, near_far, wide, wide_before, wide_after, wide_far]
    columns = w_query.shape[1]
    pieces, keyval = lax.optimization_barrier((pieces, keyval))
    away, keep = project_query(place, pieces, w_query, 1)
    summed = (keep + send_core(away)).reshape(2, 128, columns)
    far, behind = send_x(summed[0], 1), send_x(summed[1], -1)
    away, keep = project_query(place, pieces, w_query, 0)
    summed = (keep + send_core(away)).reshape(2, 128, columns)
    moves = [
        (g * 16 + j, (j // 2) * 16 + (j % 2) * 8 + g) for g in range(8) for j in range(16)
    ]
    keyval = lax.ppermute(keyval, ("gx", "yz"), moves)
    far, keyval = lax.optimization_barrier((far, keyval))
    ahead = send_x(summed[1] + far, 1)
    query = (summed[0] + ahead + behind).astype(BF16).reshape(16, 8, columns)
    query = lax.all_to_all(query, "yz", split_axis=0, concat_axis=0)

    heads_out, new_keyval = attend(
        lengths, query.reshape(128, columns), cosine, sine, keyval, key_cache, value_cache
    )
    heads_out = lax.all_to_all(
        heads_out.reshape(16, 8, columns), "yz", split_axis=0, concat_axis=0
    ).reshape(128, columns)
    before = send_x(heads_out, 1)
    after = send_x(heads_out, -1)
    pieces = [heads_out, before, after, send_x(before, 1)]
    pieces = pieces + [send_core(p) for p in pieces]
    two_low, two_high = project_output(place, pieces, w_out, (2,))
    one_low, one_high, three_low, three_high, own = project_output(
        place, pieces, w_out, (1, 3, 0)
    )

    far_low, far_high = send_outer(two_low, 1), send_outer(two_high, -1)
    far_low, far_high = lax.optimization_barrier((far_low, far_high))
    early_high, early_low = send_outer(one_high, 1), send_outer(three_low, -1)
    late_low = send_outer((one_low + far_low.astype(F32)).astype(BF16), 1)
    late_high = send_outer((three_high + far_high.astype(F32)).astype(BF16), -1)
    low = own[:128] + early_low.astype(F32) + late_low.astype(F32)
    high = own[128:] + early_high.astype(F32) + late_high.astype(F32)
    here, one, two, three = low[:64], low[64:], high[:64], high[64:]
    two = two.astype(BF16)
    far_low, far_high = send_inner(two[:32], 1), send_inner(two[32:], -1)
    one = jnp.concatenate([one[:32] + far_low.astype(F32), one[32:]], 0)
    three = jnp.concatenate([three[:32], three[32:] + far_high.astype(F32)], 0)
    mixed = finish(raw, here, send_inner(one, 1), send_inner(three, -1)).reshape(tokens.shape)
    return (mixed, new_keyval.reshape(seqs, 2, 2 * HEAD))


def solution(mesh):
    return jax.shard_map(
        body,
        mesh=mesh,
        in_specs=(
            P("yz", None, "gx"),
            P("gx"),
            P("gx", "yz"),
            P("gx", None),
            P("yz", "gx"),
            P(("gx", "yz"), None, None),
            P(("gx", "yz"), None, None),
            P(("gx", "yz")),
        ),
        out_specs=(P("yz", None, "gx"), P(("gx", "yz"), None, None)),
        check_vma=False,
    )
```

```python
import functools

import jax
import jax.numpy as jnp
from jax import lax
from jax.experimental import pallas as pl
from jax.experimental.pallas import tpu as pltpu
from jax.sharding import PartitionSpec as P

D = 18432
HEADS = 48
HEAD = 256
RING = 4
F32 = jnp.float32
BF16 = jnp.bfloat16


def shift(value, move):
    pairs = []
    for x in range(RING):
        for core in range(2):
            for y in range(RING):
                for z in range(RING):
                    dx, dy, dz = move(core)
                    target = (2 * ((x + dx) % RING) + core) * 16
                    target += RING * ((y + dy) % RING) + (z + dz) % RING
                    pairs.append(((2 * x + core) * 16 + RING * y + z, target))
    return lax.ppermute(value, ("gx", "yz"), pairs)


def send_core(value):
    pairs = [(2 * x + c, 2 * x + 1 - c) for x in range(RING) for c in range(2)]
    return lax.ppermute(value, "gx", pairs)


def send_x(value, step):
    return shift(value, lambda core: ((1 - 2 * core) * step, 0, 0))


def send_ahead(value, step):
    return shift(value, lambda core: (step, 0, 0))


def send_inner(value, step):
    return shift(value, lambda core: (0, core * step, (1 - core) * step))


def send_outer(value, step):
    return shift(value, lambda core: (0, (1 - core) * step, core * step))


def rotation_tables(positions):
    half = HEAD // 2
    freq = 10000.0 ** (-jnp.arange(half, dtype=F32) * 2.0 / HEAD)
    angle = positions.astype(F32)[..., None] * freq
    return jnp.cos(angle), jnp.sin(angle)


def sums_kernel(rows_ref, out_ref):
    rows = rows_ref[...].astype(F32)
    total = jnp.sum(rows, -1, keepdims=True)
    squares = jnp.sum(rows * rows, -1, keepdims=True)
    out_ref[...] = jnp.concatenate([total, squares], 1)


def row_sums(rows):
    vmem_spec = pl.BlockSpec(memory_space=pltpu.VMEM)
    return pl.pallas_call(
        sums_kernel,
        out_shape=jax.ShapeDtypeStruct((rows.shape[0], 2), F32),
        in_specs=[vmem_spec],
        out_specs=vmem_spec,
        compiler_params=pltpu.CompilerParams(vmem_limit_bytes=12 * 2**20),
        name="row_sums",
    )(rows)


def normalize_kernel(one_ref, two_ref, one_sums, two_sums, gain_ref, out_ref):
    count = one_ref.shape[0]
    for index, (rows_ref, sums_ref) in enumerate(((one_ref, one_sums), (two_ref, two_sums))):
        mean = sums_ref[:, 0:1] / D
        var = sums_ref[:, 1:2] / D - mean * mean
        rows = rows_ref[...].astype(F32)
        normed = (rows - mean) * lax.rsqrt(var + 1e-05) * gain_ref[...]
        out_ref[index * count : (index + 1) * count, :] = normed.astype(BF16)


def normalize(one, two, one_sums, two_sums, gain):
    vmem_spec = pl.BlockSpec(memory_space=pltpu.VMEM)
    return pl.pallas_call(
        normalize_kernel,
        out_shape=jax.ShapeDtypeStruct((2 * one.shape[0], one.shape[1]), BF16),
        in_specs=[vmem_spec] * 5,
        out_specs=vmem_spec,
        compiler_params=pltpu.CompilerParams(vmem_limit_bytes=12 * 2**20),
        name="normalize",
    )(one, two, one_sums, two_sums, gain)


def keyval_kernel(place, rows_ref, w_ref, away_ref, keep_ref, sums_ref):
    x, core = place[0], place[3]
    rows = rows_ref[: sums_ref.shape[0], :]
    sums_ref[...] = jnp.dot(rows, w_ref[...], preferred_element_type=F32)
    for slot in range(RING):
        block = 2 * lax.rem(x + slot, RING)
        target = pl.ds(8 * slot, 8)
        keep_ref[target, :] = sums_ref[pl.ds(pl.multiple_of(8 * (block + core), 8), 8), :]
        away_ref[target, :] = sums_ref[pl.ds(pl.multiple_of(8 * (block + 1 - core), 8), 8), :]


def project_keyval(place, rows, w_keyval):
    count, depth = rows.shape[0] // 2, rows.shape[1]
    columns = w_keyval.shape[1]
    vmem_spec = pl.BlockSpec(memory_space=pltpu.VMEM)
    half = jax.ShapeDtypeStruct((count // 2, columns), F32)
    return pl.pallas_call(
        keyval_kernel,
        out_shape=[half, half],
        in_specs=[pl.BlockSpec(memory_space=pltpu.SMEM)] + [vmem_spec] * 2,
        out_specs=[vmem_spec] * 2,
        scratch_shapes=[pltpu.VMEM((count, columns), F32)],
        compiler_params=pltpu.CompilerParams(vmem_limit_bytes=12 * 2**20),
        cost_estimate=pl.CostEstimate(
            flops=2 * count * depth * columns, bytes_accessed=3 * 2**20, transcendentals=0
        ),
        name="keyval_projection",
    )(place, rows, w_keyval)


def query_kernel(pair, place, *refs):
    pieces, (w_ref, away_ref, keep_ref, rows_ref) = refs[:8], refs[8:]
    x, y, z, core = place[0], place[1], place[2], place[3]
    for index, piece in enumerate(pieces):
        for part in range(2):
            outer = (0, 3, 1, 2)[index % 4]
            inner = ((0, 3), (1, 2))[index // 4][part]
            at_y = lax.rem(y + jnp.where(core == 0, outer, inner), RING)
            at_z = lax.rem(z + jnp.where(core == 0, inner, outer), RING)
            to_core = at_z // 2
            ahead = lax.rem(at_y - x + RING, RING)
            slot = jnp.where(to_core == 0, ahead, lax.rem(RING - ahead, RING))
            mine = jnp.where(to_core == core, 4, 0)
            position = mine + lax.rem(slot, 2) * 2 + lax.rem(at_z, 2)

            @pl.when(slot // 2 == pair)
            def _():
                rows_ref[position] = piece[part * 64 : (part + 1) * 64, :]

    rows = rows_ref[...].reshape(512, w_ref.shape[0])
    result = jnp.dot(rows, w_ref[...], preferred_element_type=F32)
    away_ref[...] = result[:256]
    keep_ref[...] = result[256:]


def project_query(place, pieces, w_query, pair):
    depth, columns = w_query.shape
    vmem_spec = pl.BlockSpec(memory_space=pltpu.VMEM)
    half = jax.ShapeDtypeStruct((256, columns), F32)
    return pl.pallas_call(
        functools.partial(query_kernel, pair),
        out_shape=[half, half],
        in_specs=[pl.BlockSpec(memory_space=pltpu.SMEM)] + [vmem_spec] * 9,
        out_specs=[vmem_spec] * 2,
        scratch_shapes=[pltpu.VMEM((8, 64, depth), BF16)],
        compiler_params=pltpu.CompilerParams(vmem_limit_bytes=20 * 2**20),
        cost_estimate=pl.CostEstimate(
            flops=2 * 512 * depth * columns, bytes_accessed=8 * 2**20, transcendentals=0
        ),
        name="query_projection",
    )(place, *pieces, w_query)


def attend_kernel(lengths, q_ref, cos_ref, sin_ref, kv_ref, k_ref, v_ref, out_ref, new_ref, acc_ref):
    seqs = k_ref.shape[0]
    half = HEAD // 2
    rows = q_ref.shape[0]
    scale = HEAD ** (-0.5)
    contract_last = (((1,), (1,)), ((), ()))
    pick_row = lax.broadcasted_iota(jnp.int32, (32, rows), 0)
    pick_col = lax.broadcasted_iota(jnp.int32, (32, rows), 1)
    odd = lax.rem(lax.broadcasted_iota(jnp.int32, (32, half), 0), 2) == 1
    second_step = lax.rem(lax.broadcasted_iota(jnp.int32, (96, 1), 0), 2) == 1
    first = kv_ref[:, :half].astype(F32)
    second = kv_ref[:, half:HEAD].astype(F32)
    cosine, sine = cos_ref[...], sin_ref[...]
    new_ref[:, :half] = (first * cosine - second * sine).astype(BF16)
    new_ref[:, half:HEAD] = (second * cosine + first * sine).astype(BF16)
    new_ref[:, HEAD:] = kv_ref[:, HEAD:]
    new_rows = new_ref[...].astype(F32)

    def pick_of(r):
        return (pick_col == (pick_row // 2) * 8 + 2 * r + lax.rem(pick_row, 2)).astype(BF16)

    def query_of(r):
        pick = pick_of(r)
        cosine = jnp.where(odd, cos_ref[2 * r + 1 : 2 * r + 2, :], cos_ref[2 * r : 2 * r + 1, :])
        sine = jnp.where(odd, sin_ref[2 * r + 1 : 2 * r + 2, :], sin_ref[2 * r : 2 * r + 1, :])
        parts = []
        for h in range(3):
            chosen = jnp.dot(pick, q_ref[:, h * HEAD : (h + 1) * HEAD], preferred_element_type=F32)
            first, second = chosen[:, :half], chosen[:, half:]
            parts.append(
                jnp.concatenate([first * cosine - second * sine, second * cosine + first * sine], 1)
            )
        return jnp.concatenate(parts, 0).astype(BF16)

    def scores_of(r, query):
        return lax.dot_general(query, k_ref[r], contract_last, preferred_element_type=F32) * scale

    query = query_of(0)
    scores = scores_of(0, query)
    for r in range(seqs):
        if r + 1 < seqs:
            next_query = query_of(r + 1)
            next_scores = scores_of(r + 1, next_query)
        valid = lax.broadcasted_iota(jnp.int32, scores.shape, 1) < lengths[r]
        cached = jnp.where(valid, scores, -jnp.inf)
        new = new_rows[2 * r : 2 * r + 2, :]
        wide = query.astype(F32)
        fresh0 = jnp.sum(wide * new[0:1, :HEAD], -1, keepdims=True) * scale
        fresh1 = jnp.sum(wide * new[1:2, :HEAD], -1, keepdims=True) * scale
        fresh1 = jnp.where(second_step, fresh1, -jnp.inf)
        top = jnp.maximum(jnp.max(cached, -1, keepdims=True), jnp.maximum(fresh0, fresh1))
        exp_cached = jnp.exp(cached - top)
        exp0 = jnp.exp(fresh0 - top)
        exp1 = jnp.exp(fresh1 - top)
        inverse = 1.0 / (jnp.sum(exp_cached, -1, keepdims=True) + exp0 + exp1)
        weights = (exp_cached * inverse).astype(BF16)
        weight0 = (exp0 * inverse).astype(BF16).astype(F32)
        weight1 = (exp1 * inverse).astype(BF16).astype(F32)
        result = jnp.dot(weights, v_ref[r], preferred_element_type=F32)
        result = result + weight0 * new[0:1, HEAD:] + weight1 * new[1:2, HEAD:]
        result = result.astype(BF16)
        pick = pick_of(r)
        for h in range(3):
            spread = lax.dot_general(
                pick,
                result[h * 32 : (h + 1) * 32],
                (((0,), (0,)), ((), ())),
                preferred_element_type=F32,
            )
            columns = slice(h * HEAD, (h + 1) * HEAD)
            if r == 0:
                acc_ref[:, columns] = spread
            else:
                acc_ref[:, columns] += spread
        if r + 1 < seqs:
            query, scores = next_query, next_scores
    out_ref[...] = acc_ref[...].astype(BF16)


def attend(lengths, query, cosine, sine, keyval, keys, values):
    seqs, context, _ = keys.shape
    rows, columns = query.shape
    vmem_spec = pl.BlockSpec(memory_space=pltpu.VMEM)
    return pl.pallas_call(
        attend_kernel,
        out_shape=[
            jax.ShapeDtypeStruct((rows, columns), BF16),
            jax.ShapeDtypeStruct(keyval.shape, BF16),
        ],
        in_specs=[pl.BlockSpec(memory_space=pltpu.SMEM)] + [vmem_spec] * 6,
        out_specs=[vmem_spec] * 2,
        scratch_shapes=[pltpu.VMEM((rows, columns), F32)],
        compiler_params=pltpu.CompilerParams(vmem_limit_bytes=20 * 2**20),
        cost_estimate=pl.CostEstimate(
            flops=4 * seqs * 96 * context * HEAD,
            bytes_accessed=4 * seqs * context * HEAD,
            transcendentals=seqs * 96 * context,
        ),
        name="attention",
    )(lengths, query, cosine, sine, keyval, keys, values)


def output_kernel(groups, place, *refs):
    pieces, (w_ref, *outs), rows_ref = refs[:8], refs[8:-1], refs[-1]
    x, y, z, core = place[0], place[1], place[2], place[3]
    for index, piece in enumerate(pieces):
        at_core = core if index < 4 else 1 - core
        slot = (0, 3, 1, 2)[index % 4]
        ahead = jnp.where(at_core == 0, slot, (RING - slot) % RING)
        dy = lax.rem(x + ahead - y + RING, RING)
        for part in range(2):
            dz = lax.rem(2 * at_core + part - z + RING, RING)
            outer, inner = jnp.where(core == 0, dy, dz), jnp.where(core == 0, dz, dy)
            for position, group in enumerate(groups):

                @pl.when(outer == group)
                def _():
                    rows_ref[position * RING + inner] = piece[part * 64 : (part + 1) * 64, :]

    outs = list(outs)
    for position, group in enumerate(groups):
        rows = rows_ref[RING * position : RING * position + RING].reshape(256, w_ref.shape[0])
        targets = [outs.pop(0)] if group == 0 else [outs.pop(0), outs.pop(0)]
        width = w_ref.shape[1] if len(groups) == 1 else 768
        for start in range(0, w_ref.shape[1], width):
            columns = slice(start, start + width)
            result = jnp.dot(rows, w_ref[:, columns], preferred_element_type=F32)
            if group == 0:
                targets[0][:, columns] = result
            else:
                targets[0][:, columns] = result[:128].astype(targets[0].dtype)
                targets[1][:, columns] = result[128:].astype(targets[1].dtype)


def project_output(place, pieces, w_out, groups):
    depth, columns = w_out.shape
    vmem_spec = pl.BlockSpec(memory_space=pltpu.VMEM)
    shapes = []
    for group in groups:
        if group == 0:
            shapes.append(jax.ShapeDtypeStruct((256, columns), F32))
        else:
            for added in (group == 1, group == 3):
                shapes.append(jax.ShapeDtypeStruct((128, columns), F32 if added else BF16))
    return pl.pallas_call(
        functools.partial(output_kernel, groups),
        out_shape=shapes,
        in_specs=[pl.BlockSpec(memory_space=pltpu.SMEM)] + [vmem_spec] * 9,
        out_specs=[vmem_spec] * len(shapes),
        scratch_shapes=[pltpu.VMEM((RING * len(groups), 64, depth), BF16)],
        compiler_params=pltpu.CompilerParams(vmem_limit_bytes=20 * 2**20),
        cost_estimate=pl.CostEstimate(
            flops=2 * 256 * len(groups) * depth * columns,
            bytes_accessed=8 * 2**20,
            transcendentals=0,
        ),
        name="output_projection",
    )(place, *pieces, w_out)


def finish_kernel(rows_ref, here_ref, one_ref, two_ref, out_ref):
    total = here_ref[...] + one_ref[...] + two_ref[...]
    out_ref[...] = (rows_ref[...].astype(F32) + total).astype(BF16)


def finish(rows, here, one, two):
    vmem_spec = pl.BlockSpec(memory_space=pltpu.VMEM)
    return pl.pallas_call(
        finish_kernel,
        out_shape=jax.ShapeDtypeStruct(rows.shape, BF16),
        in_specs=[vmem_spec] * 4,
        out_specs=vmem_spec,
        compiler_params=pltpu.CompilerParams(vmem_limit_bytes=12 * 2**20),
        name="finish",
    )(rows, here, one, two)


def body(tokens, gain, w_query, w_keyval, w_out, key_cache, value_cache, lengths):
    seqs = lengths.shape[0]
    gx, yz = lax.axis_index("gx"), lax.axis_index("yz")
    place = jnp.stack([gx // 2, yz // RING, lax.rem(yz, RING), lax.rem(gx, 2)]).astype(jnp.int32)
    positions = jnp.repeat(lengths, 2) + lax.rem(jnp.arange(2 * seqs, dtype=jnp.int32), 2)
    cosine, sine = rotation_tables(positions)

    count = tokens.shape[0] * 2
    features = tokens.shape[2]
    raw = lax.optimization_barrier(tokens.reshape(count, features))
    sums = row_sums(raw)
    sums = sums + send_core(sums)
    sums, cosine, sine, place, raw = lax.optimization_barrier((sums, cosine, sine, place, raw))
    before = send_inner(raw, 1)
    sums = sums + send_x(sums, 1) + send_x(sums, 2) + send_x(sums, 3)
    before_sums, after_sums, far_sums = (send_inner(sums, step) for step in (1, -1, 2))
    before_sums, after_sums, far_sums, before, raw = lax.optimization_barrier(
        (before_sums, after_sums, far_sums, before, raw)
    )
    after, far = send_inner(raw, -1), send_inner(before, 1)
    scale = gain.reshape(1, features)
    near = normalize(raw, before, sums, before_sums, scale)
    wide = normalize(after, far, after_sums, far_sums, scale)

    keyval_away, keyval_keep = project_keyval(place, near, w_keyval)
    kept = keyval_keep + send_core(keyval_away)

    near_before, near_after = send_outer(near, 1), send_outer(near, -1)
    near_before, near_after, wide, kept = lax.optimization_barrier(
        (near_before, near_after, wide, kept)
    )
    wide_after = send_outer(wide, -1)
    near_far = send_outer(near_before, 1)
    near_far, wide_again = lax.optimization_barrier((near_far, wide))
    wide_before = send_outer(wide_again, 1)
    wide_far = send_outer(wide_after, -1)

    kept = kept.reshape(RING, count // 8, 2 * HEAD)
    keyval = kept[0] + send_ahead(kept[1], 1) + send_ahead(kept[2], 2) + send_ahead(kept[3], 3)
    keyval = keyval.astype(BF16)

    pieces = [near, near_before, near_after, near_far, wide, wide_before, wide_after, wide_far]
    columns = w_query.shape[1]
    pieces, keyval = lax.optimization_barrier((pieces, keyval))
    away, keep = project_query(place, pieces, w_query, 1)
    summed = (keep + send_core(away)).reshape(2, 128, columns)
    far, behind = send_x(summed[0], 1), send_x(summed[1], -1)
    away, keep = project_query(place, pieces, w_query, 0)
    summed = (keep + send_core(away)).reshape(2, 128, columns)
    moves = [
        (g * 16 + j, (j // 2) * 16 + (j % 2) * 8 + g) for g in range(8) for j in range(16)
    ]
    keyval = lax.ppermute(keyval, ("gx", "yz"), moves)
    far, keyval = lax.optimization_barrier((far, keyval))
    ahead = send_x(summed[1] + far, 1)
    query = (summed[0] + ahead + behind).astype(BF16).reshape(16, 8, columns)
    query = lax.all_to_all(query, "yz", split_axis=0, concat_axis=0)

    heads_out, new_keyval = attend(
        lengths, query.reshape(128, columns), cosine, sine, keyval, key_cache, value_cache
    )
    heads_out = lax.all_to_all(
        heads_out.reshape(16, 8, columns), "yz", split_axis=0, concat_axis=0
    ).reshape(128, columns)
    before = send_x(heads_out, 1)
    after = send_x(heads_out, -1)
    pieces = [heads_out, before, after, send_x(before, 1)]
    pieces = pieces + [send_core(p) for p in pieces]
    two_low, two_high = project_output(place, pieces, w_out, (2,))
    one_low, one_high, three_low, three_high, own = project_output(
        place, pieces, w_out, (1, 3, 0)
    )

    far_low, far_high = send_outer(two_low, 1), send_outer(two_high, -1)
    far_low, far_high = lax.optimization_barrier((far_low, far_high))
    early_high, early_low = send_outer(one_high, 1), send_outer(three_low, -1)
    late_low = send_outer((one_low + far_low.astype(F32)).astype(BF16), 1)
    late_high = send_outer((three_high + far_high.astype(F32)).astype(BF16), -1)
    low = own[:128] + early_low.astype(F32) + late_low.astype(F32)
    high = own[128:] + early_high.astype(F32) + late_high.astype(F32)
    here, one, two, three = low[:64], low[64:], high[:64], high[64:]
    two = two.astype(BF16)
    far_low, far_high = send_inner(two[:32], 1), send_inner(two[32:], -1)
    one = jnp.concatenate([one[:32] + far_low.astype(F32), one[32:]], 0)
    three = jnp.concatenate([three[:32], three[32:] + far_high.astype(F32)], 0)
    mixed = finish(raw, here, send_inner(one, 1), send_inner(three, -1)).reshape(tokens.shape)
    return (mixed, new_keyval.reshape(seqs, 2, 2 * HEAD))


def solution(mesh):
    return jax.shard_map(
        body,
        mesh=mesh,
        in_specs=(
            P("yz", None, "gx"),
            P("gx"),
            P("gx", "yz"),
            P("gx", None),
            P("yz", "gx"),
            P(("gx", "yz"), None, None),
            P(("gx", "yz"), None, None),
            P(("gx", "yz")),
        ),
        out_specs=(P("yz", None, "gx"), P(("gx", "yz"), None, None)),
        check_vma=False,
    )
```
